768 devices in a mesh: comp: 2 (over core), gx: 24 (over z_hi, y), gy: 16 (over z_lo, x).
Axes of the slice: x: 4, y: 8, z: 12 (z_hi: 3, z_lo: 4; z = z_hi * 4 + z_lo), core: 2. Of those that a mesh axis runs over, the one named last changes fastest.
Arguments:
- ocean_state: float32 [2, 8, 8, 96, 2048], P('comp', None, None, 'gx', 'gy'), may hold values from -4 to 4
- land_sea: int32 [96, 2048], P('gx', 'gy'), may hold values 0 or 1
- depth_levels: int32 [96, 2048], P('gx', 'gy'), may hold values from 1 to 8
- photic_production_factors: float32 [8], replicated, may hold values from 0.1 to 0.5
- species_decay_factors: float32 [8], replicated, may hold values from 0.05 to 0.3
Outputs:
- advanced: float32 [2, 8, 8, 96, 2048], P('comp', None, None, 'gx', 'gy')
The draws below stay inside these ranges and needn't reach their ends.
All inputs are finite; a program needn't handle non-finite values. No bound on the sum of `land_sea` on one device may be relied on, other than what follows from the above.
Results may differ from the reference program's by a relative error of at most 0.0003.
Values sent between devices are 32-bit elements; how exact they have to be, the bound alone decides.
No kernel may reach another device: no remote copies, remote signals or barrier semaphores. Data moves between devices by JAX's collectives and lax.ppermute only.
A program may use at most 32 MiB of HBM per device.

```python
import math
import jax
import jax.numpy as jnp
from jax import lax

FIELDS = 8
NZ = 8
DYN_STEPS = 4
TRACER_STEPS = 2
NX = 96
NY = 2048


def draw_ocean_state(key, part):
    key = jax.random.fold_in(key, 11)
    subkeys = jax.random.split(key, 4)
    grid_shape = (NZ, NX, NY)
    speeds = 0.1 * jnp.clip(jax.random.normal(subkeys[0], (2,) + grid_shape, jnp.float32), -2.5, 2.5)
    scalars = jnp.clip(jax.random.normal(subkeys[1], (2,) + grid_shape, jnp.float32), -4.0, 4.0)
    trends = 0.05 * jnp.clip(jax.random.normal(subkeys[2], (4,) + grid_shape, jnp.float32), -3.0, 3.0)
    species_concentrations = jax.random.uniform(subkeys[3], (FIELDS,) + grid_shape, jnp.float32, 0.0, 2.0)
    momentum_solver = jnp.concatenate([speeds, scalars, trends], axis=0)
    return jnp.stack([momentum_solver, species_concentrations]).astype(jnp.float32)


def with_ends(values, rng, least, largest):
    spot = [jax.random.randint(jax.random.fold_in(rng, axis), (), 0, length) for axis, length in enumerate(values.shape)]
    main_axis = values.shape.index(max(values.shape))
    neighbour = spot[:main_axis] + [(spot[main_axis] + 1) % values.shape[main_axis]] + spot[main_axis + 1:]
    return values.at[tuple(spot)].set(least).at[tuple(neighbour)].set(largest)


def setup_inputs(seed: int = 0) -> dict:
    streams_of = jax.random.split(jax.random.key(seed), 6)
    ocean_state = draw_ocean_state(jax.random.fold_in(streams_of[5], 71), 0)
    land_sea = with_ends((jax.random.randint(streams_of[1], (NX, NY), 0, 8) < 7).astype(jnp.int32), jax.random.fold_in(streams_of[1], 1), 0, 1)
    depth_levels = with_ends(jax.random.randint(streams_of[2], (NX, NY), 1, NZ + 1), jax.random.fold_in(streams_of[2], 1), 1, NZ).astype(jnp.int32)
    photic_production_factors = jnp.clip(jnp.exp(jax.random.uniform(streams_of[3], (FIELDS,), jnp.float32, math.log(0.1), math.log(0.5))), 0.1, 0.5)
    species_decay_factors = jnp.clip(jnp.exp(jax.random.uniform(streams_of[4], (FIELDS,), jnp.float32, math.log(0.05), math.log(0.3))), 0.05, 0.3)
    return {"ocean_state": ocean_state, "land_sea": land_sea, "depth_levels": depth_levels, "photic_production_factors": photic_production_factors, "species_decay_factors": species_decay_factors}


CORIOLIS = 0.2
PRESSURE = 0.01


def minmod(left_diff, right_diff):
    return 0.5 * (jnp.sign(left_diff) + jnp.sign(right_diff)) * jnp.minimum(jnp.abs(left_diff), jnp.abs(right_diff))


def limited(far_low, near_low, near_high, far_high, face_speed):
    jump_mid = near_high - near_low
    left_value = near_low + 0.5 * minmod(jump_mid, near_low - far_low)
    right_value = near_high - 0.5 * minmod(jump_mid, far_high - near_high)
    return jnp.maximum(face_speed, 0.0) * left_value + jnp.minimum(face_speed, 0.0) * right_value


def advect(quantity, zonal_current, meridional_current, marine_site_indicator):
    rows_x = quantity.shape[-2] - 4
    rows_y = quantity.shape[-1] - 4
    strip = quantity[..., 2:rows_y + 2]
    face_speed = 0.5 * (zonal_current[..., 0:rows_x + 1, 1:rows_y + 1] + zonal_current[..., 1:rows_x + 2, 1:rows_y + 1])
    face_speed = face_speed * marine_site_indicator[..., 0:rows_x + 1, 1:rows_y + 1] * marine_site_indicator[..., 1:rows_x + 2, 1:rows_y + 1]
    face_flux = limited(strip[..., 0:rows_x + 1, :], strip[..., 1:rows_x + 2, :], strip[..., 2:rows_x + 3, :], strip[..., 3:rows_x + 4, :], face_speed)
    change = face_flux[..., :-1, :] - face_flux[..., 1:, :]
    strip = quantity[..., 2:rows_x + 2, :]
    face_speed = 0.5 * (meridional_current[..., 1:rows_x + 1, 0:rows_y + 1] + meridional_current[..., 1:rows_x + 1, 1:rows_y + 2])
    face_speed = face_speed * marine_site_indicator[..., 1:rows_x + 1, 0:rows_y + 1] * marine_site_indicator[..., 1:rows_x + 1, 1:rows_y + 2]
    face_flux = limited(strip[..., 0:rows_y + 1], strip[..., 1:rows_y + 2], strip[..., 2:rows_y + 3], strip[..., 3:rows_y + 4], face_speed)
    return change + face_flux[..., :-1] - face_flux[..., 1:]


def vertical_mix(quantity, vertical_stirring_coefficient):
    below_values = jnp.concatenate([quantity[..., 1:, :, :], quantity[..., -1:, :, :]], axis=-3)
    face_flux = vertical_stirring_coefficient * (below_values - quantity)
    from_above = jnp.concatenate([jnp.zeros_like(face_flux[..., :1, :, :]), face_flux[..., :-1, :, :]], axis=-3)
    return face_flux - from_above


def lateral_spreading_coefficient(seawater_heat_state, dissolved_salt_content, marine_site_indicator):
    seawater_mass_per_volume = 0.8 * dissolved_salt_content - 0.2 * seawater_heat_state
    jump_down = seawater_mass_per_volume[1:] - seawater_mass_per_volume[:-1]
    vertical_stirring_coefficient = (0.02 + 0.1 / (1.0 + 4.0 * jump_down * jump_down)) * marine_site_indicator[1:] * marine_site_indicator[:-1]
    return jnp.concatenate([vertical_stirring_coefficient, jnp.zeros_like(vertical_stirring_coefficient[:1])], axis=0)


def absorption(chlorophyll, marine_site_indicator):
    return (0.04 + 0.05 * chlorophyll * chlorophyll) * marine_site_indicator


def heating(absorb):
    lower_light = jnp.exp(-jnp.cumsum(absorb, axis=0))
    upper_light = jnp.concatenate([jnp.ones_like(lower_light[:1]), lower_light[:-1]], axis=0)
    return 0.5 * (upper_light - lower_light)


def dynamics_step(padded_with_halo_rim, marine_site_indicator, heat_rate):
    prognostic = padded_with_halo_rim[:4]
    interior = prognostic[..., 2:-2, 2:-2]
    wet_inner = marine_site_indicator[:, 2:-2, 2:-2]
    advected = advect(prognostic, padded_with_halo_rim[0, :, 1:-1, 1:-1], padded_with_halo_rim[1, :, 1:-1, 1:-1], marine_site_indicator[:, 1:-1, 1:-1])
    seawater_mass_per_volume = (0.8 * padded_with_halo_rim[3] - 0.2 * padded_with_halo_rim[2]) * marine_site_indicator
    pressure = jnp.cumsum(seawater_mass_per_volume, axis=0)
    slope_x = 0.5 * (pressure[:, 3:-1, 2:-2] - pressure[:, 1:-3, 2:-2])
    slope_y = 0.5 * (pressure[:, 2:-2, 3:-1] - pressure[:, 2:-2, 1:-3])
    vertical_stirring_coefficient = lateral_spreading_coefficient(interior[2], interior[3], wet_inner)
    forcing = jnp.stack([CORIOLIS * interior[1] - PRESSURE * slope_x, -CORIOLIS * interior[0] - PRESSURE * slope_y, heat_rate, jnp.zeros_like(heat_rate)])
    tendency = (advected + vertical_mix(interior, vertical_stirring_coefficient) + forcing) * wet_inner
    updated = (interior + 1.5 * tendency - 0.5 * padded_with_halo_rim[4:, :, 2:-2, 2:-2]) * wet_inner
    return jnp.concatenate([updated, tendency], axis=0)


def step_biogeochem_species(padded_with_halo_rim, zonal_current, meridional_current, seawater_heat_state, vertical_stirring_coefficient, marine_site_indicator, species_production, species_decay_factor):
    interior = padded_with_halo_rim[:, :, 2:-2, 2:-2]
    wet_inner = marine_site_indicator[:, 2:-2, 2:-2]
    advected = advect(padded_with_halo_rim, zonal_current, meridional_current, marine_site_indicator[:, 1:-1, 1:-1])
    solar_irradiance = jnp.exp(-jnp.cumsum(absorption(interior[0], wet_inner), axis=0))
    net_species_factor = species_production[:, None, None, None] * (solar_irradiance * jnp.exp(0.1 * seawater_heat_state))[None] - species_decay_factor[:, None, None, None]
    return (interior + advected + vertical_mix(interior, vertical_stirring_coefficient) + net_species_factor * interior) * wet_inner


def wet_cells(land_sea, depth_levels, levels):
    level_index = lax.broadcasted_iota(jnp.int32, (levels,) + land_sea.shape, 0)
    return jnp.where((land_sea[None] == 1) & (level_index < depth_levels[None]), 1.0, 0.0).astype(jnp.float32)


def pad_with_halo_rim(values, margin):
    padding = [(0, 0)] * (values.ndim - 2) + [(margin, margin), (margin, margin)]
    return jnp.pad(values, padding)


def reference(ocean_state, land_sea, depth_levels, photic_production_factors, species_decay_factors):
    marine_site_indicator = wet_cells(land_sea, depth_levels, NZ)
    marine_edge_indicator = pad_with_halo_rim(marine_site_indicator, 2)
    momentum_solver = ocean_state[0]
    species_concentrations = ocean_state[1]
    heat_rate = heating(absorption(species_concentrations[0], marine_site_indicator))
    vertical_stirring_coefficient = lateral_spreading_coefficient(momentum_solver[2], momentum_solver[3], marine_site_indicator)
    zonal_current = pad_with_halo_rim(momentum_solver[0], 1)
    meridional_current = pad_with_halo_rim(momentum_solver[1], 1)
    seawater_heat_state = momentum_solver[2]
    for step_index in range(DYN_STEPS):
        momentum_solver = dynamics_step(pad_with_halo_rim(momentum_solver, 2), marine_edge_indicator, heat_rate)
    for step_index in range(TRACER_STEPS):
        species_concentrations = step_biogeochem_species(pad_with_halo_rim(species_concentrations, 2), zonal_current, meridional_current, seawater_heat_state, vertical_stirring_coefficient, marine_edge_indicator, photic_production_factors, species_decay_factors)
    return jnp.stack([momentum_solver, species_concentrations])
```

```python
import functools

import jax
import jax.numpy as jnp
from jax import lax
from jax.experimental import pallas as pl
from jax.experimental.pallas import tpu as pltpu
from jax.sharding import PartitionSpec as P

DYN_STEPS = 4
TRACER_STEPS = 2
CORIOLIS = 0.2
PRESSURE = 0.01

LEVELS = 8
LANES = 128
FIELDS = 8
PROG = 4
ROWS = 4
HALO = 8
MAIN = 2 * FIELDS * ROWS
EDGE = 2 * ROWS
NEAR = MAIN + EDGE + 1
FAR_G = PROG * ROWS
FAR_CHL = FAR_G + PROG * 2
FAR_EDGE = FAR_CHL + 2
FAR = FAR_EDGE + EDGE + 1
DYN_ROWS = 5 * ROWS
TRC_ROWS = 3 * ROWS
TILE = (LEVELS, LANES)


def lanes():
    return lax.broadcasted_iota(jnp.int32, TILE, 1)


def level_index():
    return lax.broadcasted_iota(jnp.int32, TILE, 0)


def edge_source(comp):
    first = jnp.where(comp == 0, LANES - HALO, 0)
    lane = lanes()
    return (lane >= first) & (lane < first + HALO)


def wet_count(land_ref, depth_ref):
    return jnp.where(land_ref[...] == 1, depth_ref[...], 0).astype(jnp.float32)


def row_of(own_ref, comp, field, row):
    return own_ref[comp, field, pl.ds(row, LEVELS, stride=ROWS), :]


def pack_columns(comp_ref, own_ref, land_ref, depth_ref, out_ref):
    source = edge_source(comp_ref[0])
    for c in range(2):
        for r in range(ROWS):
            total = None
            for f in range(FIELDS):
                part = jnp.where(source, row_of(own_ref, c, f, r), 0.0)
                part = pltpu.roll(part, (16 * f + HALO) % LANES, 1)
                total = part if total is None else total + part
            out_ref[c * ROWS + r] = total
    count = wet_count(land_ref, depth_ref)
    out_ref[EDGE] = jnp.zeros(TILE, jnp.float32)
    out_ref[EDGE, 0:ROWS, :] = jnp.where(source[0:ROWS], count, 0.0)


def pack_rows(comp_ref, own_ref, land_ref, depth_ref, side_ref, near_ref, far_ref):
    first = jnp.where(comp_ref[0] == 0, 2, 0)
    for c in range(2):
        for f in range(FIELDS):
            for r in range(ROWS):
                tile = row_of(own_ref, c, f, r)
                near_ref[(c * FIELDS + f) * ROWS + r] = tile
                if c == 0 and f < PROG:
                    far_ref[f * ROWS + r] = tile
    for k in range(2):
        for f in range(PROG):
            far_ref[FAR_G + f * 2 + k] = row_of(own_ref, 0, PROG + f, first + k)
        far_ref[FAR_CHL + k] = row_of(own_ref, 1, 0, first + k)
    for t in range(EDGE):
        both = side_ref[0, t] + side_ref[1, t]
        near_ref[MAIN + t] = both
        far_ref[FAR_EDGE + t] = both
    count = wet_count(land_ref, depth_ref)
    outer = side_ref[0, EDGE, 0:ROWS, :] + side_ref[1, EDGE, 0:ROWS, :]
    near_ref[MAIN + EDGE, 0:ROWS, :] = count
    near_ref[MAIN + EDGE, ROWS : 2 * ROWS, :] = outer
    far_ref[FAR_EDGE + EDGE, 0:ROWS, :] = count
    far_ref[FAR_EDGE + EDGE, ROWS : 2 * ROWS, :] = outer


def next_column(pair):
    here, beyond = pair
    last = lanes() == LANES - 1
    a, b = pltpu.roll(here, LANES - 1, 1), pltpu.roll(beyond, LANES - 1, 1)
    return jnp.where(last, b, a), jnp.where(last, a, b)


def previous_column(pair):
    here, beyond = pair
    start = lanes() == 0
    a, b = pltpu.roll(here, 1, 1), pltpu.roll(beyond, 1, 1)
    return jnp.where(start, b, a), jnp.where(start, a, b)


def both(function, *pairs):
    return tuple(function(*values) for values in zip(*pairs))


def half_minmod(a, b):
    return 0.5 * (jnp.maximum(jnp.minimum(a, b), 0.0) + jnp.minimum(jnp.maximum(a, b), 0.0))


def level_sum(values):
    level = level_index()
    for by in (1, 2, 4):
        values = values + jnp.where(level >= by, pltpu.roll(values, by, 0), 0.0)
    return values


def below(values):
    return pltpu.roll(values, LEVELS - 1, 0)


def above(values):
    return pltpu.roll(values, 1, 0)


def density(temperature, salinity):
    return 0.8 * salinity - 0.2 * temperature


def stirring(rho, column_wet):
    jump = below(rho) - rho
    return (0.02 + 0.1 / (1.0 + 4.0 * jump * jump)) * column_wet


def column_mix(quantity, mixing):
    flux = mixing * (below(quantity) - quantity)
    return flux - above(flux)


def across(quantity, shifted, plus, minus):
    jump = both(lambda n, q: n - q, shifted, quantity)
    slope = both(half_minmod, jump, previous_column(jump))
    low = both(lambda q, s: q + s, quantity, slope)
    high = next_column(both(lambda q, s: q - s, quantity, slope))
    flux = both(lambda p, lo, m, hi: p * lo + m * hi, plus, low, minus, high)
    return both(lambda before, after: before - after, previous_column(flux), flux)


def split(speed):
    return jnp.maximum(speed, 0.0), jnp.minimum(speed, 0.0)


def face_start(ref, fields, row):
    out = []
    for f in fields:
        here = [ref[f, row, t] for t in range(2)]
        jump = [ref[f, row + 1, t] - here[t] for t in range(2)]
        left = [here[t] + half_minmod(jump[t], here[t] - ref[f, row - 1, t]) for t in range(2)]
        out.append((tuple(jump), tuple(left)))
    return out


def face_step(ref, field, row, jump, left, plus, minus):
    jumps, lefts, fluxes = [], [], []
    for t in range(2):
        near = ref[field, row + 1, t]
        ahead = ref[field, row + 2, t] - near
        slope = half_minmod(ahead, jump[t])
        fluxes.append(plus[t] * left[t] + minus[t] * (near - slope))
        jumps.append(ahead)
        lefts.append(near + slope)
    return tuple(jumps), tuple(lefts), tuple(fluxes)


def load_wet(count_ref, index, row, wet_ref, at):
    level = level_index().astype(jnp.float32)
    for t in range(2):
        count = count_ref[index + (slice(t * ROWS + row, t * ROWS + row + 1), slice(None))]
        wet_ref[at, t] = jnp.where(level < count, 1.0, 0.0)


def unpack_edge(edge, field):
    return pltpu.roll(edge, (2 * LANES - HALO - 16 * field) % LANES, 1)


def masks(wet_ref, facex_ref, facey_ref, facez_ref, rows):
    not_last = level_index() < LEVELS - 1

    def body(i, carry):
        here = (wet_ref[i, 0], wet_ref[i, 1])
        beside = next_column(here)
        for t in range(2):
            facey_ref[i, t] = 0.5 * here[t] * beside[t]
            facez_ref[i, t] = jnp.where(not_last, here[t] * below(here[t]), 0.0)
        return carry

    lax.fori_loop(0, rows, body, 0)

    def body_x(i, carry):
        for t in range(2):
            facex_ref[i, t] = 0.5 * wet_ref[i, t] * wet_ref[i + 1, t]
        return carry

    lax.fori_loop(0, rows - 1, body_x, 0)


def dynamics(own_ref, near_ref, far_ref, out_ref, q_ref, g_ref, heat_ref, wet_ref, facex_ref, facey_ref, facez_ref):
    blocks = ((far_ref, (0,)), (near_ref, (0,)), (own_ref, ()), (near_ref, (1,)), (far_ref, (1,)))
    for b, (ref, lead) in enumerate(blocks):
        far = b in (0, 4)
        edge_at = FAR_EDGE if far else MAIN
        for r in range(ROWS):
            row = b * ROWS + r
            load_wet(ref, lead + (edge_at + EDGE,), r, wet_ref, row)
            edge = ref[lead + (edge_at + r,)]
            for f in range(PROG):
                q_ref[0, f, row, 0] = ref[lead + (f * ROWS + r,)]
                q_ref[0, f, row, 1] = unpack_edge(edge, f)
            k = r - 2 if b == 0 else r
            if not 2 <= row < DYN_ROWS - 2:
                continue
            for f in range(PROG):
                at = FAR_G + f * 2 + k if far else (PROG + f) * ROWS + r
                g_ref[f, row, 0] = ref[lead + (at,)]
                g_ref[f, row, 1] = unpack_edge(edge, PROG + f)
            chl_at = FAR_CHL + k if far else FIELDS * ROWS + r
            chl_edge = ref[lead + (edge_at + ROWS + r,)]
            chl = (ref[lead + (chl_at,)], unpack_edge(chl_edge, 0))
            for t in range(2):
                absorb = (0.04 + 0.05 * chl[t] * chl[t]) * wet_ref[row, t]
                lower = jnp.exp(-level_sum(absorb))
                upper = jnp.where(level_index() == 0, 1.0, above(lower))
                heat_ref[row, t] = 0.5 * (upper - lower)
    masks(wet_ref, facex_ref, facey_ref, facez_ref, DYN_ROWS)

    def column(src, row):
        rho = [density(src[2, row, t], src[3, row, t]) for t in range(2)]
        pressure = [level_sum(rho[t] * wet_ref[row, t]) for t in range(2)]
        return tuple(rho), tuple(pressure)

    for step in range(DYN_STEPS):
        src, dst = q_ref.at[step % 2], q_ref.at[(step + 1) % 2]
        first, end = 2 * (step + 1), DYN_ROWS - 2 * (step + 1)
        last_step = step == DYN_STEPS - 1

        def speed_x(row):
            return [split(facex_ref[row, t] * (src[0, row, t] + src[0, row + 1, t])) for t in range(2)]

        started = face_start(src, range(PROG), first - 1)
        speeds = speed_x(first - 1)
        streams = tuple(
            face_step(src, f, first - 1, *started[f], [s[0] for s in speeds], [s[1] for s in speeds])
            for f in range(PROG)
        )
        _, before = column(src, first - 1)
        rho, pressure = column(src, first)

        def body(i, carry, src=src, dst=dst, speed_x=speed_x, last_step=last_step):
            streams, before, rho, pressure = carry
            rho_after, after = column(src, i + 1)
            wet = [wet_ref[i, t] for t in range(2)]
            here = [(src[f, i, 0], src[f, i, 1]) for f in range(PROG)]
            shifted = [next_column(h) for h in here]
            speeds = speed_x(i)
            plus_x, minus_x = [s[0] for s in speeds], [s[1] for s in speeds]
            speeds = [split(facey_ref[i, t] * (here[1][t] + shifted[1][t])) for t in range(2)]
            plus_y, minus_y = [s[0] for s in speeds], [s[1] for s in speeds]
            mixing = [stirring(rho[t], facez_ref[i, t]) for t in range(2)]
            east, west = next_column(pressure), previous_column(pressure)
            new = []
            for f in range(PROG):
                jump, left, entering = streams[f]
                jump, left, leaving = face_step(src, f, i, jump, left, plus_x, minus_x)
                new.append((jump, left, leaving))
                sideways = across(here[f], shifted[f], plus_y, minus_y)
                for t in range(1 if last_step else 2):
                    tendency = entering[t] - leaving[t] + sideways[t] + column_mix(here[f][t], mixing[t])
                    if f == 0:
                        tendency += CORIOLIS * here[1][t] - (0.5 * PRESSURE) * (after[t] - before[t])
                    elif f == 1:
                        tendency += -CORIOLIS * here[0][t] - (0.5 * PRESSURE) * (east[t] - west[t])
                    elif f == 2:
                        tendency += heat_ref[i, t]
                    tendency = tendency * wet[t]
                    updated = (here[f][t] + 1.5 * tendency - 0.5 * g_ref[f, i, t]) * wet[t]
                    if last_step:
                        rows = pl.ds(i - 2 * ROWS, LEVELS, stride=ROWS)
                        out_ref[f, rows, :] = updated
                        out_ref[PROG + f, rows, :] = tendency
                    else:
                        dst[f, i, t] = updated
                        g_ref[f, i, t] = tendency
            return tuple(new), pressure, rho_after, after

        lax.fori_loop(first, end, body, (streams, before, rho, pressure))


def tracers(
    growth_ref, decay_ref, own_ref, near_ref, out_ref,
    c_ref, flow_ref, speed_ref, mix_ref, warm_ref, light_ref, wet_ref, facex_ref, facey_ref, facez_ref,
):
    blocks = ((near_ref, (0,)), (own_ref, ()), (near_ref, (1,)))
    for b, (ref, lead) in enumerate(blocks):
        for r in range(ROWS):
            row = b * ROWS + r
            load_wet(ref, lead + (MAIN + EDGE,), r, wet_ref, row)
            edge = ref[lead + (MAIN + ROWS + r,)]
            for f in range(FIELDS):
                c_ref[0, f, row, 0] = ref[lead + ((FIELDS + f) * ROWS + r,)]
                c_ref[0, f, row, 1] = unpack_edge(edge, f)
            edge = ref[lead + (MAIN + r,)]
            for f in range(PROG):
                flow_ref[f, row, 0] = ref[lead + (f * ROWS + r,)]
                flow_ref[f, row, 1] = unpack_edge(edge, f)
    masks(wet_ref, facex_ref, facey_ref, facez_ref, TRC_ROWS)

    def prepare(i, carry):
        beside = next_column((flow_ref[1, i, 0], flow_ref[1, i, 1]))
        for t in range(2):
            plus, minus = split(facex_ref[i, t] * (flow_ref[0, i, t] + flow_ref[0, i + 1, t]))
            speed_ref[0, i, t] = plus
            speed_ref[1, i, t] = minus
            plus, minus = split(facey_ref[i, t] * (flow_ref[1, i, t] + beside[t]))
            speed_ref[2, i, t] = plus
            speed_ref[3, i, t] = minus
            mix_ref[i, t] = stirring(density(flow_ref[2, i, t], flow_ref[3, i, t]), facez_ref[i, t])
            warm_ref[i, t] = jnp.exp(0.1 * flow_ref[2, i, t])
        return carry

    lax.fori_loop(1, TRC_ROWS - 2, prepare, 0)

    group = 4
    for step in range(TRACER_STEPS):
        src, dst = c_ref.at[step % 2], c_ref.at[(step + 1) % 2]
        first, end = 2 * (step + 1), TRC_ROWS - 2 * (step + 1)
        last_step = step == TRACER_STEPS - 1

        def shade(i, carry, src=src):
            for t in range(2):
                chl = src[0, i, t]
                absorb = (0.04 + 0.05 * chl * chl) * wet_ref[i, t]
                light_ref[i, t] = jnp.exp(-level_sum(absorb)) * warm_ref[i, t]
            return carry

        lax.fori_loop(first, end, shade, 0)

        def some(n, carry, src=src, dst=dst, first=first, end=end, last_step=last_step):
            fields = [n * group + k for k in range(group)]

            def pair(ref, *index):
                return (ref[index + (0,)], ref[index + (1,)])

            started = face_start(src, fields, first - 1)
            plus, minus = pair(speed_ref, 0, first - 1), pair(speed_ref, 1, first - 1)
            streams = tuple(
                face_step(src, f, first - 1, *started[k], plus, minus) for k, f in enumerate(fields)
            )

            def body(i, streams):
                plus_x, minus_x = pair(speed_ref, 0, i), pair(speed_ref, 1, i)
                plus_y, minus_y = pair(speed_ref, 2, i), pair(speed_ref, 3, i)
                new = []
                for k, f in enumerate(fields):
                    jump, left, entering = streams[k]
                    jump, left, leaving = face_step(src, f, i, jump, left, plus_x, minus_x)
                    new.append((jump, left, leaving))
                    here = pair(src, f, i)
                    sideways = across(here, next_column(here), plus_y, minus_y)
                    for t in range(1 if last_step else 2):
                        net = growth_ref[f] * light_ref[i, t] - decay_ref[f]
                        change = entering[t] - leaving[t] + sideways[t] + column_mix(here[t], mix_ref[i, t])
                        updated = (here[t] + change + net * here[t]) * wet_ref[i, t]
                        if last_step:
                            out_ref[f, pl.ds(i - ROWS, LEVELS, stride=ROWS), :] = updated
                        else:
                            dst[f, i, t] = updated
                return tuple(new)

            lax.fori_loop(first, end, body, streams)
            return carry

        lax.fori_loop(0, FIELDS // group, some, 0)


def advance(
    comp_ref, growth_ref, decay_ref, own_ref, near_ref, far_ref, out_ref,
    q_ref, g_ref, heat_ref, c_ref, flow_ref, speed_ref, mix_ref, warm_ref, light_ref,
    wet_ref, facex_ref, facey_ref, facez_ref,
):
    @pl.when(comp_ref[0] == 0)
    def _():
        dynamics(own_ref, near_ref, far_ref, out_ref, q_ref, g_ref, heat_ref, wet_ref, facex_ref, facey_ref, facez_ref)

    @pl.when(comp_ref[0] == 1)
    def _():
        tracers(
            growth_ref, decay_ref, own_ref, near_ref, out_ref,
            c_ref, flow_ref, speed_ref, mix_ref, warm_ref, light_ref, wet_ref, facex_ref, facey_ref, facez_ref,
        )


def call(kernel, smem, vmem, outs, scratch=(), flops=0):
    out_shape = tuple(jax.ShapeDtypeStruct(s, jnp.float32) for s in outs)
    size = 4 * sum(a.size for a in vmem) + 4 * sum(s.size for s in out_shape)
    result = pl.pallas_call(
        kernel,
        out_shape=out_shape,
        in_specs=[pl.BlockSpec(memory_space=pltpu.SMEM)] * len(smem)
        + [pl.BlockSpec(memory_space=pltpu.VMEM)] * len(vmem),
        out_specs=tuple(pl.BlockSpec(memory_space=pltpu.VMEM) for _ in outs),
        scratch_shapes=[pltpu.VMEM(s + TILE, jnp.float32) for s in scratch],
        compiler_params=pltpu.CompilerParams(vmem_limit_bytes=24 * 1024 * 1024),
        cost_estimate=pl.CostEstimate(flops=flops, bytes_accessed=size, transcendentals=0),
    )(*smem, *vmem)
    return result


def neighbours(gx, gy, by_x, by_y):
    pairs = []
    for c, way in ((0, 1), (1, -1)):
        for i in range(gx):
            for j in range(gy):
                a, b = i + way * by_x, j + way * by_y
                if 0 <= a < gx and 0 <= b < gy:
                    pairs.append(((c * gx + i) * gy + j, (c * gx + a) * gy + b))
    return pairs


def local(ocean_state, land_sea, depth_levels, growth, decay):
    axes = ("comp", "gx", "gy")
    gx, gy = lax.axis_size("gx"), lax.axis_size("gy")
    comp = lax.axis_index("comp").astype(jnp.int32).reshape(1)
    fields = ocean_state.reshape(FIELDS, LEVELS * ROWS, LANES)
    own = lax.all_gather(fields, "comp")
    (columns,) = call(pack_columns, [comp], [own, land_sea, depth_levels], [(EDGE + 1,) + TILE])
    columns = lax.ppermute(columns, axes, neighbours(gx, gy, 0, 1))
    sides = lax.all_gather(columns, "comp")
    near, far = call(
        pack_rows, [comp], [own, land_sea, depth_levels, sides], [(NEAR,) + TILE, (FAR,) + TILE]
    )
    near_in = lax.ppermute(near, axes, neighbours(gx, gy, 1, 0))
    far_in = lax.ppermute(far, axes, neighbours(gx, gy, 2, 0))
    near_in, far_in = lax.all_gather((near_in, far_in), "comp")
    scratch = [
        (2, PROG, DYN_ROWS, 2),
        (PROG, DYN_ROWS, 2),
        (DYN_ROWS, 2),
        (2, FIELDS, TRC_ROWS, 2),
        (PROG, TRC_ROWS, 2),
        (4, TRC_ROWS, 2),
        (TRC_ROWS, 2),
        (TRC_ROWS, 2),
        (TRC_ROWS, 2),
        (DYN_ROWS, 2),
        (DYN_ROWS, 2),
        (DYN_ROWS, 2),
        (DYN_ROWS, 2),
    ]
    (out,) = call(
        advance, [comp, growth, decay], [near, near_in, far_in],
        [(FIELDS, LEVELS * ROWS, LANES)], scratch, flops=20_000_000,
    )
    return out.reshape(ocean_state.shape)


def solution(mesh):
    placed = (P("comp", None, None, "gx", "gy"), P("gx", "gy"), P("gx", "gy"), P(), P())
    return jax.shard_map(
        local,
        mesh=mesh,
        in_specs=placed,
        out_specs=P("comp", None, None, "gx", "gy"),
        check_vma=False,
    )
```

```python
import functools

import jax
import jax.numpy as jnp
from jax import lax
from jax.experimental import pallas as pl
from jax.experimental.pallas import tpu as pltpu
from jax.sharding import PartitionSpec as P

DYN_STEPS = 4
TRACER_STEPS = 2
CORIOLIS = 0.2
PRESSURE = 0.01

LEVELS = 8
LANES = 128
FIELDS = 8
PROG = 4
ROWS = 4
HALO = 8
MAIN = 2 * FIELDS * ROWS
EDGE = 2 * ROWS
SIDE = EDGE + 1
FAR_G = PROG * ROWS
FAR_CHL = FAR_G + PROG * 2
FAR_EDGE = FAR_CHL + 2
FAR_CHL_EDGE = FAR_EDGE + ROWS
FAR_WET = FAR_CHL_EDGE + 2
FAR = FAR_WET + 1
IN_SIDE = MAIN
IN_FAR = MAIN + SIDE
IN = IN_FAR + FAR
DYN_ROWS = 5 * ROWS
TRC_ROWS = 3 * ROWS
TILE = (LEVELS, LANES)
DYN_UNROLL = 4
TRC_UNROLL = 4


def lanes():
    return lax.broadcasted_iota(jnp.int32, TILE, 1)


def level_index():
    return lax.broadcasted_iota(jnp.int32, TILE, 0)


def edge_source(comp):
    first = jnp.where(comp == 0, LANES - HALO, 0)
    lane = lanes()
    return (lane >= first) & (lane < first + HALO)


def wet_count(land_ref, depth_ref):
    return jnp.where(land_ref[...] == 1, depth_ref[...], 0).astype(jnp.float32)


def row_of(own_ref, comp, field, row):
    return own_ref[comp, field, pl.ds(row, LEVELS, stride=ROWS), :]


def pack_columns(comp_ref, growth_ref, decay_ref, own_ref, land_ref, depth_ref, out_ref, rates_ref):
    source = edge_source(comp_ref[0])
    for c in range(2):
        for r in range(ROWS):
            total = None
            for f in range(FIELDS):
                part = jnp.where(source, row_of(own_ref, c, f, r), 0.0)
                part = pltpu.roll(part, (16 * f + HALO) % LANES, 1)
                total = part if total is None else total + part
            out_ref[c * ROWS + r] = total
    count = wet_count(land_ref, depth_ref)
    out_ref[EDGE] = jnp.zeros(TILE, jnp.float32)
    out_ref[EDGE, 0:ROWS, :] = jnp.where(source[0:ROWS], count, 0.0)
    for f in range(FIELDS):
        rates_ref[0, f : f + 1, :] = jnp.full((1, LANES), growth_ref[f])
        rates_ref[1, f : f + 1, :] = jnp.full((1, LANES), decay_ref[f])


def pack_rows(comp_ref, own_ref, land_ref, depth_ref, columns_ref, side_ref, far_ref):
    first = jnp.where(comp_ref[0] == 0, 2, 0)
    for f in range(PROG):
        for r in range(ROWS):
            far_ref[f * ROWS + r] = row_of(own_ref, 0, f, r)
    for k in range(2):
        for f in range(PROG):
            far_ref[FAR_G + f * 2 + k] = row_of(own_ref, 0, PROG + f, first + k)
        far_ref[FAR_CHL + k] = row_of(own_ref, 1, 0, first + k)
        at = ROWS + first + k
        far_ref[FAR_CHL_EDGE + k] = columns_ref[0, at] + columns_ref[1, at]
    for t in range(EDGE):
        joined = columns_ref[0, t] + columns_ref[1, t]
        side_ref[t] = joined
        if t < ROWS:
            far_ref[FAR_EDGE + t] = joined
    count = wet_count(land_ref, depth_ref)
    outer = columns_ref[0, EDGE, 0:ROWS, :] + columns_ref[1, EDGE, 0:ROWS, :]
    for ref, at in ((side_ref, EDGE), (far_ref, FAR_WET)):
        ref[at, 0:ROWS, :] = count
        ref[at, ROWS : 2 * ROWS, :] = outer


def join(main_ref, side_ref, far_ref, out_ref):
    at = 0
    for ref in (main_ref, side_ref, far_ref):
        size = ref.shape[0]
        out_ref[at : at + size, :] = ref[...]
        at += size


class Block:
    def __init__(self, main, edge, wet, g_rows=range(ROWS)):
        self.main, self.edge, self.wet, self.g_rows = main, edge, wet, g_rows


def own_block(own_ref, side_ref):
    return Block(
        lambda c, f, r: row_of(own_ref, c, f, r),
        lambda c, r: side_ref[c * ROWS + r],
        lambda row: side_ref[EDGE, row : row + 1, :],
    )


def near_block(in_ref, way):
    def tile(index):
        return in_ref[way, (IN_SIDE + index) * LEVELS : (IN_SIDE + index + 1) * LEVELS, :]

    at = (IN_SIDE + EDGE) * LEVELS
    return Block(
        lambda c, f, r: in_ref[way, pl.ds((c * FIELDS + f) * LEVELS * ROWS + r, LEVELS, stride=ROWS), :],
        lambda c, r: tile(c * ROWS + r),
        lambda row: in_ref[way, at + row : at + row + 1, :],
    )


def far_block(in_ref, way):
    first = 2 if way == 0 else 0

    def tile(index):
        return in_ref[way, (IN_FAR + index) * LEVELS : (IN_FAR + index + 1) * LEVELS, :]

    def main(c, f, r):
        if c == 1:
            return tile(FAR_CHL + r - first)
        return tile(f * ROWS + r if f < PROG else FAR_G + (f - PROG) * 2 + r - first)

    at = (IN_FAR + FAR_WET) * LEVELS
    return Block(
        main,
        lambda c, r: tile(FAR_EDGE + r if c == 0 else FAR_CHL_EDGE + r - first),
        lambda row: in_ref[way, at + row : at + row + 1, :],
        range(first, first + 2),
    )


def next_column(pair):
    here, beyond = pair
    last = lanes() == LANES - 1
    a, b = pltpu.roll(here, LANES - 1, 1), pltpu.roll(beyond, LANES - 1, 1)
    return jnp.where(last, b, a), jnp.where(last, a, b)


def previous_column(pair):
    here, beyond = pair
    start = lanes() == 0
    a, b = pltpu.roll(here, 1, 1), pltpu.roll(beyond, 1, 1)
    return jnp.where(start, b, a), jnp.where(start, a, b)


def both(function, *pairs):
    return tuple(function(*values) for values in zip(*pairs))


def half_minmod(a, b):
    return 0.5 * (jnp.maximum(jnp.minimum(a, b), 0.0) + jnp.minimum(jnp.maximum(a, b), 0.0))


def level_sum(values):
    level = level_index()
    for by in (1, 2, 4):
        values = values + jnp.where(level >= by, pltpu.roll(values, by, 0), 0.0)
    return values


def below(values):
    return pltpu.roll(values, LEVELS - 1, 0)


def above(values):
    return pltpu.roll(values, 1, 0)


def density(temperature, salinity):
    return 0.8 * salinity - 0.2 * temperature


def stirring(rho, column_wet):
    jump = below(rho) - rho
    return (0.02 + 0.1 / (1.0 + 4.0 * jump * jump)) * column_wet


def column_mix(quantity, mixing):
    flux = mixing * (below(quantity) - quantity)
    return flux - above(flux)


def across(quantity, shifted, out_speed, in_speed):
    slope = both(lambda n, q, p: half_minmod(n - q, q - p), shifted, quantity, previous_column(quantity))
    low = both(lambda q, s: q + s, quantity, slope)
    high = both(lambda q, s: q - s, quantity, slope)
    leaving = both(lambda s, lo, hi: s[0] * lo + s[1] * hi, out_speed, low, next_column(high))
    entering = both(lambda s, lo, hi: s[0] * lo + s[1] * hi, in_speed, previous_column(low), high)
    return both(lambda before, after: before - after, entering, leaving)


def split(speed):
    return jnp.maximum(speed, 0.0), jnp.minimum(speed, 0.0)


def face_start(ref, fields, row):
    out = []
    for f in fields:
        here = [ref[f, row, t] for t in range(2)]
        jump = [ref[f, row + 1, t] - here[t] for t in range(2)]
        left = [here[t] + half_minmod(jump[t], here[t] - ref[f, row - 1, t]) for t in range(2)]
        out.append((tuple(jump), tuple(left)))
    return out


def face_step(ref, field, row, jump, left, plus, minus):
    jumps, lefts, fluxes = [], [], []
    for t in range(2):
        near = ref[field, row + 1, t]
        ahead = ref[field, row + 2, t] - near
        slope = half_minmod(ahead, jump[t])
        fluxes.append(plus[t] * left[t] + minus[t] * (near - slope))
        jumps.append(ahead)
        lefts.append(near + slope)
    return tuple(jumps), tuple(lefts), tuple(fluxes)


def load_wet(block, r, wet_ref, row):
    level = level_index().astype(jnp.float32)
    for t in range(2):
        wet_ref[row, t] = jnp.where(level < block.wet(t * ROWS + r), 1.0, 0.0)


def unpack_edge(edge, field):
    return pltpu.roll(edge, (2 * LANES - HALO - 16 * field) % LANES, 1)


def masks(wet_ref, facex_ref, facey_ref, facez_ref, rows):
    not_last = level_index() < LEVELS - 1

    def body(i, carry):
        here = (wet_ref[i, 0], wet_ref[i, 1])
        beside = next_column(here)
        for t in range(2):
            facey_ref[i, t] = 0.5 * here[t] * beside[t]
            facez_ref[i, t] = jnp.where(not_last, here[t] * below(here[t]), 0.0)
        return carry

    lax.fori_loop(0, rows, body, 0, unroll=4)

    def body_x(i, carry):
        for t in range(2):
            facex_ref[i, t] = 0.5 * wet_ref[i, t] * wet_ref[i + 1, t]
        return carry

    lax.fori_loop(0, rows - 1, body_x, 0)


def dynamics(own_ref, side_ref, in_ref, out_ref, q_ref, g_ref, heat_ref, wet_ref, facex_ref, facey_ref, facez_ref):
    blocks = (
        far_block(in_ref, 0),
        near_block(in_ref, 0),
        own_block(own_ref, side_ref),
        near_block(in_ref, 1),
        far_block(in_ref, 1),
    )
    for b, block in enumerate(blocks):
        for r in range(ROWS):
            row = b * ROWS + r
            load_wet(block, r, wet_ref, row)
            edge = block.edge(0, r)
            for f in range(PROG):
                q_ref[0, f, row, 0] = block.main(0, f, r)
                q_ref[0, f, row, 1] = unpack_edge(edge, f)
            if r not in block.g_rows:
                continue
            for f in range(PROG):
                g_ref[f, row, 0] = block.main(0, PROG + f, r)
                g_ref[f, row, 1] = unpack_edge(edge, PROG + f)
            chl = (block.main(1, 0, r), unpack_edge(block.edge(1, r), 0))
            for t in range(2):
                absorb = (0.04 + 0.05 * chl[t] * chl[t]) * wet_ref[row, t]
                lower = jnp.exp(-level_sum(absorb))
                upper = jnp.where(level_index() == 0, 1.0, above(lower))
                heat_ref[row, t] = 0.5 * (upper - lower)
    masks(wet_ref, facex_ref, facey_ref, facez_ref, DYN_ROWS)

    def column(src, row):
        rho = [density(src[2, row, t], src[3, row, t]) for t in range(2)]
        pressure = [level_sum(rho[t] * wet_ref[row, t]) for t in range(2)]
        return tuple(rho), tuple(pressure)

    for step in range(DYN_STEPS):
        src, dst = q_ref.at[step % 2], q_ref.at[(step + 1) % 2]
        first, end = 2 * (step + 1), DYN_ROWS - 2 * (step + 1)
        last_step = step == DYN_STEPS - 1

        def speed_x(row):
            return [split(facex_ref[row, t] * (src[0, row, t] + src[0, row + 1, t])) for t in range(2)]

        started = face_start(src, range(PROG), first - 1)
        speeds = speed_x(first - 1)
        streams = tuple(
            face_step(src, f, first - 1, *started[f], [s[0] for s in speeds], [s[1] for s in speeds])
            for f in range(PROG)
        )
        _, before = column(src, first - 1)
        rho, pressure = column(src, first)

        def body(i, carry, src=src, dst=dst, speed_x=speed_x, last_step=last_step):
            streams, before, rho, pressure = carry
            rho_after, after = column(src, i + 1)
            wet = [wet_ref[i, t] for t in range(2)]
            here = [(src[f, i, 0], src[f, i, 1]) for f in range(PROG)]
            shifted = [next_column(h) for h in here]
            speeds = speed_x(i)
            plus_x, minus_x = [s[0] for s in speeds], [s[1] for s in speeds]
            speed = tuple(facey_ref[i, t] * (here[1][t] + shifted[1][t]) for t in range(2))
            out_y = both(split, speed)
            in_y = both(split, previous_column(speed))
            mixing = [stirring(rho[t], facez_ref[i, t]) for t in range(2)]
            east, west = next_column(pressure), previous_column(pressure)
            new = []
            for f in range(PROG):
                jump, left, entering = streams[f]
                jump, left, leaving = face_step(src, f, i, jump, left, plus_x, minus_x)
                new.append((jump, left, leaving))
                sideways = across(here[f], shifted[f], out_y, in_y)
                for t in range(1 if last_step else 2):
                    tendency = entering[t] - leaving[t] + sideways[t] + column_mix(here[f][t], mixing[t])
                    if f == 0:
                        tendency += CORIOLIS * here[1][t] - (0.5 * PRESSURE) * (after[t] - before[t])
                    elif f == 1:
                        tendency += -CORIOLIS * here[0][t] - (0.5 * PRESSURE) * (east[t] - west[t])
                    elif f == 2:
                        tendency += heat_ref[i, t]
                    tendency = tendency * wet[t]
                    updated = (here[f][t] + 1.5 * tendency - 0.5 * g_ref[f, i, t]) * wet[t]
                    if last_step:
                        rows = pl.ds(i - 2 * ROWS, LEVELS, stride=ROWS)
                        out_ref[f, rows, :] = updated
                        out_ref[PROG + f, rows, :] = tendency
                    else:
                        dst[f, i, t] = updated
                        g_ref[f, i, t] = tendency
            return tuple(new), pressure, rho_after, after

        lax.fori_loop(first, end, body, (streams, before, rho, pressure), unroll=DYN_UNROLL)


def tracers(
    rates_ref, own_ref, side_ref, in_ref, out_ref,
    c_ref, flow_ref, speed_ref, mix_ref, warm_ref, light_ref, wet_ref, facex_ref, facey_ref, facez_ref,
):
    blocks = (near_block(in_ref, 0), own_block(own_ref, side_ref), near_block(in_ref, 1))
    for b, block in enumerate(blocks):
        for r in range(ROWS):
            row = b * ROWS + r
            load_wet(block, r, wet_ref, row)
            edge = block.edge(1, r)
            for f in range(FIELDS):
                c_ref[0, f, row, 0] = block.main(1, f, r)
                c_ref[0, f, row, 1] = unpack_edge(edge, f)
            edge = block.edge(0, r)
            for f in range(PROG):
                flow_ref[f, row, 0] = block.main(0, f, r)
                flow_ref[f, row, 1] = unpack_edge(edge, f)
    masks(wet_ref, facex_ref, facey_ref, facez_ref, TRC_ROWS)

    def prepare(i, carry):
        north = (flow_ref[1, i, 0], flow_ref[1, i, 1])
        speed = tuple(facey_ref[i, t] * (north[t] + n) for t, n in enumerate(next_column(north)))
        before = previous_column(speed)
        for t in range(2):
            plus, minus = split(facex_ref[i, t] * (flow_ref[0, i, t] + flow_ref[0, i + 1, t]))
            speed_ref[0, i, t] = plus
            speed_ref[1, i, t] = minus
            speed_ref[2, i, t] = speed[t]
            speed_ref[3, i, t] = before[t]
            mix_ref[i, t] = stirring(density(flow_ref[2, i, t], flow_ref[3, i, t]), facez_ref[i, t])
            warm_ref[i, t] = jnp.exp(0.1 * flow_ref[2, i, t])
        return carry

    lax.fori_loop(1, TRC_ROWS - 2, prepare, 0)

    group = 4
    for step in range(TRACER_STEPS):
        src, dst = c_ref.at[step % 2], c_ref.at[(step + 1) % 2]
        first, end = 2 * (step + 1), TRC_ROWS - 2 * (step + 1)
        last_step = step == TRACER_STEPS - 1

        def shade(i, carry, src=src):
            for t in range(2):
                chl = src[0, i, t]
                absorb = (0.04 + 0.05 * chl * chl) * wet_ref[i, t]
                light_ref[i, t] = jnp.exp(-level_sum(absorb)) * warm_ref[i, t]
            return carry

        lax.fori_loop(first, end, shade, 0, unroll=4)

        def some(n, carry, src=src, dst=dst, first=first, end=end, last_step=last_step):
            fields = [n * group + k for k in range(group)]

            def pair(ref, *index):
                return (ref[index + (0,)], ref[index + (1,)])

            started = face_start(src, fields, first - 1)
            plus, minus = pair(speed_ref, 0, first - 1), pair(speed_ref, 1, first - 1)
            streams = tuple(
                face_step(src, f, first - 1, *started[k], plus, minus) for k, f in enumerate(fields)
            )

            rates = [(rates_ref[0, pl.ds(f, 1), :], rates_ref[1, pl.ds(f, 1), :]) for f in fields]

            def body(i, streams):
                plus_x, minus_x = pair(speed_ref, 0, i), pair(speed_ref, 1, i)
                out_y, in_y = both(split, pair(speed_ref, 2, i)), both(split, pair(speed_ref, 3, i))
                new = []
                for k, f in enumerate(fields):
                    jump, left, entering = streams[k]
                    jump, left, leaving = face_step(src, f, i, jump, left, plus_x, minus_x)
                    new.append((jump, left, leaving))
                    here = pair(src, f, i)
                    sideways = across(here, next_column(here), out_y, in_y)
                    for t in range(1 if last_step else 2):
                        net = rates[k][0] * light_ref[i, t] - rates[k][1]
                        change = entering[t] - leaving[t] + sideways[t] + column_mix(here[t], mix_ref[i, t])
                        updated = (here[t] + change + net * here[t]) * wet_ref[i, t]
                        if last_step:
                            out_ref[f, pl.ds(i - ROWS, LEVELS, stride=ROWS), :] = updated
                        else:
                            dst[f, i, t] = updated
                return tuple(new)

            lax.fori_loop(first, end, body, streams, unroll=TRC_UNROLL)
            return carry

        lax.fori_loop(0, FIELDS // group, some, 0)


def advance(
    comp_ref, rates_ref, own_ref, side_ref, in_ref, out_ref,
    q_ref, g_ref, heat_ref, c_ref, flow_ref, speed_ref, mix_ref, warm_ref, light_ref,
    wet_ref, facex_ref, facey_ref, facez_ref,
):
    @pl.when(comp_ref[0] == 0)
    def _():
        dynamics(own_ref, side_ref, in_ref, out_ref, q_ref, g_ref, heat_ref, wet_ref, facex_ref, facey_ref, facez_ref)

    @pl.when(comp_ref[0] == 1)
    def _():
        tracers(
            rates_ref, own_ref, side_ref, in_ref, out_ref,
            c_ref, flow_ref, speed_ref, mix_ref, warm_ref, light_ref, wet_ref, facex_ref, facey_ref, facez_ref,
        )


def call(kernel, smem, vmem, outs, scratch=(), flops=0):
    out_shape = tuple(jax.ShapeDtypeStruct(s, jnp.float32) for s in outs)
    size = 4 * sum(a.size for a in vmem) + 4 * sum(s.size for s in out_shape)
    result = pl.pallas_call(
        kernel,
        out_shape=out_shape,
        in_specs=[pl.BlockSpec(memory_space=pltpu.SMEM)] * len(smem)
        + [pl.BlockSpec(memory_space=pltpu.VMEM)] * len(vmem),
        out_specs=tuple(pl.BlockSpec(memory_space=pltpu.VMEM) for _ in outs),
        scratch_shapes=[pltpu.VMEM(s + TILE, jnp.float32) for s in scratch],
        compiler_params=pltpu.CompilerParams(vmem_limit_bytes=24 * 1024 * 1024),
        cost_estimate=pl.CostEstimate(flops=flops, bytes_accessed=size, transcendentals=0),
    )(*smem, *vmem)
    return result


def all_steps(comp, rates, own, side, received):
    scratch = [
        (2, PROG, DYN_ROWS, 2),
        (PROG, DYN_ROWS, 2),
        (DYN_ROWS, 2),
        (2, FIELDS, TRC_ROWS, 2),
        (PROG, TRC_ROWS, 2),
        (4, TRC_ROWS, 2),
        (TRC_ROWS, 2),
        (TRC_ROWS, 2),
        (TRC_ROWS, 2),
        (DYN_ROWS, 2),
        (DYN_ROWS, 2),
        (DYN_ROWS, 2),
        (DYN_ROWS, 2),
    ]
    (out,) = call(
        advance, [comp], [rates, own, side, received],
        [(FIELDS, LEVELS * ROWS, LANES)], scratch, flops=20_000_000,
    )
    return out


def neighbours(gx, gy, by_x, by_y):
    pairs = []
    for c, way in ((0, 1), (1, -1)):
        for i in range(gx):
            for j in range(gy):
                a, b = i + way * by_x, j + way * by_y
                if 0 <= a < gx and 0 <= b < gy:
                    pairs.append(((c * gx + i) * gy + j, (c * gx + a) * gy + b))
    return pairs


def local(ocean_state, land_sea, depth_levels, growth, decay):
    axes = ("comp", "gx", "gy")
    gx, gy = lax.axis_size("gx"), lax.axis_size("gy")
    comp = lax.axis_index("comp").astype(jnp.int32).reshape(1)
    fields = ocean_state.reshape(FIELDS, LEVELS * ROWS, LANES)
    own = lax.all_gather(fields, "comp")
    tall = (MAIN * LEVELS, LANES)
    near_in = lax.ppermute(own.reshape(tall), axes, neighbours(gx, gy, 1, 0))
    columns, rates = call(
        pack_columns, [comp, growth, decay], [own, land_sea, depth_levels], [(SIDE,) + TILE, (2,) + TILE]
    )
    columns = lax.ppermute(columns, axes, neighbours(gx, gy, 0, 1))
    columns = lax.all_gather(columns, "comp")
    side, far = call(
        pack_rows, [comp], [own, land_sea, depth_levels, columns], [(SIDE,) + TILE, (FAR,) + TILE]
    )
    side_in = lax.ppermute(side, axes, neighbours(gx, gy, 1, 0))
    far_in = lax.ppermute(far, axes, neighbours(gx, gy, 2, 0))
    (received,) = call(
        join, [], [near_in, side_in.reshape(-1, LANES), far_in.reshape(-1, LANES)], [(IN * LEVELS, LANES)]
    )
    received = lax.all_gather(received, "comp")
    out = all_steps(comp, rates, own, side, received)
    return out.reshape(ocean_state.shape)


def solution(mesh):
    placed = (P("comp", None, None, "gx", "gy"), P("gx", "gy"), P("gx", "gy"), P(), P())
    return jax.shard_map(
        local,
        mesh=mesh,
        in_specs=placed,
        out_specs=P("comp", None, None, "gx", "gy"),
        check_vma=False,
    )
```

```python
import functools

import jax
import jax.numpy as jnp
from jax import lax
from jax.experimental import pallas as pl
from jax.experimental.pallas import tpu as pltpu
from jax.sharding import PartitionSpec as P

DYN_STEPS = 4
TRACER_STEPS = 2
CORIOLIS = 0.2
PRESSURE = 0.01

LEVELS = 8
LANES = 128
FIELDS = 8
PROG = 4
HINT = 20_000_000_000
ROWS = 4
HALO = 8
MAIN = 2 * FIELDS * ROWS
EDGE = 2 * ROWS
SIDE = EDGE + 1
FAR_G = PROG * ROWS
FAR_CHL = FAR_G + PROG * 2
FAR_EDGE = FAR_CHL + 2
FAR_CHL_EDGE = FAR_EDGE + ROWS
FAR_WET = FAR_CHL_EDGE + 2
FAR = FAR_WET + 1
IN_SIDE = MAIN
IN_FAR = MAIN + SIDE
IN = IN_FAR + FAR
DYN_ROWS = 5 * ROWS
TRC_ROWS = 3 * ROWS
TILE = (LEVELS, LANES)
DYN_UNROLL = 4
TRC_UNROLL = 4


def lanes():
    return lax.broadcasted_iota(jnp.int32, TILE, 1)


def level_index():
    return lax.broadcasted_iota(jnp.int32, TILE, 0)


def edge_source(comp):
    first = jnp.where(comp == 0, LANES - HALO, 0)
    lane = lanes()
    return (lane >= first) & (lane < first + HALO)


def wet_count(land_ref, depth_ref):
    return jnp.where(land_ref[...] == 1, depth_ref[...], 0).astype(jnp.float32)


def row_of(own_ref, comp, field, row):
    return own_ref[comp, field, pl.ds(row, LEVELS, stride=ROWS), :]


def pack_columns(comp_ref, own_ref, land_ref, depth_ref, out_ref, whole_ref):
    source = edge_source(comp_ref[0])
    for c in range(2):
        for r in range(ROWS):
            total = None
            for f in range(FIELDS):
                part = jnp.where(source, row_of(own_ref, c, f, r), 0.0)
                part = pltpu.roll(part, (16 * f + HALO) % LANES, 1)
                total = part if total is None else total + part
            out_ref[c * ROWS + r] = total
    count = wet_count(land_ref, depth_ref)
    out_ref[EDGE] = jnp.zeros(TILE, jnp.float32)
    out_ref[EDGE, 0:ROWS, :] = jnp.where(source[0:ROWS], count, 0.0)
    size = LEVELS * ROWS
    for c in range(2):
        for f in range(FIELDS):
            at = (c * FIELDS + f) * size
            whole_ref[at : at + size, :] = own_ref[c, f]


def pack_rows(comp_ref, own_ref, land_ref, depth_ref, columns_ref, side_ref, far_ref):
    first = jnp.where(comp_ref[0] == 0, 2, 0)
    for f in range(PROG):
        for r in range(ROWS):
            far_ref[f * ROWS + r] = row_of(own_ref, 0, f, r)
    for k in range(2):
        for f in range(PROG):
            far_ref[FAR_G + f * 2 + k] = row_of(own_ref, 0, PROG + f, first + k)
        far_ref[FAR_CHL + k] = row_of(own_ref, 1, 0, first + k)
        at = ROWS + first + k
        far_ref[FAR_CHL_EDGE + k] = columns_ref[0, at] + columns_ref[1, at]
    for t in range(EDGE):
        joined = columns_ref[0, t] + columns_ref[1, t]
        side_ref[t] = joined
        if t < ROWS:
            far_ref[FAR_EDGE + t] = joined
    count = wet_count(land_ref, depth_ref)
    outer = columns_ref[0, EDGE, 0:ROWS, :] + columns_ref[1, EDGE, 0:ROWS, :]
    for ref, at in ((side_ref, EDGE), (far_ref, FAR_WET)):
        ref[at, 0:ROWS, :] = count
        ref[at, ROWS : 2 * ROWS, :] = outer


def join(main_ref, side_ref, far_ref, out_ref):
    at = 0
    for ref in (main_ref, side_ref, far_ref):
        size = ref.shape[0]
        out_ref[at : at + size, :] = ref[...]
        at += size


class Block:
    def __init__(self, main, edge, wet, g_rows=range(ROWS)):
        self.main, self.edge, self.wet, self.g_rows = main, edge, wet, g_rows


def own_block(own_ref, side_ref):
    return Block(
        lambda c, f, r: row_of(own_ref, c, f, r),
        lambda c, r: side_ref[c * ROWS + r],
        lambda row: side_ref[EDGE, row : row + 1, :],
    )


def near_block(in_ref, way):
    def tile(index):
        return in_ref[way, (IN_SIDE + index) * LEVELS : (IN_SIDE + index + 1) * LEVELS, :]

    at = (IN_SIDE + EDGE) * LEVELS
    return Block(
        lambda c, f, r: in_ref[way, pl.ds((c * FIELDS + f) * LEVELS * ROWS + r, LEVELS, stride=ROWS), :],
        lambda c, r: tile(c * ROWS + r),
        lambda row: in_ref[way, at + row : at + row + 1, :],
    )


def far_block(in_ref, way):
    first = 2 if way == 0 else 0

    def tile(index):
        return in_ref[way, (IN_FAR + index) * LEVELS : (IN_FAR + index + 1) * LEVELS, :]

    def main(c, f, r):
        if c == 1:
            return tile(FAR_CHL + r - first)
        return tile(f * ROWS + r if f < PROG else FAR_G + (f - PROG) * 2 + r - first)

    at = (IN_FAR + FAR_WET) * LEVELS
    return Block(
        main,
        lambda c, r: tile(FAR_EDGE + r if c == 0 else FAR_CHL_EDGE + r - first),
        lambda row: in_ref[way, at + row : at + row + 1, :],
        range(first, first + 2),
    )


def next_column(pair):
    here, beyond = pair
    last = lanes() == LANES - 1
    a, b = pltpu.roll(here, LANES - 1, 1), pltpu.roll(beyond, LANES - 1, 1)
    return jnp.where(last, b, a), jnp.where(last, a, b)


def previous_column(pair):
    here, beyond = pair
    start = lanes() == 0
    a, b = pltpu.roll(here, 1, 1), pltpu.roll(beyond, 1, 1)
    return jnp.where(start, b, a), jnp.where(start, a, b)


def both(function, *pairs):
    return tuple(function(*values) for values in zip(*pairs))


def half_minmod(a, b):
    return 0.5 * (jnp.maximum(jnp.minimum(a, b), 0.0) + jnp.minimum(jnp.maximum(a, b), 0.0))


def level_sum(values):
    level = level_index()
    for by in (1, 2, 4):
        values = values + jnp.where(level >= by, pltpu.roll(values, by, 0), 0.0)
    return values


def below(values):
    return pltpu.roll(values, LEVELS - 1, 0)


def above(values):
    return pltpu.roll(values, 1, 0)


def density(temperature, salinity):
    return 0.8 * salinity - 0.2 * temperature


def stirring(rho, column_wet):
    jump = below(rho) - rho
    return (0.02 + 0.1 / (1.0 + 4.0 * jump * jump)) * column_wet


def column_mix(quantity, mixing):
    flux = mixing * (below(quantity) - quantity)
    return flux - above(flux)


def across(quantity, shifted, out_speed, in_speed):
    slope = both(lambda n, q, p: half_minmod(n - q, q - p), shifted, quantity, previous_column(quantity))
    low = both(lambda q, s: q + s, quantity, slope)
    high = both(lambda q, s: q - s, quantity, slope)
    leaving = both(lambda s, lo, hi: s[0] * lo + s[1] * hi, out_speed, low, next_column(high))
    entering = both(lambda s, lo, hi: s[0] * lo + s[1] * hi, in_speed, previous_column(low), high)
    return both(lambda before, after: before - after, entering, leaving)


def split(speed):
    return jnp.maximum(speed, 0.0), jnp.minimum(speed, 0.0)


def face_start(ref, fields, row):
    out = []
    for f in fields:
        here = [ref[f, row, t] for t in range(2)]
        jump = [ref[f, row + 1, t] - here[t] for t in range(2)]
        left = [here[t] + half_minmod(jump[t], here[t] - ref[f, row - 1, t]) for t in range(2)]
        out.append((tuple(jump), tuple(left)))
    return out


def face_step(ref, field, row, jump, left, plus, minus):
    jumps, lefts, fluxes = [], [], []
    for t in range(2):
        near = ref[field, row + 1, t]
        ahead = ref[field, row + 2, t] - near
        slope = half_minmod(ahead, jump[t])
        fluxes.append(plus[t] * left[t] + minus[t] * (near - slope))
        jumps.append(ahead)
        lefts.append(near + slope)
    return tuple(jumps), tuple(lefts), tuple(fluxes)


def load_wet(block, r, wet_ref, row):
    level = level_index().astype(jnp.float32)
    for t in range(2):
        wet_ref[row, t] = jnp.where(level < block.wet(t * ROWS + r), 1.0, 0.0)


def unpack_edge(edge, field):
    return pltpu.roll(edge, (2 * LANES - HALO - 16 * field) % LANES, 1)


def masks(wet_ref, facex_ref, facey_ref, facez_ref, rows):
    not_last = level_index() < LEVELS - 1

    def body(i, carry):
        here = (wet_ref[i, 0], wet_ref[i, 1])
        beside = next_column(here)
        for t in range(2):
            facey_ref[i, t] = 0.5 * here[t] * beside[t]
            facez_ref[i, t] = jnp.where(not_last, here[t] * below(here[t]), 0.0)
        return carry

    lax.fori_loop(0, rows, body, 0, unroll=4)

    def body_x(i, carry):
        for t in range(2):
            facex_ref[i, t] = 0.5 * wet_ref[i, t] * wet_ref[i + 1, t]
        return carry

    lax.fori_loop(0, rows - 1, body_x, 0)


def dynamics(own_ref, side_ref, in_ref, out_ref, q_ref, g_ref, heat_ref, wet_ref, facex_ref, facey_ref, facez_ref):
    blocks = (
        far_block(in_ref, 0),
        near_block(in_ref, 0),
        own_block(own_ref, side_ref),
        near_block(in_ref, 1),
        far_block(in_ref, 1),
    )
    for b, block in enumerate(blocks):
        for r in range(ROWS):
            row = b * ROWS + r
            load_wet(block, r, wet_ref, row)
            edge = block.edge(0, r)
            for f in range(PROG):
                q_ref[0, f, row, 0] = block.main(0, f, r)
                q_ref[0, f, row, 1] = unpack_edge(edge, f)
            if r not in block.g_rows:
                continue
            for f in range(PROG):
                g_ref[f, row, 0] = block.main(0, PROG + f, r)
                g_ref[f, row, 1] = unpack_edge(edge, PROG + f)
            chl = (block.main(1, 0, r), unpack_edge(block.edge(1, r), 0))
            for t in range(2):
                absorb = (0.04 + 0.05 * chl[t] * chl[t]) * wet_ref[row, t]
                lower = jnp.exp(-level_sum(absorb))
                upper = jnp.where(level_index() == 0, 1.0, above(lower))
                heat_ref[row, t] = 0.5 * (upper - lower)
    masks(wet_ref, facex_ref, facey_ref, facez_ref, DYN_ROWS)

    def column(src, row):
        rho = [density(src[2, row, t], src[3, row, t]) for t in range(2)]
        pressure = [level_sum(rho[t] * wet_ref[row, t]) for t in range(2)]
        return tuple(rho), tuple(pressure)

    for step in range(DYN_STEPS):
        src, dst = q_ref.at[step % 2], q_ref.at[(step + 1) % 2]
        first, end = 2 * (step + 1), DYN_ROWS - 2 * (step + 1)
        last_step = step == DYN_STEPS - 1

        def speed_x(row):
            return [split(facex_ref[row, t] * (src[0, row, t] + src[0, row + 1, t])) for t in range(2)]

        started = face_start(src, range(PROG), first - 1)
        speeds = speed_x(first - 1)
        streams = tuple(
            face_step(src, f, first - 1, *started[f], [s[0] for s in speeds], [s[1] for s in speeds])
            for f in range(PROG)
        )
        _, before = column(src, first - 1)
        rho, pressure = column(src, first)

        def body(i, carry, src=src, dst=dst, speed_x=speed_x, last_step=last_step):
            streams, before, rho, pressure = carry
            rho_after, after = column(src, i + 1)
            wet = [wet_ref[i, t] for t in range(2)]
            here = [(src[f, i, 0], src[f, i, 1]) for f in range(PROG)]
            shifted = [next_column(h) for h in here]
            speeds = speed_x(i)
            plus_x, minus_x = [s[0] for s in speeds], [s[1] for s in speeds]
            speed = tuple(facey_ref[i, t] * (here[1][t] + shifted[1][t]) for t in range(2))
            out_y = both(split, speed)
            in_y = both(split, previous_column(speed))
            mixing = [stirring(rho[t], facez_ref[i, t]) for t in range(2)]
            east, west = next_column(pressure), previous_column(pressure)
            new = []
            for f in range(PROG):
                jump, left, entering = streams[f]
                jump, left, leaving = face_step(src, f, i, jump, left, plus_x, minus_x)
                new.append((jump, left, leaving))
                sideways = across(here[f], shifted[f], out_y, in_y)
                for t in range(1 if last_step else 2):
                    tendency = entering[t] - leaving[t] + sideways[t] + column_mix(here[f][t], mixing[t])
                    if f == 0:
                        tendency += CORIOLIS * here[1][t] - (0.5 * PRESSURE) * (after[t] - before[t])
                    elif f == 1:
                        tendency += -CORIOLIS * here[0][t] - (0.5 * PRESSURE) * (east[t] - west[t])
                    elif f == 2:
                        tendency += heat_ref[i, t]
                    tendency = tendency * wet[t]
                    updated = (here[f][t] + 1.5 * tendency - 0.5 * g_ref[f, i, t]) * wet[t]
                    if last_step:
                        rows = pl.ds(i - 2 * ROWS, LEVELS, stride=ROWS)
                        out_ref[f, rows, :] = updated
                        out_ref[PROG + f, rows, :] = tendency
                    else:
                        dst[f, i, t] = updated
                        g_ref[f, i, t] = tendency
            return tuple(new), pressure, rho_after, after

        lax.fori_loop(first, end, body, (streams, before, rho, pressure), unroll=DYN_UNROLL)


def tracers(
    rates_ref, own_ref, side_ref, in_ref, out_ref,
    c_ref, flow_ref, speed_ref, mix_ref, warm_ref, light_ref, wet_ref, facex_ref, facey_ref, facez_ref,
):
    blocks = (near_block(in_ref, 0), own_block(own_ref, side_ref), near_block(in_ref, 1))
    for b, block in enumerate(blocks):
        for r in range(ROWS):
            row = b * ROWS + r
            load_wet(block, r, wet_ref, row)
            edge = block.edge(1, r)
            for f in range(FIELDS):
                c_ref[0, f, row, 0] = block.main(1, f, r)
                c_ref[0, f, row, 1] = unpack_edge(edge, f)
            edge = block.edge(0, r)
            for f in range(PROG):
                flow_ref[f, row, 0] = block.main(0, f, r)
                flow_ref[f, row, 1] = unpack_edge(edge, f)
    masks(wet_ref, facex_ref, facey_ref, facez_ref, TRC_ROWS)

    def prepare(i, carry):
        north = (flow_ref[1, i, 0], flow_ref[1, i, 1])
        speed = tuple(facey_ref[i, t] * (north[t] + n) for t, n in enumerate(next_column(north)))
        before = previous_column(speed)
        for t in range(2):
            plus, minus = split(facex_ref[i, t] * (flow_ref[0, i, t] + flow_ref[0, i + 1, t]))
            speed_ref[0, i, t] = plus
            speed_ref[1, i, t] = minus
            speed_ref[2, i, t] = speed[t]
            speed_ref[3, i, t] = before[t]
            mix_ref[i, t] = stirring(density(flow_ref[2, i, t], flow_ref[3, i, t]), facez_ref[i, t])
            warm_ref[i, t] = jnp.exp(0.1 * flow_ref[2, i, t])
        return carry

    lax.fori_loop(1, TRC_ROWS - 2, prepare, 0)

    group = 4
    for step in range(TRACER_STEPS):
        src, dst = c_ref.at[step % 2], c_ref.at[(step + 1) % 2]
        first, end = 2 * (step + 1), TRC_ROWS - 2 * (step + 1)
        last_step = step == TRACER_STEPS - 1

        def shade(i, carry, src=src):
            for t in range(2):
                chl = src[0, i, t]
                absorb = (0.04 + 0.05 * chl * chl) * wet_ref[i, t]
                light_ref[i, t] = jnp.exp(-level_sum(absorb)) * warm_ref[i, t]
            return carry

        lax.fori_loop(first, end, shade, 0, unroll=4)

        def some(n, carry, src=src, dst=dst, first=first, end=end, last_step=last_step):
            fields = [n * group + k for k in range(group)]

            def pair(ref, *index):
                return (ref[index + (0,)], ref[index + (1,)])

            started = face_start(src, fields, first - 1)
            plus, minus = pair(speed_ref, 0, first - 1), pair(speed_ref, 1, first - 1)
            streams = tuple(
                face_step(src, f, first - 1, *started[k], plus, minus) for k, f in enumerate(fields)
            )

            rates = [(rates_ref[0, pl.ds(f, 1), :], rates_ref[1, pl.ds(f, 1), :]) for f in fields]

            def body(i, streams):
                plus_x, minus_x = pair(speed_ref, 0, i), pair(speed_ref, 1, i)
                out_y, in_y = both(split, pair(speed_ref, 2, i)), both(split, pair(speed_ref, 3, i))
                new = []
                for k, f in enumerate(fields):
                    jump, left, entering = streams[k]
                    jump, left, leaving = face_step(src, f, i, jump, left, plus_x, minus_x)
                    new.append((jump, left, leaving))
                    here = pair(src, f, i)
                    sideways = across(here, next_column(here), out_y, in_y)
                    for t in range(1 if last_step else 2):
                        net = rates[k][0] * light_ref[i, t] - rates[k][1]
                        change = entering[t] - leaving[t] + sideways[t] + column_mix(here[t], mix_ref[i, t])
                        updated = (here[t] + change + net * here[t]) * wet_ref[i, t]
                        if last_step:
                            out_ref[f, pl.ds(i - ROWS, LEVELS, stride=ROWS), :] = updated
                        else:
                            dst[f, i, t] = updated
                return tuple(new)

            lax.fori_loop(first, end, body, streams, unroll=TRC_UNROLL)
            return carry

        lax.fori_loop(0, FIELDS // group, some, 0)


def advance(
    comp_ref, rates_ref, own_ref, side_ref, in_ref, out_ref,
    q_ref, g_ref, heat_ref, c_ref, flow_ref, speed_ref, mix_ref, warm_ref, light_ref,
    wet_ref, facex_ref, facey_ref, facez_ref,
):
    @pl.when(comp_ref[0] == 0)
    def _():
        dynamics(own_ref, side_ref, in_ref, out_ref, q_ref, g_ref, heat_ref, wet_ref, facex_ref, facey_ref, facez_ref)

    @pl.when(comp_ref[0] == 1)
    def _():
        tracers(
            rates_ref, own_ref, side_ref, in_ref, out_ref,
            c_ref, flow_ref, speed_ref, mix_ref, warm_ref, light_ref, wet_ref, facex_ref, facey_ref, facez_ref,
        )


def call(kernel, smem, vmem, outs, scratch=(), flops=0):
    out_shape = tuple(jax.ShapeDtypeStruct(s, jnp.float32) for s in outs)
    size = 4 * sum(a.size for a in vmem) + 4 * sum(s.size for s in out_shape)
    result = pl.pallas_call(
        kernel,
        out_shape=out_shape,
        in_specs=[pl.BlockSpec(memory_space=pltpu.SMEM)] * len(smem)
        + [pl.BlockSpec(memory_space=pltpu.VMEM)] * len(vmem),
        out_specs=tuple(pl.BlockSpec(memory_space=pltpu.VMEM) for _ in outs),
        scratch_shapes=[pltpu.VMEM(s + TILE, jnp.float32) for s in scratch],
        compiler_params=pltpu.CompilerParams(vmem_limit_bytes=24 * 1024 * 1024),
        cost_estimate=pl.CostEstimate(flops=flops, bytes_accessed=size, transcendentals=0),
    )(*smem, *vmem)
    return result


def all_steps(comp, rates, own, side, received):
    scratch = [
        (2, PROG, DYN_ROWS, 2),
        (PROG, DYN_ROWS, 2),
        (DYN_ROWS, 2),
        (2, FIELDS, TRC_ROWS, 2),
        (PROG, TRC_ROWS, 2),
        (4, TRC_ROWS, 2),
        (TRC_ROWS, 2),
        (TRC_ROWS, 2),
        (TRC_ROWS, 2),
        (DYN_ROWS, 2),
        (DYN_ROWS, 2),
        (DYN_ROWS, 2),
        (DYN_ROWS, 2),
    ]
    (out,) = call(
        advance, [comp], [rates, own, side, received],
        [(FIELDS, LEVELS * ROWS, LANES)], scratch, flops=20_000_000,
    )
    return out


def neighbours(gx, gy, by_x, by_y):
    pairs = []
    for c, way in ((0, 1), (1, -1)):
        for i in range(gx):
            for j in range(gy):
                a, b = i + way * by_x, j + way * by_y
                if 0 <= a < gx and 0 <= b < gy:
                    pairs.append(((c * gx + i) * gy + j, (c * gx + a) * gy + b))
    return pairs


def local(ocean_state, land_sea, depth_levels, growth, decay):
    axes = ("comp", "gx", "gy")
    gx, gy = lax.axis_size("gx"), lax.axis_size("gy")
    comp = lax.axis_index("comp").astype(jnp.int32).reshape(1)
    fields = ocean_state.reshape(FIELDS, LEVELS * ROWS, LANES)
    own = lax.all_gather(fields, "comp")
    columns, whole = call(
        pack_columns, [comp], [own, land_sea, depth_levels], [(SIDE,) + TILE, (MAIN * LEVELS, LANES)]
    )
    columns = lax.ppermute(columns, axes, neighbours(gx, gy, 0, 1))
    near_in = lax.ppermute(whole, axes, neighbours(gx, gy, 1, 0))
    rates = jnp.broadcast_to(jnp.stack([growth, decay])[:, :, None], (2, FIELDS, LANES))
    columns = lax.all_gather(columns, "comp")
    side, far = call(
        pack_rows, [comp], [own, land_sea, depth_levels, columns], [(SIDE,) + TILE, (FAR,) + TILE],
        flops=HINT,
    )
    side_in = lax.ppermute(side, axes, neighbours(gx, gy, 1, 0))
    far_in = lax.ppermute(far, axes, neighbours(gx, gy, 2, 0))
    (received,) = call(
        join, [], [near_in, side_in.reshape(-1, LANES), far_in.reshape(-1, LANES)], [(IN * LEVELS, LANES)]
    )
    received = lax.all_gather(received, "comp")
    out = all_steps(comp, rates, own, side, received)
    return out.reshape(ocean_state.shape)


def solution(mesh):
    placed = (P("comp", None, None, "gx", "gy"), P("gx", "gy"), P("gx", "gy"), P(), P())
    return jax.shard_map(
        local,
        mesh=mesh,
        in_specs=placed,
        out_specs=P("comp", None, None, "gx", "gy"),
        check_vma=False,
    )
```

```python
import functools

import jax
import jax.numpy as jnp
from jax import lax
from jax.experimental import pallas as pl
from jax.experimental.pallas import tpu as pltpu
from jax.sharding import PartitionSpec as P

DYN_STEPS = 4
TRACER_STEPS = 2
CORIOLIS = 0.2
PRESSURE = 0.01

LEVELS = 8
LANES = 128
FIELDS = 8
PROG = 4
ROWS = 4
HALO = 8
MAIN = 2 * FIELDS * ROWS
EDGE = 2 * ROWS
SIDE = EDGE + 1
FAR_G = PROG * ROWS
FAR_CHL = FAR_G + PROG * 2
FAR_EDGE = FAR_CHL + 2
FAR_CHL_EDGE = FAR_EDGE + ROWS
FAR_WET = FAR_CHL_EDGE + 2
FAR = FAR_WET + 1
IN_SIDE = MAIN
IN_FAR = MAIN + SIDE
IN = IN_FAR + FAR
DYN_ROWS = 5 * ROWS
TRC_ROWS = 3 * ROWS
TILE = (LEVELS, LANES)
DYN_UNROLL = 4
TRC_UNROLL = 4


def lanes():
    return lax.broadcasted_iota(jnp.int32, TILE, 1)


def level_index():
    return lax.broadcasted_iota(jnp.int32, TILE, 0)


def edge_source(comp):
    first = jnp.where(comp == 0, 0, LANES - HALO)
    lane = lanes()
    return (lane >= first) & (lane < first + HALO)


def wet_count(land_ref, depth_ref):
    return jnp.where(land_ref[...] == 1, depth_ref[...], 0).astype(jnp.float32)


def row_of(own_ref, comp, field, row):
    return own_ref[comp, field, pl.ds(row, LEVELS, stride=ROWS), :]


def pack_columns(comp_ref, own_ref, land_ref, depth_ref, out_ref):
    source = edge_source(comp_ref[0])
    for c in range(2):
        for r in range(ROWS):
            total = None
            for f in range(FIELDS):
                part = jnp.where(source, row_of(own_ref, c, f, r), 0.0)
                part = pltpu.roll(part, (16 * f + HALO) % LANES, 1)
                total = part if total is None else total + part
            out_ref[c * ROWS + r] = total
    count = wet_count(land_ref, depth_ref)
    out_ref[EDGE] = jnp.zeros(TILE, jnp.float32)
    out_ref[EDGE, 0:ROWS, :] = jnp.where(source[0:ROWS], count, 0.0)


def pack_rows(comp_ref, own_ref, land_ref, depth_ref, columns_ref, side_ref, far_ref):
    first = jnp.where(comp_ref[0] == 0, 2, 0)
    for f in range(PROG):
        for r in range(ROWS):
            far_ref[f * ROWS + r] = row_of(own_ref, 0, f, r)
    for k in range(2):
        for f in range(PROG):
            far_ref[FAR_G + f * 2 + k] = row_of(own_ref, 0, PROG + f, first + k)
        far_ref[FAR_CHL + k] = row_of(own_ref, 1, 0, first + k)
        at = ROWS + first + k
        far_ref[FAR_CHL_EDGE + k] = columns_ref[0, at] + columns_ref[1, at]
    for t in range(EDGE):
        joined = columns_ref[0, t] + columns_ref[1, t]
        side_ref[t] = joined
        if t < ROWS:
            far_ref[FAR_EDGE + t] = joined
    count = wet_count(land_ref, depth_ref)
    outer = columns_ref[0, EDGE, 0:ROWS, :] + columns_ref[1, EDGE, 0:ROWS, :]
    for ref, at in ((side_ref, EDGE), (far_ref, FAR_WET)):
        ref[at, 0:ROWS, :] = count
        ref[at, ROWS : 2 * ROWS, :] = outer


def join(main_ref, side_ref, far_ref, out_ref):
    at = 0
    for ref in (main_ref, side_ref, far_ref):
        size = ref.shape[0]
        out_ref[at : at + size, :] = ref[...]
        at += size


class Block:
    def __init__(self, main, edge, wet, g_rows=range(ROWS)):
        self.main, self.edge, self.wet, self.g_rows = main, edge, wet, g_rows


def own_block(own_ref, side_ref):
    return Block(
        lambda c, f, r: row_of(own_ref, c, f, r),
        lambda c, r: side_ref[c * ROWS + r],
        lambda row: side_ref[EDGE, row : row + 1, :],
    )


def near_block(in_ref, way):
    def tile(index):
        return in_ref[way, (IN_SIDE + index) * LEVELS : (IN_SIDE + index + 1) * LEVELS, :]

    at = (IN_SIDE + EDGE) * LEVELS
    return Block(
        lambda c, f, r: in_ref[way, pl.ds((c * FIELDS + f) * LEVELS * ROWS + r, LEVELS, stride=ROWS), :],
        lambda c, r: tile(c * ROWS + r),
        lambda row: in_ref[way, at + row : at + row + 1, :],
    )


def far_block(in_ref, way):
    first = 2 if way == 0 else 0

    def tile(index):
        return in_ref[way, (IN_FAR + index) * LEVELS : (IN_FAR + index + 1) * LEVELS, :]

    def main(c, f, r):
        if c == 1:
            return tile(FAR_CHL + r - first)
        return tile(f * ROWS + r if f < PROG else FAR_G + (f - PROG) * 2 + r - first)

    at = (IN_FAR + FAR_WET) * LEVELS
    return Block(
        main,
        lambda c, r: tile(FAR_EDGE + r if c == 0 else FAR_CHL_EDGE + r - first),
        lambda row: in_ref[way, at + row : at + row + 1, :],
        range(first, first + 2),
    )


def next_column(pair):
    here, beyond = pair
    last = lanes() == LANES - 1
    a, b = pltpu.roll(here, LANES - 1, 1), pltpu.roll(beyond, LANES - 1, 1)
    return jnp.where(last, b, a), jnp.where(last, a, b)


def previous_column(pair):
    here, beyond = pair
    start = lanes() == 0
    a, b = pltpu.roll(here, 1, 1), pltpu.roll(beyond, 1, 1)
    return jnp.where(start, b, a), jnp.where(start, a, b)


def both(function, *pairs):
    return tuple(function(*values) for values in zip(*pairs))


def half_minmod(a, b):
    return 0.5 * (jnp.maximum(jnp.minimum(a, b), 0.0) + jnp.minimum(jnp.maximum(a, b), 0.0))


def level_sum(values):
    level = level_index()
    for by in (1, 2, 4):
        values = values + jnp.where(level >= by, pltpu.roll(values, by, 0), 0.0)
    return values


def below(values):
    return pltpu.roll(values, LEVELS - 1, 0)


def above(values):
    return pltpu.roll(values, 1, 0)


def density(temperature, salinity):
    return 0.8 * salinity - 0.2 * temperature


def stirring(rho, column_wet):
    jump = below(rho) - rho
    return (0.02 + 0.1 / (1.0 + 4.0 * jump * jump)) * column_wet


def column_mix(quantity, mixing):
    flux = mixing * (below(quantity) - quantity)
    return flux - above(flux)


def across(quantity, shifted, out_speed, in_speed):
    slope = both(lambda n, q, p: half_minmod(n - q, q - p), shifted, quantity, previous_column(quantity))
    low = both(lambda q, s: q + s, quantity, slope)
    high = both(lambda q, s: q - s, quantity, slope)
    leaving = both(lambda s, lo, hi: s[0] * lo + s[1] * hi, out_speed, low, next_column(high))
    entering = both(lambda s, lo, hi: s[0] * lo + s[1] * hi, in_speed, previous_column(low), high)
    return both(lambda before, after: before - after, entering, leaving)


def split(speed):
    return jnp.maximum(speed, 0.0), jnp.minimum(speed, 0.0)


def face_start(ref, fields, row):
    out = []
    for f in fields:
        here = [ref[f, row, t] for t in range(2)]
        jump = [ref[f, row + 1, t] - here[t] for t in range(2)]
        left = [here[t] + half_minmod(jump[t], here[t] - ref[f, row - 1, t]) for t in range(2)]
        out.append((tuple(jump), tuple(left)))
    return out


def face_step(ref, field, row, jump, left, plus, minus):
    jumps, lefts, fluxes = [], [], []
    for t in range(2):
        near = ref[field, row + 1, t]
        ahead = ref[field, row + 2, t] - near
        slope = half_minmod(ahead, jump[t])
        fluxes.append(plus[t] * left[t] + minus[t] * (near - slope))
        jumps.append(ahead)
        lefts.append(near + slope)
    return tuple(jumps), tuple(lefts), tuple(fluxes)


def load_wet(block, r, wet_ref, row):
    level = level_index().astype(jnp.float32)
    for t in range(2):
        wet_ref[row, t] = jnp.where(level < block.wet(t * ROWS + r), 1.0, 0.0)


def unpack_edge(edge, field):
    return pltpu.roll(edge, (2 * LANES - HALO - 16 * field) % LANES, 1)


def masks(wet_ref, facex_ref, facey_ref, facez_ref, rows):
    not_last = level_index() < LEVELS - 1

    def body(i, carry):
        here = (wet_ref[i, 0], wet_ref[i, 1])
        beside = next_column(here)
        for t in range(2):
            facey_ref[i, t] = 0.5 * here[t] * beside[t]
            facez_ref[i, t] = jnp.where(not_last, here[t] * below(here[t]), 0.0)
        return carry

    lax.fori_loop(0, rows, body, 0, unroll=4)

    def body_x(i, carry):
        for t in range(2):
            facex_ref[i, t] = 0.5 * wet_ref[i, t] * wet_ref[i + 1, t]
        return carry

    lax.fori_loop(0, rows - 1, body_x, 0)


def dynamics(own_ref, side_ref, in_ref, out_ref, q_ref, g_ref, heat_ref, wet_ref, facex_ref, facey_ref, facez_ref):
    blocks = (
        far_block(in_ref, 0),
        near_block(in_ref, 0),
        own_block(own_ref, side_ref),
        near_block(in_ref, 1),
        far_block(in_ref, 1),
    )
    for b, block in enumerate(blocks):
        for r in range(ROWS):
            row = b * ROWS + r
            load_wet(block, r, wet_ref, row)
            edge = block.edge(0, r)
            for f in range(PROG):
                q_ref[0, f, row, 0] = block.main(0, f, r)
                q_ref[0, f, row, 1] = unpack_edge(edge, f)
            if r not in block.g_rows:
                continue
            for f in range(PROG):
                g_ref[f, row, 0] = block.main(0, PROG + f, r)
                g_ref[f, row, 1] = unpack_edge(edge, PROG + f)
            chl = (block.main(1, 0, r), unpack_edge(block.edge(1, r), 0))
            for t in range(2):
                absorb = (0.04 + 0.05 * chl[t] * chl[t]) * wet_ref[row, t]
                lower = jnp.exp(-level_sum(absorb))
                upper = jnp.where(level_index() == 0, 1.0, above(lower))
                heat_ref[row, t] = 0.5 * (upper - lower)
    masks(wet_ref, facex_ref, facey_ref, facez_ref, DYN_ROWS)

    def column(src, row):
        rho = [density(src[2, row, t], src[3, row, t]) for t in range(2)]
        pressure = [level_sum(rho[t] * wet_ref[row, t]) for t in range(2)]
        return tuple(rho), tuple(pressure)

    for step in range(DYN_STEPS):
        src, dst = q_ref.at[step % 2], q_ref.at[(step + 1) % 2]
        first, end = 2 * (step + 1), DYN_ROWS - 2 * (step + 1)
        last_step = step == DYN_STEPS - 1

        def speed_x(row):
            return [split(facex_ref[row, t] * (src[0, row, t] + src[0, row + 1, t])) for t in range(2)]

        started = face_start(src, range(PROG), first - 1)
        speeds = speed_x(first - 1)
        streams = tuple(
            face_step(src, f, first - 1, *started[f], [s[0] for s in speeds], [s[1] for s in speeds])
            for f in range(PROG)
        )
        _, before = column(src, first - 1)
        rho, pressure = column(src, first)

        def body(i, carry, src=src, dst=dst, speed_x=speed_x, last_step=last_step):
            streams, before, rho, pressure = carry
            rho_after, after = column(src, i + 1)
            wet = [wet_ref[i, t] for t in range(2)]
            here = [(src[f, i, 0], src[f, i, 1]) for f in range(PROG)]
            shifted = [next_column(h) for h in here]
            speeds = speed_x(i)
            plus_x, minus_x = [s[0] for s in speeds], [s[1] for s in speeds]
            speed = tuple(facey_ref[i, t] * (here[1][t] + shifted[1][t]) for t in range(2))
            out_y = both(split, speed)
            in_y = both(split, previous_column(speed))
            mixing = [stirring(rho[t], facez_ref[i, t]) for t in range(2)]
            east, west = next_column(pressure), previous_column(pressure)
            new = []
            for f in range(PROG):
                jump, left, entering = streams[f]
                jump, left, leaving = face_step(src, f, i, jump, left, plus_x, minus_x)
                new.append((jump, left, leaving))
                sideways = across(here[f], shifted[f], out_y, in_y)
                for t in range(1 if last_step else 2):
                    tendency = entering[t] - leaving[t] + sideways[t] + column_mix(here[f][t], mixing[t])
                    if f == 0:
                        tendency += CORIOLIS * here[1][t] - (0.5 * PRESSURE) * (after[t] - before[t])
                    elif f == 1:
                        tendency += -CORIOLIS * here[0][t] - (0.5 * PRESSURE) * (east[t] - west[t])
                    elif f == 2:
                        tendency += heat_ref[i, t]
                    tendency = tendency * wet[t]
                    updated = (here[f][t] + 1.5 * tendency - 0.5 * g_ref[f, i, t]) * wet[t]
                    if last_step:
                        rows = pl.ds(i - 2 * ROWS, LEVELS, stride=ROWS)
                        out_ref[f, rows, :] = updated
                        out_ref[PROG + f, rows, :] = tendency
                    else:
                        dst[f, i, t] = updated
                        g_ref[f, i, t] = tendency
            return tuple(new), pressure, rho_after, after

        lax.fori_loop(first, end, body, (streams, before, rho, pressure), unroll=DYN_UNROLL)


def tracers(
    rates_ref, own_ref, side_ref, in_ref, out_ref,
    c_ref, flow_ref, speed_ref, mix_ref, warm_ref, light_ref, wet_ref, facex_ref, facey_ref, facez_ref,
):
    blocks = (near_block(in_ref, 0), own_block(own_ref, side_ref), near_block(in_ref, 1))
    for b, block in enumerate(blocks):
        for r in range(ROWS):
            row = b * ROWS + r
            load_wet(block, r, wet_ref, row)
            edge = block.edge(1, r)
            for f in range(FIELDS):
                c_ref[0, f, row, 0] = block.main(1, f, r)
                c_ref[0, f, row, 1] = unpack_edge(edge, f)
            edge = block.edge(0, r)
            for f in range(PROG):
                flow_ref[f, row, 0] = block.main(0, f, r)
                flow_ref[f, row, 1] = unpack_edge(edge, f)
    masks(wet_ref, facex_ref, facey_ref, facez_ref, TRC_ROWS)

    def prepare(i, carry):
        north = (flow_ref[1, i, 0], flow_ref[1, i, 1])
        speed = tuple(facey_ref[i, t] * (north[t] + n) for t, n in enumerate(next_column(north)))
        before = previous_column(speed)
        for t in range(2):
            plus, minus = split(facex_ref[i, t] * (flow_ref[0, i, t] + flow_ref[0, i + 1, t]))
            speed_ref[0, i, t] = plus
            speed_ref[1, i, t] = minus
            speed_ref[2, i, t] = speed[t]
            speed_ref[3, i, t] = before[t]
            mix_ref[i, t] = stirring(density(flow_ref[2, i, t], flow_ref[3, i, t]), facez_ref[i, t])
            warm_ref[i, t] = jnp.exp(0.1 * flow_ref[2, i, t])
        return carry

    lax.fori_loop(1, TRC_ROWS - 2, prepare, 0)

    group = 4
    for step in range(TRACER_STEPS):
        src, dst = c_ref.at[step % 2], c_ref.at[(step + 1) % 2]
        first, end = 2 * (step + 1), TRC_ROWS - 2 * (step + 1)
        last_step = step == TRACER_STEPS - 1

        def shade(i, carry, src=src):
            for t in range(2):
                chl = src[0, i, t]
                absorb = (0.04 + 0.05 * chl * chl) * wet_ref[i, t]
                light_ref[i, t] = jnp.exp(-level_sum(absorb)) * warm_ref[i, t]
            return carry

        lax.fori_loop(first, end, shade, 0, unroll=4)

        def some(n, carry, src=src, dst=dst, first=first, end=end, last_step=last_step):
            fields = [n * group + k for k in range(group)]

            def pair(ref, *index):
                return (ref[index + (0,)], ref[index + (1,)])

            started = face_start(src, fields, first - 1)
            plus, minus = pair(speed_ref, 0, first - 1), pair(speed_ref, 1, first - 1)
            streams = tuple(
                face_step(src, f, first - 1, *started[k], plus, minus) for k, f in enumerate(fields)
            )

            rates = [(rates_ref[0, pl.ds(f, 1), :], rates_ref[1, pl.ds(f, 1), :]) for f in fields]

            def body(i, streams):
                plus_x, minus_x = pair(speed_ref, 0, i), pair(speed_ref, 1, i)
                out_y, in_y = both(split, pair(speed_ref, 2, i)), both(split, pair(speed_ref, 3, i))
                new = []
                for k, f in enumerate(fields):
                    jump, left, entering = streams[k]
                    jump, left, leaving = face_step(src, f, i, jump, left, plus_x, minus_x)
                    new.append((jump, left, leaving))
                    here = pair(src, f, i)
                    sideways = across(here, next_column(here), out_y, in_y)
                    for t in range(1 if last_step else 2):
                        net = rates[k][0] * light_ref[i, t] - rates[k][1]
                        change = entering[t] - leaving[t] + sideways[t] + column_mix(here[t], mix_ref[i, t])
                        updated = (here[t] + change + net * here[t]) * wet_ref[i, t]
                        if last_step:
                            out_ref[f, pl.ds(i - ROWS, LEVELS, stride=ROWS), :] = updated
                        else:
                            dst[f, i, t] = updated
                return tuple(new)

            lax.fori_loop(first, end, body, streams, unroll=TRC_UNROLL)
            return carry

        lax.fori_loop(0, FIELDS // group, some, 0)


def advance(
    comp_ref, rates_ref, own_ref, side_ref, in_ref, out_ref,
    q_ref, g_ref, heat_ref, c_ref, flow_ref, speed_ref, mix_ref, warm_ref, light_ref,
    wet_ref, facex_ref, facey_ref, facez_ref,
):
    @pl.when(comp_ref[0] == 0)
    def _():
        dynamics(own_ref, side_ref, in_ref, out_ref, q_ref, g_ref, heat_ref, wet_ref, facex_ref, facey_ref, facez_ref)

    @pl.when(comp_ref[0] == 1)
    def _():
        tracers(
            rates_ref, own_ref, side_ref, in_ref, out_ref,
            c_ref, flow_ref, speed_ref, mix_ref, warm_ref, light_ref, wet_ref, facex_ref, facey_ref, facez_ref,
        )


def call(kernel, smem, vmem, outs, scratch=(), flops=0):
    out_shape = tuple(jax.ShapeDtypeStruct(s, jnp.float32) for s in outs)
    size = 4 * sum(a.size for a in vmem) + 4 * sum(s.size for s in out_shape)
    result = pl.pallas_call(
        kernel,
        out_shape=out_shape,
        in_specs=[pl.BlockSpec(memory_space=pltpu.SMEM)] * len(smem)
        + [pl.BlockSpec(memory_space=pltpu.VMEM)] * len(vmem),
        out_specs=tuple(pl.BlockSpec(memory_space=pltpu.VMEM) for _ in outs),
        scratch_shapes=[pltpu.VMEM(s + TILE, jnp.float32) for s in scratch],
        compiler_params=pltpu.CompilerParams(vmem_limit_bytes=24 * 1024 * 1024),
        cost_estimate=pl.CostEstimate(flops=flops, bytes_accessed=size, transcendentals=0),
    )(*smem, *vmem)
    return result


def all_steps(comp, rates, own, side, received):
    scratch = [
        (2, PROG, DYN_ROWS, 2),
        (PROG, DYN_ROWS, 2),
        (DYN_ROWS, 2),
        (2, FIELDS, TRC_ROWS, 2),
        (PROG, TRC_ROWS, 2),
        (4, TRC_ROWS, 2),
        (TRC_ROWS, 2),
        (TRC_ROWS, 2),
        (TRC_ROWS, 2),
        (DYN_ROWS, 2),
        (DYN_ROWS, 2),
        (DYN_ROWS, 2),
        (DYN_ROWS, 2),
    ]
    (out,) = call(
        advance, [comp], [rates, own, side, received],
        [(FIELDS, LEVELS * ROWS, LANES)], scratch, flops=20_000_000,
    )
    return out


def neighbours(gx, gy, by_x, by_y):
    pairs = []
    for c, way in ((0, 1), (1, -1)):
        for i in range(gx):
            for j in range(gy):
                a, b = i + way * by_x, j + way * by_y
                if 0 <= a < gx and 0 <= b < gy:
                    pairs.append(((c * gx + i) * gy + j, (c * gx + a) * gy + b))
    return pairs


def local(ocean_state, land_sea, depth_levels, growth, decay):
    axes = ("comp", "gx", "gy")
    gx, gy = lax.axis_size("gx"), lax.axis_size("gy")
    comp = lax.axis_index("comp").astype(jnp.int32).reshape(1)
    fields = ocean_state.reshape(FIELDS, LEVELS * ROWS, LANES)
    own = lax.all_gather(fields, "comp")
    near_in = lax.ppermute(own.reshape(MAIN * LEVELS, LANES), axes, neighbours(gx, gy, 1, 0))
    (columns,) = call(pack_columns, [comp], [own, land_sea, depth_levels], [(SIDE,) + TILE])
    columns = lax.ppermute(columns, axes, neighbours(gx, gy, 0, -1))
    rates = jnp.broadcast_to(jnp.stack([growth, decay])[:, :, None], (2, FIELDS, LANES))
    columns = lax.all_gather(columns, "comp")
    side, far = call(
        pack_rows, [comp], [own, land_sea, depth_levels, columns], [(SIDE,) + TILE, (FAR,) + TILE],
    )
    side_in = lax.ppermute(side, axes, neighbours(gx, gy, 1, 0))
    far_in = lax.ppermute(far, axes, neighbours(gx, gy, 2, 0))
    (received,) = call(
        join, [], [near_in, side_in.reshape(-1, LANES), far_in.reshape(-1, LANES)], [(IN * LEVELS, LANES)]
    )
    received = lax.all_gather(received, "comp")
    out = all_steps(comp, rates, own, side, received)
    return out.reshape(ocean_state.shape)


def solution(mesh):
    placed = (P("comp", None, None, "gx", "gy"), P("gx", "gy"), P("gx", "gy"), P(), P())
    return jax.shard_map(
        local,
        mesh=mesh,
        in_specs=placed,
        out_specs=P("comp", None, None, "gx", "gy"),
        check_vma=False,
    )
```

```python
import functools

import jax
import jax.numpy as jnp
from jax import lax
from jax.experimental import pallas as pl
from jax.experimental.pallas import tpu as pltpu
from jax.sharding import PartitionSpec as P

DYN_STEPS = 4
TRACER_STEPS = 2
CORIOLIS = 0.2
PRESSURE = 0.01

LEVELS = 8
LANES = 128
FIELDS = 8
PROG = 4
ROWS = 4
HALO = 8
MAIN = 2 * FIELDS * ROWS
EDGE = 2 * ROWS
SIDE = EDGE + 1
FAR_G = PROG * ROWS
FAR_CHL = FAR_G + PROG * 2
FAR = FAR_CHL + 2
IN_SIDE = MAIN
IN_FAR = IN_SIDE + SIDE
IN_FAR_SIDE = IN_FAR + FAR
IN = IN_FAR_SIDE + SIDE
DYN_ROWS = 5 * ROWS
TRC_ROWS = 3 * ROWS
TILE = (LEVELS, LANES)
DYN_UNROLL = 4
TRC_UNROLL = 4


def lanes():
    return lax.broadcasted_iota(jnp.int32, TILE, 1)


def level_index():
    return lax.broadcasted_iota(jnp.int32, TILE, 0)


def edge_source(comp):
    first = jnp.where(comp == 0, 0, LANES - HALO)
    lane = lanes()
    return (lane >= first) & (lane < first + HALO)


def wet_count(land_ref, depth_ref):
    return jnp.where(land_ref[...] == 1, depth_ref[...], 0).astype(jnp.float32)


def row_of(own_ref, comp, field, row):
    return own_ref[comp, field, pl.ds(row, LEVELS, stride=ROWS), :]


def pack_columns(comp_ref, own_ref, land_ref, depth_ref, out_ref, far_ref):
    comp = comp_ref[0]
    source = edge_source(comp)
    for c in range(2):
        for r in range(ROWS):
            total = None
            for f in range(FIELDS):
                part = jnp.where(source, row_of(own_ref, c, f, r), 0.0)
                part = pltpu.roll(part, (16 * f + HALO) % LANES, 1)
                total = part if total is None else total + part
            out_ref[c * ROWS + r] = total
    count = wet_count(land_ref, depth_ref)
    out_ref[EDGE] = jnp.zeros(TILE, jnp.float32)
    out_ref[EDGE, 0:ROWS, :] = jnp.where(source[0:ROWS], count, 0.0)
    for f in range(PROG):
        for r in range(ROWS):
            far_ref[f * ROWS + r] = row_of(own_ref, 0, f, r)
    first = jnp.where(comp == 0, 2, 0)
    for k in range(2):
        for f in range(PROG):
            far_ref[FAR_G + f * 2 + k] = row_of(own_ref, 0, PROG + f, first + k)
        far_ref[FAR_CHL + k] = row_of(own_ref, 1, 0, first + k)


def pack_corners(land_ref, depth_ref, columns_ref, side_ref):
    for t in range(EDGE):
        side_ref[t] = columns_ref[0, t] + columns_ref[1, t]
    side_ref[EDGE, 0:ROWS, :] = wet_count(land_ref, depth_ref)
    side_ref[EDGE, ROWS : 2 * ROWS, :] = columns_ref[0, EDGE, 0:ROWS, :] + columns_ref[1, EDGE, 0:ROWS, :]


def join(*refs):
    at = 0
    for ref in refs[:-1]:
        size = ref.shape[0]
        refs[-1][at : at + size, :] = ref[...]
        at += size


class Block:
    def __init__(self, main, edge, wet, g_rows=range(ROWS)):
        self.main, self.edge, self.wet, self.g_rows = main, edge, wet, g_rows


def own_block(own_ref, side_ref):
    return Block(
        lambda c, f, r: row_of(own_ref, c, f, r),
        lambda c, r: side_ref[c * ROWS + r],
        lambda row: side_ref[EDGE, row : row + 1, :],
    )


def near_block(in_ref, way):
    def tile(index):
        return in_ref[way, (IN_SIDE + index) * LEVELS : (IN_SIDE + index + 1) * LEVELS, :]

    at = (IN_SIDE + EDGE) * LEVELS
    return Block(
        lambda c, f, r: in_ref[way, pl.ds((c * FIELDS + f) * LEVELS * ROWS + r, LEVELS, stride=ROWS), :],
        lambda c, r: tile(c * ROWS + r),
        lambda row: in_ref[way, at + row : at + row + 1, :],
    )


def far_block(in_ref, way):
    first = 2 if way == 0 else 0

    def tile(index):
        return in_ref[way, (IN_FAR + index) * LEVELS : (IN_FAR + index + 1) * LEVELS, :]

    def main(c, f, r):
        if c == 1:
            return tile(FAR_CHL + r - first)
        return tile(f * ROWS + r if f < PROG else FAR_G + (f - PROG) * 2 + r - first)

    at = (IN_FAR_SIDE + EDGE) * LEVELS
    return Block(
        main,
        lambda c, r: tile(FAR + c * ROWS + r),
        lambda row: in_ref[way, at + row : at + row + 1, :],
        range(first, first + 2),
    )


def next_column(pair):
    here, beyond = pair
    last = lanes() == LANES - 1
    a, b = pltpu.roll(here, LANES - 1, 1), pltpu.roll(beyond, LANES - 1, 1)
    return jnp.where(last, b, a), jnp.where(last, a, b)


def previous_column(pair):
    here, beyond = pair
    start = lanes() == 0
    a, b = pltpu.roll(here, 1, 1), pltpu.roll(beyond, 1, 1)
    return jnp.where(start, b, a), jnp.where(start, a, b)


def both(function, *pairs):
    return tuple(function(*values) for values in zip(*pairs))


def half_minmod(a, b):
    return 0.5 * (jnp.maximum(jnp.minimum(a, b), 0.0) + jnp.minimum(jnp.maximum(a, b), 0.0))


def level_sum(values):
    level = level_index()
    for by in (1, 2, 4):
        values = values + jnp.where(level >= by, pltpu.roll(values, by, 0), 0.0)
    return values


def below(values):
    return pltpu.roll(values, LEVELS - 1, 0)


def above(values):
    return pltpu.roll(values, 1, 0)


def density(temperature, salinity):
    return 0.8 * salinity - 0.2 * temperature


def stirring(rho, column_wet):
    jump = below(rho) - rho
    return (0.02 + 0.1 / (1.0 + 4.0 * jump * jump)) * column_wet


def column_mix(quantity, mixing):
    flux = mixing * (below(quantity) - quantity)
    return flux - above(flux)


def across(quantity, shifted, out_speed, in_speed):
    slope = both(lambda n, q, p: half_minmod(n - q, q - p), shifted, quantity, previous_column(quantity))
    low = both(lambda q, s: q + s, quantity, slope)
    high = both(lambda q, s: q - s, quantity, slope)
    leaving = both(lambda s, lo, hi: s[0] * lo + s[1] * hi, out_speed, low, next_column(high))
    entering = both(lambda s, lo, hi: s[0] * lo + s[1] * hi, in_speed, previous_column(low), high)
    return both(lambda before, after: before - after, entering, leaving)


def split(speed):
    return jnp.maximum(speed, 0.0), jnp.minimum(speed, 0.0)


def face_start(ref, fields, row):
    out = []
    for f in fields:
        here = [ref[f, row, t] for t in range(2)]
        jump = [ref[f, row + 1, t] - here[t] for t in range(2)]
        left = [here[t] + half_minmod(jump[t], here[t] - ref[f, row - 1, t]) for t in range(2)]
        out.append((tuple(jump), tuple(left)))
    return out


def face_step(ref, field, row, jump, left, plus, minus):
    jumps, lefts, fluxes = [], [], []
    for t in range(2):
        near = ref[field, row + 1, t]
        ahead = ref[field, row + 2, t] - near
        slope = half_minmod(ahead, jump[t])
        fluxes.append(plus[t] * left[t] + minus[t] * (near - slope))
        jumps.append(ahead)
        lefts.append(near + slope)
    return tuple(jumps), tuple(lefts), tuple(fluxes)


def load_wet(block, r, wet_ref, row):
    level = level_index().astype(jnp.float32)
    for t in range(2):
        wet_ref[row, t] = jnp.where(level < block.wet(t * ROWS + r), 1.0, 0.0)


def unpack_edge(edge, field):
    return pltpu.roll(edge, (2 * LANES - HALO - 16 * field) % LANES, 1)


def masks(wet_ref, facex_ref, facey_ref, facez_ref, rows):
    not_last = level_index() < LEVELS - 1

    def body(i, carry):
        here = (wet_ref[i, 0], wet_ref[i, 1])
        beside = next_column(here)
        for t in range(2):
            facey_ref[i, t] = 0.5 * here[t] * beside[t]
            facez_ref[i, t] = jnp.where(not_last, here[t] * below(here[t]), 0.0)
        return carry

    lax.fori_loop(0, rows, body, 0, unroll=4)

    def body_x(i, carry):
        for t in range(2):
            facex_ref[i, t] = 0.5 * wet_ref[i, t] * wet_ref[i + 1, t]
        return carry

    lax.fori_loop(0, rows - 1, body_x, 0)


def dynamics(own_ref, side_ref, in_ref, out_ref, q_ref, g_ref, heat_ref, wet_ref, facex_ref, facey_ref, facez_ref):
    blocks = (
        far_block(in_ref, 0),
        near_block(in_ref, 0),
        own_block(own_ref, side_ref),
        near_block(in_ref, 1),
        far_block(in_ref, 1),
    )
    for b, block in enumerate(blocks):
        for r in range(ROWS):
            row = b * ROWS + r
            load_wet(block, r, wet_ref, row)
            edge = block.edge(0, r)
            for f in range(PROG):
                q_ref[0, f, row, 0] = block.main(0, f, r)
                q_ref[0, f, row, 1] = unpack_edge(edge, f)
            if r not in block.g_rows:
                continue
            for f in range(PROG):
                g_ref[f, row, 0] = block.main(0, PROG + f, r)
                g_ref[f, row, 1] = unpack_edge(edge, PROG + f)
            chl = (block.main(1, 0, r), unpack_edge(block.edge(1, r), 0))
            for t in range(2):
                absorb = (0.04 + 0.05 * chl[t] * chl[t]) * wet_ref[row, t]
                lower = jnp.exp(-level_sum(absorb))
                upper = jnp.where(level_index() == 0, 1.0, above(lower))
                heat_ref[row, t] = 0.5 * (upper - lower)
    masks(wet_ref, facex_ref, facey_ref, facez_ref, DYN_ROWS)

    def column(src, row):
        rho = [density(src[2, row, t], src[3, row, t]) for t in range(2)]
        pressure = [level_sum(rho[t] * wet_ref[row, t]) for t in range(2)]
        return tuple(rho), tuple(pressure)

    for step in range(DYN_STEPS):
        src, dst = q_ref.at[step % 2], q_ref.at[(step + 1) % 2]
        first, end = 2 * (step + 1), DYN_ROWS - 2 * (step + 1)
        last_step = step == DYN_STEPS - 1

        def speed_x(row):
            return [split(facex_ref[row, t] * (src[0, row, t] + src[0, row + 1, t])) for t in range(2)]

        started = face_start(src, range(PROG), first - 1)
        speeds = speed_x(first - 1)
        streams = tuple(
            face_step(src, f, first - 1, *started[f], [s[0] for s in speeds], [s[1] for s in speeds])
            for f in range(PROG)
        )
        _, before = column(src, first - 1)
        rho, pressure = column(src, first)

        def body(i, carry, src=src, dst=dst, speed_x=speed_x, last_step=last_step):
            streams, before, rho, pressure = carry
            rho_after, after = column(src, i + 1)
            wet = [wet_ref[i, t] for t in range(2)]
            here = [(src[f, i, 0], src[f, i, 1]) for f in range(PROG)]
            shifted = [next_column(h) for h in here]
            speeds = speed_x(i)
            plus_x, minus_x = [s[0] for s in speeds], [s[1] for s in speeds]
            speed = tuple(facey_ref[i, t] * (here[1][t] + shifted[1][t]) for t in range(2))
            out_y = both(split, speed)
            in_y = both(split, previous_column(speed))
            mixing = [stirring(rho[t], facez_ref[i, t]) for t in range(2)]
            east, west = next_column(pressure), previous_column(pressure)
            new = []
            for f in range(PROG):
                jump, left, entering = streams[f]
                jump, left, leaving = face_step(src, f, i, jump, left, plus_x, minus_x)
                new.append((jump, left, leaving))
                sideways = across(here[f], shifted[f], out_y, in_y)
                for t in range(1 if last_step else 2):
                    tendency = entering[t] - leaving[t] + sideways[t] + column_mix(here[f][t], mixing[t])
                    if f == 0:
                        tendency += CORIOLIS * here[1][t] - (0.5 * PRESSURE) * (after[t] - before[t])
                    elif f == 1:
                        tendency += -CORIOLIS * here[0][t] - (0.5 * PRESSURE) * (east[t] - west[t])
                    elif f == 2:
                        tendency += heat_ref[i, t]
                    tendency = tendency * wet[t]
                    updated = (here[f][t] + 1.5 * tendency - 0.5 * g_ref[f, i, t]) * wet[t]
                    if last_step:
                        rows = pl.ds(i - 2 * ROWS, LEVELS, stride=ROWS)
                        out_ref[f, rows, :] = updated
                        out_ref[PROG + f, rows, :] = tendency
                    else:
                        dst[f, i, t] = updated
                        g_ref[f, i, t] = tendency
            return tuple(new), pressure, rho_after, after

        lax.fori_loop(first, end, body, (streams, before, rho, pressure), unroll=DYN_UNROLL)


def tracers(
    rates_ref, own_ref, side_ref, in_ref, out_ref,
    c_ref, flow_ref, speed_ref, mix_ref, warm_ref, light_ref, wet_ref, facex_ref, facey_ref, facez_ref,
):
    blocks = (near_block(in_ref, 0), own_block(own_ref, side_ref), near_block(in_ref, 1))
    for b, block in enumerate(blocks):
        for r in range(ROWS):
            row = b * ROWS + r
            load_wet(block, r, wet_ref, row)
            edge = block.edge(1, r)
            for f in range(FIELDS):
                c_ref[0, f, row, 0] = block.main(1, f, r)
                c_ref[0, f, row, 1] = unpack_edge(edge, f)
            edge = block.edge(0, r)
            for f in range(PROG):
                flow_ref[f, row, 0] = block.main(0, f, r)
                flow_ref[f, row, 1] = unpack_edge(edge, f)
    masks(wet_ref, facex_ref, facey_ref, facez_ref, TRC_ROWS)

    def prepare(i, carry):
        north = (flow_ref[1, i, 0], flow_ref[1, i, 1])
        speed = tuple(facey_ref[i, t] * (north[t] + n) for t, n in enumerate(next_column(north)))
        before = previous_column(speed)
        for t in range(2):
            plus, minus = split(facex_ref[i, t] * (flow_ref[0, i, t] + flow_ref[0, i + 1, t]))
            speed_ref[0, i, t] = plus
            speed_ref[1, i, t] = minus
            speed_ref[2, i, t] = speed[t]
            speed_ref[3, i, t] = before[t]
            mix_ref[i, t] = stirring(density(flow_ref[2, i, t], flow_ref[3, i, t]), facez_ref[i, t])
            warm_ref[i, t] = jnp.exp(0.1 * flow_ref[2, i, t])
        return carry

    lax.fori_loop(1, TRC_ROWS - 2, prepare, 0)

    group = 4
    for step in range(TRACER_STEPS):
        src, dst = c_ref.at[step % 2], c_ref.at[(step + 1) % 2]
        first, end = 2 * (step + 1), TRC_ROWS - 2 * (step + 1)
        last_step = step == TRACER_STEPS - 1

        def shade(i, carry, src=src):
            for t in range(2):
                chl = src[0, i, t]
                absorb = (0.04 + 0.05 * chl * chl) * wet_ref[i, t]
                light_ref[i, t] = jnp.exp(-level_sum(absorb)) * warm_ref[i, t]
            return carry

        lax.fori_loop(first, end, shade, 0, unroll=4)

        def some(n, carry, src=src, dst=dst, first=first, end=end, last_step=last_step):
            fields = [n * group + k for k in range(group)]

            def pair(ref, *index):
                return (ref[index + (0,)], ref[index + (1,)])

            started = face_start(src, fields, first - 1)
            plus, minus = pair(speed_ref, 0, first - 1), pair(speed_ref, 1, first - 1)
            streams = tuple(
                face_step(src, f, first - 1, *started[k], plus, minus) for k, f in enumerate(fields)
            )

            rates = [(rates_ref[0, pl.ds(f, 1), :], rates_ref[1, pl.ds(f, 1), :]) for f in fields]

            def body(i, streams):
                plus_x, minus_x = pair(speed_ref, 0, i), pair(speed_ref, 1, i)
                out_y, in_y = both(split, pair(speed_ref, 2, i)), both(split, pair(speed_ref, 3, i))
                new = []
                for k, f in enumerate(fields):
                    jump, left, entering = streams[k]
                    jump, left, leaving = face_step(src, f, i, jump, left, plus_x, minus_x)
                    new.append((jump, left, leaving))
                    here = pair(src, f, i)
                    sideways = across(here, next_column(here), out_y, in_y)
                    for t in range(1 if last_step else 2):
                        net = rates[k][0] * light_ref[i, t] - rates[k][1]
                        change = entering[t] - leaving[t] + sideways[t] + column_mix(here[t], mix_ref[i, t])
                        updated = (here[t] + change + net * here[t]) * wet_ref[i, t]
                        if last_step:
                            out_ref[f, pl.ds(i - ROWS, LEVELS, stride=ROWS), :] = updated
                        else:
                            dst[f, i, t] = updated
                return tuple(new)

            lax.fori_loop(first, end, body, streams, unroll=TRC_UNROLL)
            return carry

        lax.fori_loop(0, FIELDS // group, some, 0)


def advance(
    comp_ref, rates_ref, own_ref, side_ref, in_ref, out_ref,
    q_ref, g_ref, heat_ref, c_ref, flow_ref, speed_ref, mix_ref, warm_ref, light_ref,
    wet_ref, facex_ref, facey_ref, facez_ref,
):
    @pl.when(comp_ref[0] == 0)
    def _():
        dynamics(own_ref, side_ref, in_ref, out_ref, q_ref, g_ref, heat_ref, wet_ref, facex_ref, facey_ref, facez_ref)

    @pl.when(comp_ref[0] == 1)
    def _():
        tracers(
            rates_ref, own_ref, side_ref, in_ref, out_ref,
            c_ref, flow_ref, speed_ref, mix_ref, warm_ref, light_ref, wet_ref, facex_ref, facey_ref, facez_ref,
        )


def call(kernel, smem, vmem, outs, scratch=(), flops=0):
    out_shape = tuple(jax.ShapeDtypeStruct(s, jnp.float32) for s in outs)
    size = 4 * sum(a.size for a in vmem) + 4 * sum(s.size for s in out_shape)
    result = pl.pallas_call(
        kernel,
        out_shape=out_shape,
        in_specs=[pl.BlockSpec(memory_space=pltpu.SMEM)] * len(smem)
        + [pl.BlockSpec(memory_space=pltpu.VMEM)] * len(vmem),
        out_specs=tuple(pl.BlockSpec(memory_space=pltpu.VMEM) for _ in outs),
        scratch_shapes=[pltpu.VMEM(s + TILE, jnp.float32) for s in scratch],
        compiler_params=pltpu.CompilerParams(vmem_limit_bytes=24 * 1024 * 1024),
        cost_estimate=pl.CostEstimate(flops=flops, bytes_accessed=size, transcendentals=0),
    )(*smem, *vmem)
    return result


def all_steps(comp, rates, own, side, received):
    scratch = [
        (2, PROG, DYN_ROWS, 2),
        (PROG, DYN_ROWS, 2),
        (DYN_ROWS, 2),
        (2, FIELDS, TRC_ROWS, 2),
        (PROG, TRC_ROWS, 2),
        (4, TRC_ROWS, 2),
        (TRC_ROWS, 2),
        (TRC_ROWS, 2),
        (TRC_ROWS, 2),
        (DYN_ROWS, 2),
        (DYN_ROWS, 2),
        (DYN_ROWS, 2),
        (DYN_ROWS, 2),
    ]
    (out,) = call(
        advance, [comp], [rates, own, side, received],
        [(FIELDS, LEVELS * ROWS, LANES)], scratch, flops=20_000_000,
    )
    return out


def neighbours(gx, gy, by_x, by_y):
    pairs = []
    for c, way in ((0, 1), (1, -1)):
        for i in range(gx):
            for j in range(gy):
                a, b = i + way * by_x, j + way * by_y
                if 0 <= a < gx and 0 <= b < gy:
                    pairs.append(((c * gx + i) * gy + j, (c * gx + a) * gy + b))
    return pairs


def local(ocean_state, land_sea, depth_levels, growth, decay):
    axes = ("comp", "gx", "gy")
    gx, gy = lax.axis_size("gx"), lax.axis_size("gy")
    comp = lax.axis_index("comp").astype(jnp.int32).reshape(1)
    fields = ocean_state.reshape(FIELDS, LEVELS * ROWS, LANES)
    own = lax.all_gather(fields, "comp")
    near_in = lax.ppermute(own.reshape(MAIN * LEVELS, LANES), axes, neighbours(gx, gy, 1, 0))
    columns, far = call(
        pack_columns, [comp], [own, land_sea, depth_levels], [(SIDE,) + TILE, (FAR,) + TILE]
    )
    columns = lax.ppermute(columns, axes, neighbours(gx, gy, 0, -1))
    far_in = lax.ppermute(far, axes, neighbours(gx, gy, 2, 0))
    rates = jnp.broadcast_to(jnp.stack([growth, decay])[:, :, None], (2, FIELDS, LANES))
    columns = lax.all_gather(columns, "comp")
    (side,) = call(pack_corners, [], [land_sea, depth_levels, columns], [(SIDE,) + TILE])
    side_in = lax.ppermute(side, axes, neighbours(gx, gy, 1, 0))
    far_side_in = lax.ppermute(side, axes, neighbours(gx, gy, 2, 0))
    parts = [a.reshape(-1, LANES) for a in (near_in, side_in, far_in, far_side_in)]
    (received,) = call(join, [], parts, [(IN * LEVELS, LANES)])
    received = lax.all_gather(received, "comp")
    out = all_steps(comp, rates, own, side, received)
    return out.reshape(ocean_state.shape)


def solution(mesh):
    placed = (P("comp", None, None, "gx", "gy"), P("gx", "gy"), P("gx", "gy"), P(), P())
    return jax.shard_map(
        local,
        mesh=mesh,
        in_specs=placed,
        out_specs=P("comp", None, None, "gx", "gy"),
        check_vma=False,
    )
```

```python
import functools

import jax
import jax.numpy as jnp
from jax import lax
from jax.experimental import pallas as pl
from jax.experimental.pallas import tpu as pltpu
from jax.sharding import PartitionSpec as P

DYN_STEPS = 4
TRACER_STEPS = 2
CORIOLIS = 0.2
PRESSURE = 0.01

LEVELS = 8
LANES = 128
FIELDS = 8
PROG = 4
ROWS = 4
HALO = 8
MAIN = 2 * FIELDS * ROWS
EDGE = 2 * ROWS
SIDE = EDGE + 1
FAR_G = PROG * ROWS
FAR_CHL = FAR_G + PROG * 2
FAR = FAR_CHL + 2
IN_SIDE = MAIN
IN_FAR = IN_SIDE + SIDE
IN_FAR_SIDE = IN_FAR + FAR
IN = IN_FAR_SIDE + SIDE
DYN_ROWS = 5 * ROWS
TRC_ROWS = 3 * ROWS
TILE = (LEVELS, LANES)
DYN_UNROLL = 4
TRC_UNROLL = 4


def lanes():
    return lax.broadcasted_iota(jnp.int32, TILE, 1)


def level_index():
    return lax.broadcasted_iota(jnp.int32, TILE, 0)


def edge_source(comp):
    first = jnp.where(comp == 0, 0, LANES - HALO)
    lane = lanes()
    return (lane >= first) & (lane < first + HALO)


def wet_count(land_ref, depth_ref):
    return jnp.where(land_ref[...] == 1, depth_ref[...], 0).astype(jnp.float32)


def row_of(own_ref, comp, field, row):
    return own_ref[comp, field, pl.ds(row, LEVELS, stride=ROWS), :]


def pack_columns(comp_ref, own_ref, land_ref, depth_ref, out_ref, far_ref):
    comp = comp_ref[0]
    source = edge_source(comp)
    for c in range(2):
        for r in range(ROWS):
            total = None
            for f in range(FIELDS):
                part = jnp.where(source, row_of(own_ref, c, f, r), 0.0)
                part = pltpu.roll(part, (16 * f + HALO) % LANES, 1)
                total = part if total is None else total + part
            out_ref[c * ROWS + r] = total
    count = wet_count(land_ref, depth_ref)
    out_ref[EDGE] = jnp.zeros(TILE, jnp.float32)
    out_ref[EDGE, 0:ROWS, :] = jnp.where(source[0:ROWS], count, 0.0)
    for f in range(PROG):
        for r in range(ROWS):
            far_ref[f * ROWS + r] = row_of(own_ref, 0, f, r)
    first = jnp.where(comp == 0, 0, 2)
    for k in range(2):
        for f in range(PROG):
            far_ref[FAR_G + f * 2 + k] = row_of(own_ref, 0, PROG + f, first + k)
        far_ref[FAR_CHL + k] = row_of(own_ref, 1, 0, first + k)


def pack_corners(land_ref, depth_ref, columns_ref, side_ref):
    for t in range(EDGE):
        side_ref[t] = columns_ref[0, t] + columns_ref[1, t]
    side_ref[EDGE, 0:ROWS, :] = wet_count(land_ref, depth_ref)
    side_ref[EDGE, ROWS : 2 * ROWS, :] = columns_ref[0, EDGE, 0:ROWS, :] + columns_ref[1, EDGE, 0:ROWS, :]


def join(*refs):
    at = 0
    for ref in refs[:-1]:
        size = ref.shape[0]
        refs[-1][at : at + size, :] = ref[...]
        at += size


class Block:
    def __init__(self, main, edge, wet, g_rows=range(ROWS)):
        self.main, self.edge, self.wet, self.g_rows = main, edge, wet, g_rows


def own_block(own_ref, side_ref):
    return Block(
        lambda c, f, r: row_of(own_ref, c, f, r),
        lambda c, r: side_ref[c * ROWS + r],
        lambda row: side_ref[EDGE, row : row + 1, :],
    )


def near_block(in_ref, way):
    def tile(index):
        return in_ref[way, (IN_SIDE + index) * LEVELS : (IN_SIDE + index + 1) * LEVELS, :]

    at = (IN_SIDE + EDGE) * LEVELS
    return Block(
        lambda c, f, r: in_ref[way, pl.ds((c * FIELDS + f) * LEVELS * ROWS + r, LEVELS, stride=ROWS), :],
        lambda c, r: tile(c * ROWS + r),
        lambda row: in_ref[way, at + row : at + row + 1, :],
    )


def far_block(in_ref, way):
    first = 2 if way == 0 else 0
    core = 1 - way

    def tile(index):
        return in_ref[core, (IN_FAR + index) * LEVELS : (IN_FAR + index + 1) * LEVELS, :]

    def main(c, f, r):
        if c == 1:
            return tile(FAR_CHL + r - first)
        return tile(f * ROWS + r if f < PROG else FAR_G + (f - PROG) * 2 + r - first)

    at = (IN_FAR_SIDE + EDGE) * LEVELS
    return Block(
        main,
        lambda c, r: tile(FAR + c * ROWS + r),
        lambda row: in_ref[core, at + row : at + row + 1, :],
        range(first, first + 2),
    )


def next_column(pair):
    here, beyond = pair
    last = lanes() == LANES - 1
    a, b = pltpu.roll(here, LANES - 1, 1), pltpu.roll(beyond, LANES - 1, 1)
    return jnp.where(last, b, a), jnp.where(last, a, b)


def previous_column(pair):
    here, beyond = pair
    start = lanes() == 0
    a, b = pltpu.roll(here, 1, 1), pltpu.roll(beyond, 1, 1)
    return jnp.where(start, b, a), jnp.where(start, a, b)


def both(function, *pairs):
    return tuple(function(*values) for values in zip(*pairs))


def half_minmod(a, b):
    return 0.5 * (jnp.maximum(jnp.minimum(a, b), 0.0) + jnp.minimum(jnp.maximum(a, b), 0.0))


def level_sum(values):
    level = level_index()
    for by in (1, 2, 4):
        values = values + jnp.where(level >= by, pltpu.roll(values, by, 0), 0.0)
    return values


def below(values):
    return pltpu.roll(values, LEVELS - 1, 0)


def above(values):
    return pltpu.roll(values, 1, 0)


def density(temperature, salinity):
    return 0.8 * salinity - 0.2 * temperature


def stirring(rho, column_wet):
    jump = below(rho) - rho
    return (0.02 + 0.1 / (1.0 + 4.0 * jump * jump)) * column_wet


def column_mix(quantity, mixing):
    flux = mixing * (below(quantity) - quantity)
    return flux - above(flux)


def across(quantity, shifted, out_speed, in_speed):
    slope = both(lambda n, q, p: half_minmod(n - q, q - p), shifted, quantity, previous_column(quantity))
    low = both(lambda q, s: q + s, quantity, slope)
    high = both(lambda q, s: q - s, quantity, slope)
    leaving = both(lambda s, lo, hi: s[0] * lo + s[1] * hi, out_speed, low, next_column(high))
    entering = both(lambda s, lo, hi: s[0] * lo + s[1] * hi, in_speed, previous_column(low), high)
    return both(lambda before, after: before - after, entering, leaving)


def split(speed):
    return jnp.maximum(speed, 0.0), jnp.minimum(speed, 0.0)


def face_start(ref, fields, row):
    out = []
    for f in fields:
        here = [ref[f, row, t] for t in range(2)]
        jump = [ref[f, row + 1, t] - here[t] for t in range(2)]
        left = [here[t] + half_minmod(jump[t], here[t] - ref[f, row - 1, t]) for t in range(2)]
        out.append((tuple(jump), tuple(left)))
    return out


def face_step(ref, field, row, jump, left, plus, minus):
    jumps, lefts, fluxes = [], [], []
    for t in range(2):
        near = ref[field, row + 1, t]
        ahead = ref[field, row + 2, t] - near
        slope = half_minmod(ahead, jump[t])
        fluxes.append(plus[t] * left[t] + minus[t] * (near - slope))
        jumps.append(ahead)
        lefts.append(near + slope)
    return tuple(jumps), tuple(lefts), tuple(fluxes)


def load_wet(block, r, wet_ref, row):
    level = level_index().astype(jnp.float32)
    for t in range(2):
        wet_ref[row, t] = jnp.where(level < block.wet(t * ROWS + r), 1.0, 0.0)


def unpack_edge(edge, field):
    return pltpu.roll(edge, (2 * LANES - HALO - 16 * field) % LANES, 1)


def masks(wet_ref, facex_ref, facey_ref, facez_ref, rows):
    not_last = level_index() < LEVELS - 1

    def body(i, carry):
        here = (wet_ref[i, 0], wet_ref[i, 1])
        beside = next_column(here)
        for t in range(2):
            facey_ref[i, t] = 0.5 * here[t] * beside[t]
            facez_ref[i, t] = jnp.where(not_last, here[t] * below(here[t]), 0.0)
        return carry

    lax.fori_loop(0, rows, body, 0, unroll=4)

    def body_x(i, carry):
        for t in range(2):
            facex_ref[i, t] = 0.5 * wet_ref[i, t] * wet_ref[i + 1, t]
        return carry

    lax.fori_loop(0, rows - 1, body_x, 0)


def dynamics(own_ref, side_ref, in_ref, out_ref, q_ref, g_ref, heat_ref, wet_ref, facex_ref, facey_ref, facez_ref):
    blocks = (
        far_block(in_ref, 0),
        near_block(in_ref, 0),
        own_block(own_ref, side_ref),
        near_block(in_ref, 1),
        far_block(in_ref, 1),
    )
    for b, block in enumerate(blocks):
        for r in range(ROWS):
            row = b * ROWS + r
            load_wet(block, r, wet_ref, row)
            edge = block.edge(0, r)
            for f in range(PROG):
                q_ref[0, f, row, 0] = block.main(0, f, r)
                q_ref[0, f, row, 1] = unpack_edge(edge, f)
            if r not in block.g_rows:
                continue
            for f in range(PROG):
                g_ref[f, row, 0] = block.main(0, PROG + f, r)
                g_ref[f, row, 1] = unpack_edge(edge, PROG + f)
            chl = (block.main(1, 0, r), unpack_edge(block.edge(1, r), 0))
            for t in range(2):
                absorb = (0.04 + 0.05 * chl[t] * chl[t]) * wet_ref[row, t]
                lower = jnp.exp(-level_sum(absorb))
                upper = jnp.where(level_index() == 0, 1.0, above(lower))
                heat_ref[row, t] = 0.5 * (upper - lower)
    masks(wet_ref, facex_ref, facey_ref, facez_ref, DYN_ROWS)

    def column(src, row):
        rho = [density(src[2, row, t], src[3, row, t]) for t in range(2)]
        pressure = [level_sum(rho[t] * wet_ref[row, t]) for t in range(2)]
        return tuple(rho), tuple(pressure)

    for step in range(DYN_STEPS):
        src, dst = q_ref.at[step % 2], q_ref.at[(step + 1) % 2]
        first, end = 2 * (step + 1), DYN_ROWS - 2 * (step + 1)
        last_step = step == DYN_STEPS - 1

        def speed_x(row):
            return [split(facex_ref[row, t] * (src[0, row, t] + src[0, row + 1, t])) for t in range(2)]

        started = face_start(src, range(PROG), first - 1)
        speeds = speed_x(first - 1)
        streams = tuple(
            face_step(src, f, first - 1, *started[f], [s[0] for s in speeds], [s[1] for s in speeds])
            for f in range(PROG)
        )
        _, before = column(src, first - 1)
        rho, pressure = column(src, first)

        def body(i, carry, src=src, dst=dst, speed_x=speed_x, last_step=last_step):
            streams, before, rho, pressure = carry
            rho_after, after = column(src, i + 1)
            wet = [wet_ref[i, t] for t in range(2)]
            here = [(src[f, i, 0], src[f, i, 1]) for f in range(PROG)]
            shifted = [next_column(h) for h in here]
            speeds = speed_x(i)
            plus_x, minus_x = [s[0] for s in speeds], [s[1] for s in speeds]
            speed = tuple(facey_ref[i, t] * (here[1][t] + shifted[1][t]) for t in range(2))
            out_y = both(split, speed)
            in_y = both(split, previous_column(speed))
            mixing = [stirring(rho[t], facez_ref[i, t]) for t in range(2)]
            east, west = next_column(pressure), previous_column(pressure)
            new = []
            for f in range(PROG):
                jump, left, entering = streams[f]
                jump, left, leaving = face_step(src, f, i, jump, left, plus_x, minus_x)
                new.append((jump, left, leaving))
                sideways = across(here[f], shifted[f], out_y, in_y)
                for t in range(1 if last_step else 2):
                    tendency = entering[t] - leaving[t] + sideways[t] + column_mix(here[f][t], mixing[t])
                    if f == 0:
                        tendency += CORIOLIS * here[1][t] - (0.5 * PRESSURE) * (after[t] - before[t])
                    elif f == 1:
                        tendency += -CORIOLIS * here[0][t] - (0.5 * PRESSURE) * (east[t] - west[t])
                    elif f == 2:
                        tendency += heat_ref[i, t]
                    tendency = tendency * wet[t]
                    updated = (here[f][t] + 1.5 * tendency - 0.5 * g_ref[f, i, t]) * wet[t]
                    if last_step:
                        rows = pl.ds(i - 2 * ROWS, LEVELS, stride=ROWS)
                        out_ref[f, rows, :] = updated
                        out_ref[PROG + f, rows, :] = tendency
                    else:
                        dst[f, i, t] = updated
                        g_ref[f, i, t] = tendency
            return tuple(new), pressure, rho_after, after

        lax.fori_loop(first, end, body, (streams, before, rho, pressure), unroll=DYN_UNROLL)


def tracers(
    rates_ref, own_ref, side_ref, in_ref, out_ref,
    c_ref, flow_ref, speed_ref, mix_ref, warm_ref, light_ref, wet_ref, facex_ref, facey_ref, facez_ref,
):
    blocks = (near_block(in_ref, 0), own_block(own_ref, side_ref), near_block(in_ref, 1))
    for b, block in enumerate(blocks):
        for r in range(ROWS):
            row = b * ROWS + r
            load_wet(block, r, wet_ref, row)
            edge = block.edge(1, r)
            for f in range(FIELDS):
                c_ref[0, f, row, 0] = block.main(1, f, r)
                c_ref[0, f, row, 1] = unpack_edge(edge, f)
            edge = block.edge(0, r)
            for f in range(PROG):
                flow_ref[f, row, 0] = block.main(0, f, r)
                flow_ref[f, row, 1] = unpack_edge(edge, f)
    masks(wet_ref, facex_ref, facey_ref, facez_ref, TRC_ROWS)

    def prepare(i, carry):
        north = (flow_ref[1, i, 0], flow_ref[1, i, 1])
        speed = tuple(facey_ref[i, t] * (north[t] + n) for t, n in enumerate(next_column(north)))
        before = previous_column(speed)
        for t in range(2):
            plus, minus = split(facex_ref[i, t] * (flow_ref[0, i, t] + flow_ref[0, i + 1, t]))
            speed_ref[0, i, t] = plus
            speed_ref[1, i, t] = minus
            speed_ref[2, i, t] = speed[t]
            speed_ref[3, i, t] = before[t]
            mix_ref[i, t] = stirring(density(flow_ref[2, i, t], flow_ref[3, i, t]), facez_ref[i, t])
            warm_ref[i, t] = jnp.exp(0.1 * flow_ref[2, i, t])
        return carry

    lax.fori_loop(1, TRC_ROWS - 2, prepare, 0)

    group = 4
    for step in range(TRACER_STEPS):
        src, dst = c_ref.at[step % 2], c_ref.at[(step + 1) % 2]
        first, end = 2 * (step + 1), TRC_ROWS - 2 * (step + 1)
        last_step = step == TRACER_STEPS - 1

        def shade(i, carry, src=src):
            for t in range(2):
                chl = src[0, i, t]
                absorb = (0.04 + 0.05 * chl * chl) * wet_ref[i, t]
                light_ref[i, t] = jnp.exp(-level_sum(absorb)) * warm_ref[i, t]
            return carry

        lax.fori_loop(first, end, shade, 0, unroll=4)

        def some(n, carry, src=src, dst=dst, first=first, end=end, last_step=last_step):
            fields = [n * group + k for k in range(group)]

            def pair(ref, *index):
                return (ref[index + (0,)], ref[index + (1,)])

            started = face_start(src, fields, first - 1)
            plus, minus = pair(speed_ref, 0, first - 1), pair(speed_ref, 1, first - 1)
            streams = tuple(
                face_step(src, f, first - 1, *started[k], plus, minus) for k, f in enumerate(fields)
            )

            rates = [(rates_ref[0, pl.ds(f, 1), :], rates_ref[1, pl.ds(f, 1), :]) for f in fields]

            def body(i, streams):
                plus_x, minus_x = pair(speed_ref, 0, i), pair(speed_ref, 1, i)
                out_y, in_y = both(split, pair(speed_ref, 2, i)), both(split, pair(speed_ref, 3, i))
                new = []
                for k, f in enumerate(fields):
                    jump, left, entering = streams[k]
                    jump, left, leaving = face_step(src, f, i, jump, left, plus_x, minus_x)
                    new.append((jump, left, leaving))
                    here = pair(src, f, i)
                    sideways = across(here, next_column(here), out_y, in_y)
                    for t in range(1 if last_step else 2):
                        net = rates[k][0] * light_ref[i, t] - rates[k][1]
                        change = entering[t] - leaving[t] + sideways[t] + column_mix(here[t], mix_ref[i, t])
                        updated = (here[t] + change + net * here[t]) * wet_ref[i, t]
                        if last_step:
                            out_ref[f, pl.ds(i - ROWS, LEVELS, stride=ROWS), :] = updated
                        else:
                            dst[f, i, t] = updated
                return tuple(new)

            lax.fori_loop(first, end, body, streams, unroll=TRC_UNROLL)
            return carry

        lax.fori_loop(0, FIELDS // group, some, 0)


def advance(
    comp_ref, rates_ref, own_ref, side_ref, in_ref, out_ref,
    q_ref, g_ref, heat_ref, c_ref, flow_ref, speed_ref, mix_ref, warm_ref, light_ref,
    wet_ref, facex_ref, facey_ref, facez_ref,
):
    @pl.when(comp_ref[0] == 0)
    def _():
        dynamics(own_ref, side_ref, in_ref, out_ref, q_ref, g_ref, heat_ref, wet_ref, facex_ref, facey_ref, facez_ref)

    @pl.when(comp_ref[0] == 1)
    def _():
        tracers(
            rates_ref, own_ref, side_ref, in_ref, out_ref,
            c_ref, flow_ref, speed_ref, mix_ref, warm_ref, light_ref, wet_ref, facex_ref, facey_ref, facez_ref,
        )


def call(kernel, smem, vmem, outs, scratch=(), flops=0):
    out_shape = tuple(jax.ShapeDtypeStruct(s, jnp.float32) for s in outs)
    size = 4 * sum(a.size for a in vmem) + 4 * sum(s.size for s in out_shape)
    result = pl.pallas_call(
        kernel,
        out_shape=out_shape,
        in_specs=[pl.BlockSpec(memory_space=pltpu.SMEM)] * len(smem)
        + [pl.BlockSpec(memory_space=pltpu.VMEM)] * len(vmem),
        out_specs=tuple(pl.BlockSpec(memory_space=pltpu.VMEM) for _ in outs),
        scratch_shapes=[pltpu.VMEM(s + TILE, jnp.float32) for s in scratch],
        compiler_params=pltpu.CompilerParams(vmem_limit_bytes=24 * 1024 * 1024),
        cost_estimate=pl.CostEstimate(flops=flops, bytes_accessed=size, transcendentals=0),
    )(*smem, *vmem)
    return result


def all_steps(comp, rates, own, side, received):
    scratch = [
        (2, PROG, DYN_ROWS, 2),
        (PROG, DYN_ROWS, 2),
        (DYN_ROWS, 2),
        (2, FIELDS, TRC_ROWS, 2),
        (PROG, TRC_ROWS, 2),
        (4, TRC_ROWS, 2),
        (TRC_ROWS, 2),
        (TRC_ROWS, 2),
        (TRC_ROWS, 2),
        (DYN_ROWS, 2),
        (DYN_ROWS, 2),
        (DYN_ROWS, 2),
        (DYN_ROWS, 2),
    ]
    (out,) = call(
        advance, [comp], [rates, own, side, received],
        [(FIELDS, LEVELS * ROWS, LANES)], scratch, flops=20_000_000,
    )
    return out


def neighbours(gx, gy, by_x, by_y):
    pairs = []
    for c, way in ((0, 1), (1, -1)):
        for i in range(gx):
            for j in range(gy):
                a, b = i + way * by_x, j + way * by_y
                if 0 <= a < gx and 0 <= b < gy:
                    pairs.append(((c * gx + i) * gy + j, (c * gx + a) * gy + b))
    return pairs


def local(ocean_state, land_sea, depth_levels, growth, decay):
    axes = ("comp", "gx", "gy")
    gx, gy = lax.axis_size("gx"), lax.axis_size("gy")
    comp = lax.axis_index("comp").astype(jnp.int32).reshape(1)
    fields = ocean_state.reshape(FIELDS, LEVELS * ROWS, LANES)
    own = lax.all_gather(fields, "comp")
    near_in = lax.ppermute(own.reshape(MAIN * LEVELS, LANES), axes, neighbours(gx, gy, 1, 0))
    columns, far = call(
        pack_columns, [comp], [own, land_sea, depth_levels], [(SIDE,) + TILE, (FAR,) + TILE]
    )
    columns = lax.ppermute(columns, axes, neighbours(gx, gy, 0, -1))
    far_in = lax.ppermute(far, axes, neighbours(gx, gy, -2, 0))
    rates = jnp.broadcast_to(jnp.stack([growth, decay])[:, :, None], (2, FIELDS, LANES))
    columns = lax.all_gather(columns, "comp")
    (side,) = call(pack_corners, [], [land_sea, depth_levels, columns], [(SIDE,) + TILE])
    side_in = lax.ppermute(side, axes, neighbours(gx, gy, 1, 0))
    far_side_in = lax.ppermute(side, axes, neighbours(gx, gy, -2, 0))
    parts = [a.reshape(-1, LANES) for a in (near_in, side_in, far_in, far_side_in)]
    (received,) = call(join, [], parts, [(IN * LEVELS, LANES)])
    received = lax.all_gather(received, "comp")
    out = all_steps(comp, rates, own, side, received)
    return out.reshape(ocean_state.shape)


def solution(mesh):
    placed = (P("comp", None, None, "gx", "gy"), P("gx", "gy"), P("gx", "gy"), P(), P())
    return jax.shard_map(
        local,
        mesh=mesh,
        in_specs=placed,
        out_specs=P("comp", None, None, "gx", "gy"),
        check_vma=False,
    )
```

```python
import functools

import jax
import jax.numpy as jnp
from jax import lax
from jax.experimental import pallas as pl
from jax.experimental.pallas import tpu as pltpu
from jax.sharding import PartitionSpec as P

DYN_STEPS = 4
TRACER_STEPS = 2
CORIOLIS = 0.2
PRESSURE = 0.01

LEVELS = 8
LANES = 128
FIELDS = 8
PROG = 4
ROWS = 4
HALO = 8
MAIN = 2 * FIELDS * ROWS
EDGE = 2 * ROWS
SIDE = EDGE + 1
FAR_G = PROG * ROWS
FAR_CHL = FAR_G + PROG * 2
FAR = FAR_CHL + 2
IN_SIDE = MAIN
IN_FAR = IN_SIDE + SIDE
IN_FAR_SIDE = IN_FAR + FAR
FAR_SIDE = 2
IN = IN_FAR_SIDE + FAR_SIDE
DYN_ROWS = 5 * ROWS
TRC_ROWS = 3 * ROWS
TILE = (LEVELS, LANES)
DYN_UNROLL = 4
TRC_UNROLL = 4


def lanes():
    return lax.broadcasted_iota(jnp.int32, TILE, 1)


def level_index():
    return lax.broadcasted_iota(jnp.int32, TILE, 0)


def edge_source(comp):
    first = jnp.where(comp == 0, 0, LANES - HALO)
    lane = lanes()
    return (lane >= first) & (lane < first + HALO)


def wet_count(land_ref, depth_ref):
    return jnp.where(land_ref[...] == 1, depth_ref[...], 0).astype(jnp.float32)


def row_of(own_ref, comp, field, row):
    return own_ref[comp, field, pl.ds(row, LEVELS, stride=ROWS), :]


def pack_columns(comp_ref, own_ref, land_ref, depth_ref, out_ref, far_ref):
    comp = comp_ref[0]
    source = edge_source(comp)
    for c in range(2):
        for r in range(ROWS):
            total = None
            for f in range(FIELDS):
                part = jnp.where(source, row_of(own_ref, c, f, r), 0.0)
                part = pltpu.roll(part, (16 * f + HALO) % LANES, 1)
                total = part if total is None else total + part
            out_ref[c * ROWS + r] = total
    count = wet_count(land_ref, depth_ref)
    out_ref[EDGE] = jnp.zeros(TILE, jnp.float32)
    out_ref[EDGE, 0:ROWS, :] = jnp.where(source[0:ROWS], count, 0.0)
    for f in range(PROG):
        for r in range(ROWS):
            far_ref[f * ROWS + r] = row_of(own_ref, 0, f, r)
    first = jnp.where(comp == 0, 2, 0)
    for k in range(2):
        for f in range(PROG):
            far_ref[FAR_G + f * 2 + k] = row_of(own_ref, 0, PROG + f, first + k)
        far_ref[FAR_CHL + k] = row_of(own_ref, 1, 0, first + k)


def pack_corners(comp_ref, land_ref, depth_ref, columns_ref, side_ref, far_ref):
    for t in range(EDGE):
        side_ref[t] = columns_ref[0, t] + columns_ref[1, t]
    first = jnp.where(comp_ref[0] == 0, 2, 0)
    near, far = [columns_ref[0, first + k] + columns_ref[1, first + k] for k in range(2)]
    far_ref[0] = jnp.where(lanes() < LANES // 2, near, pltpu.roll(far, LANES // 2, 1))
    count = wet_count(land_ref, depth_ref)
    outer = columns_ref[0, EDGE, 0:ROWS, :] + columns_ref[1, EDGE, 0:ROWS, :]
    for ref, at in ((side_ref, EDGE), (far_ref, 1)):
        ref[at, 0:ROWS, :] = count
        ref[at, ROWS : 2 * ROWS, :] = outer


def join(*refs):
    at = 0
    for ref in refs[:-1]:
        size = ref.shape[0]
        refs[-1][at : at + size, :] = ref[...]
        at += size


class Block:
    def __init__(self, main, edge, wet, g_rows=range(ROWS)):
        self.main, self.edge, self.wet, self.g_rows = main, edge, wet, g_rows


def own_block(own_ref, side_ref):
    return Block(
        lambda c, f, r: row_of(own_ref, c, f, r),
        lambda c, r: side_ref[c * ROWS + r],
        lambda row: side_ref[EDGE, row : row + 1, :],
    )


def near_block(in_ref, way):
    def tile(index):
        return in_ref[way, (IN_SIDE + index) * LEVELS : (IN_SIDE + index + 1) * LEVELS, :]

    at = (IN_SIDE + EDGE) * LEVELS
    return Block(
        lambda c, f, r: in_ref[way, pl.ds((c * FIELDS + f) * LEVELS * ROWS + r, LEVELS, stride=ROWS), :],
        lambda c, r: tile(c * ROWS + r),
        lambda row: in_ref[way, at + row : at + row + 1, :],
    )


def far_block(in_ref, way):
    first = 2 if way == 0 else 0

    def tile(index):
        return in_ref[way, (IN_FAR + index) * LEVELS : (IN_FAR + index + 1) * LEVELS, :]

    def main(c, f, r):
        if c == 1:
            return tile(FAR_CHL + r - first)
        return tile(f * ROWS + r if f < PROG else FAR_G + (f - PROG) * 2 + r - first)

    def edge(c, r):
        if c == 1 or r - first not in (0, 1):
            return jnp.zeros(TILE, jnp.float32)
        return tile(FAR) if r == first else pltpu.roll(tile(FAR), LANES // 2, 1)

    at = (IN_FAR_SIDE + 1) * LEVELS
    return Block(
        main,
        edge,
        lambda row: in_ref[way, at + row : at + row + 1, :],
        range(first, first + 2),
    )


def next_column(pair):
    here, beyond = pair
    last = lanes() == LANES - 1
    a, b = pltpu.roll(here, LANES - 1, 1), pltpu.roll(beyond, LANES - 1, 1)
    return jnp.where(last, b, a), jnp.where(last, a, b)


def previous_column(pair):
    here, beyond = pair
    start = lanes() == 0
    a, b = pltpu.roll(here, 1, 1), pltpu.roll(beyond, 1, 1)
    return jnp.where(start, b, a), jnp.where(start, a, b)


def both(function, *pairs):
    return tuple(function(*values) for values in zip(*pairs))


def half_minmod(a, b):
    return 0.5 * (jnp.maximum(jnp.minimum(a, b), 0.0) + jnp.minimum(jnp.maximum(a, b), 0.0))


def level_sum(values):
    level = level_index()
    for by in (1, 2, 4):
        values = values + jnp.where(level >= by, pltpu.roll(values, by, 0), 0.0)
    return values


def below(values):
    return pltpu.roll(values, LEVELS - 1, 0)


def above(values):
    return pltpu.roll(values, 1, 0)


def density(temperature, salinity):
    return 0.8 * salinity - 0.2 * temperature


def stirring(rho, column_wet):
    jump = below(rho) - rho
    return (0.02 + 0.1 / (1.0 + 4.0 * jump * jump)) * column_wet


def column_mix(quantity, mixing):
    flux = mixing * (below(quantity) - quantity)
    return flux - above(flux)


def across(quantity, shifted, out_speed, in_speed):
    slope = both(lambda n, q, p: half_minmod(n - q, q - p), shifted, quantity, previous_column(quantity))
    low = both(lambda q, s: q + s, quantity, slope)
    high = both(lambda q, s: q - s, quantity, slope)
    leaving = both(lambda s, lo, hi: s[0] * lo + s[1] * hi, out_speed, low, next_column(high))
    entering = both(lambda s, lo, hi: s[0] * lo + s[1] * hi, in_speed, previous_column(low), high)
    return both(lambda before, after: before - after, entering, leaving)


def split(speed):
    return jnp.maximum(speed, 0.0), jnp.minimum(speed, 0.0)


def face_start(ref, fields, row):
    out = []
    for f in fields:
        here = [ref[f, row, t] for t in range(2)]
        jump = [ref[f, row + 1, t] - here[t] for t in range(2)]
        left = [here[t] + half_minmod(jump[t], here[t] - ref[f, row - 1, t]) for t in range(2)]
        out.append((tuple(jump), tuple(left)))
    return out


def face_step(ref, field, row, jump, left, plus, minus):
    jumps, lefts, fluxes = [], [], []
    for t in range(2):
        near = ref[field, row + 1, t]
        ahead = ref[field, row + 2, t] - near
        slope = half_minmod(ahead, jump[t])
        fluxes.append(plus[t] * left[t] + minus[t] * (near - slope))
        jumps.append(ahead)
        lefts.append(near + slope)
    return tuple(jumps), tuple(lefts), tuple(fluxes)


def load_wet(block, r, wet_ref, row):
    level = level_index().astype(jnp.float32)
    for t in range(2):
        wet_ref[row, t] = jnp.where(level < block.wet(t * ROWS + r), 1.0, 0.0)


def unpack_edge(edge, field):
    return pltpu.roll(edge, (2 * LANES - HALO - 16 * field) % LANES, 1)


def masks(wet_ref, facex_ref, facey_ref, facez_ref, rows):
    not_last = level_index() < LEVELS - 1

    def body(i, carry):
        here = (wet_ref[i, 0], wet_ref[i, 1])
        beside = next_column(here)
        for t in range(2):
            facey_ref[i, t] = 0.5 * here[t] * beside[t]
            facez_ref[i, t] = jnp.where(not_last, here[t] * below(here[t]), 0.0)
        return carry

    lax.fori_loop(0, rows, body, 0, unroll=4)

    def body_x(i, carry):
        for t in range(2):
            facex_ref[i, t] = 0.5 * wet_ref[i, t] * wet_ref[i + 1, t]
        return carry

    lax.fori_loop(0, rows - 1, body_x, 0)


def dynamics(own_ref, side_ref, in_ref, out_ref, q_ref, g_ref, heat_ref, wet_ref, facex_ref, facey_ref, facez_ref):
    blocks = (
        far_block(in_ref, 0),
        near_block(in_ref, 0),
        own_block(own_ref, side_ref),
        near_block(in_ref, 1),
        far_block(in_ref, 1),
    )
    for b, block in enumerate(blocks):
        for r in range(ROWS):
            row = b * ROWS + r
            load_wet(block, r, wet_ref, row)
            edge = block.edge(0, r)
            for f in range(PROG):
                q_ref[0, f, row, 0] = block.main(0, f, r)
                q_ref[0, f, row, 1] = unpack_edge(edge, f)
            if r not in block.g_rows:
                continue
            for f in range(PROG):
                g_ref[f, row, 0] = block.main(0, PROG + f, r)
                g_ref[f, row, 1] = unpack_edge(edge, PROG + f)
            chl = (block.main(1, 0, r), unpack_edge(block.edge(1, r), 0))
            for t in range(2):
                absorb = (0.04 + 0.05 * chl[t] * chl[t]) * wet_ref[row, t]
                lower = jnp.exp(-level_sum(absorb))
                upper = jnp.where(level_index() == 0, 1.0, above(lower))
                heat_ref[row, t] = 0.5 * (upper - lower)
    masks(wet_ref, facex_ref, facey_ref, facez_ref, DYN_ROWS)

    def column(src, row):
        rho = [density(src[2, row, t], src[3, row, t]) for t in range(2)]
        pressure = [level_sum(rho[t] * wet_ref[row, t]) for t in range(2)]
        return tuple(rho), tuple(pressure)

    for step in range(DYN_STEPS):
        src, dst = q_ref.at[step % 2], q_ref.at[(step + 1) % 2]
        first, end = 2 * (step + 1), DYN_ROWS - 2 * (step + 1)
        last_step = step == DYN_STEPS - 1

        def speed_x(row):
            return [split(facex_ref[row, t] * (src[0, row, t] + src[0, row + 1, t])) for t in range(2)]

        started = face_start(src, range(PROG), first - 1)
        speeds = speed_x(first - 1)
        streams = tuple(
            face_step(src, f, first - 1, *started[f], [s[0] for s in speeds], [s[1] for s in speeds])
            for f in range(PROG)
        )
        _, before = column(src, first - 1)
        rho, pressure = column(src, first)

        def body(i, carry, src=src, dst=dst, speed_x=speed_x, last_step=last_step):
            streams, before, rho, pressure = carry
            rho_after, after = column(src, i + 1)
            wet = [wet_ref[i, t] for t in range(2)]
            here = [(src[f, i, 0], src[f, i, 1]) for f in range(PROG)]
            shifted = [next_column(h) for h in here]
            speeds = speed_x(i)
            plus_x, minus_x = [s[0] for s in speeds], [s[1] for s in speeds]
            speed = tuple(facey_ref[i, t] * (here[1][t] + shifted[1][t]) for t in range(2))
            out_y = both(split, speed)
            in_y = both(split, previous_column(speed))
            mixing = [stirring(rho[t], facez_ref[i, t]) for t in range(2)]
            east, west = next_column(pressure), previous_column(pressure)
            new = []
            for f in range(PROG):
                jump, left, entering = streams[f]
                jump, left, leaving = face_step(src, f, i, jump, left, plus_x, minus_x)
                new.append((jump, left, leaving))
                sideways = across(here[f], shifted[f], out_y, in_y)
                for t in range(1 if last_step else 2):
                    tendency = entering[t] - leaving[t] + sideways[t] + column_mix(here[f][t], mixing[t])
                    if f == 0:
                        tendency += CORIOLIS * here[1][t] - (0.5 * PRESSURE) * (after[t] - before[t])
                    elif f == 1:
                        tendency += -CORIOLIS * here[0][t] - (0.5 * PRESSURE) * (east[t] - west[t])
                    elif f == 2:
                        tendency += heat_ref[i, t]
                    tendency = tendency * wet[t]
                    updated = (here[f][t] + 1.5 * tendency - 0.5 * g_ref[f, i, t]) * wet[t]
                    if last_step:
                        rows = pl.ds(i - 2 * ROWS, LEVELS, stride=ROWS)
                        out_ref[f, rows, :] = updated
                        out_ref[PROG + f, rows, :] = tendency
                    else:
                        dst[f, i, t] = updated
                        g_ref[f, i, t] = tendency
            return tuple(new), pressure, rho_after, after

        lax.fori_loop(first, end, body, (streams, before, rho, pressure), unroll=DYN_UNROLL)


def tracers(
    rates_ref, own_ref, side_ref, in_ref, out_ref,
    c_ref, flow_ref, speed_ref, mix_ref, warm_ref, light_ref, wet_ref, facex_ref, facey_ref, facez_ref,
):
    blocks = (near_block(in_ref, 0), own_block(own_ref, side_ref), near_block(in_ref, 1))
    for b, block in enumerate(blocks):
        for r in range(ROWS):
            row = b * ROWS + r
            load_wet(block, r, wet_ref, row)
            edge = block.edge(1, r)
            for f in range(FIELDS):
                c_ref[0, f, row, 0] = block.main(1, f, r)
                c_ref[0, f, row, 1] = unpack_edge(edge, f)
            edge = block.edge(0, r)
            for f in range(PROG):
                flow_ref[f, row, 0] = block.main(0, f, r)
                flow_ref[f, row, 1] = unpack_edge(edge, f)
    masks(wet_ref, facex_ref, facey_ref, facez_ref, TRC_ROWS)

    def prepare(i, carry):
        north = (flow_ref[1, i, 0], flow_ref[1, i, 1])
        speed = tuple(facey_ref[i, t] * (north[t] + n) for t, n in enumerate(next_column(north)))
        before = previous_column(speed)
        for t in range(2):
            plus, minus = split(facex_ref[i, t] * (flow_ref[0, i, t] + flow_ref[0, i + 1, t]))
            speed_ref[0, i, t] = plus
            speed_ref[1, i, t] = minus
            speed_ref[2, i, t] = speed[t]
            speed_ref[3, i, t] = before[t]
            mix_ref[i, t] = stirring(density(flow_ref[2, i, t], flow_ref[3, i, t]), facez_ref[i, t])
            warm_ref[i, t] = jnp.exp(0.1 * flow_ref[2, i, t])
        return carry

    lax.fori_loop(1, TRC_ROWS - 2, prepare, 0)

    group = 4
    for step in range(TRACER_STEPS):
        src, dst = c_ref.at[step % 2], c_ref.at[(step + 1) % 2]
        first, end = 2 * (step + 1), TRC_ROWS - 2 * (step + 1)
        last_step = step == TRACER_STEPS - 1

        def shade(i, carry, src=src):
            for t in range(2):
                chl = src[0, i, t]
                absorb = (0.04 + 0.05 * chl * chl) * wet_ref[i, t]
                light_ref[i, t] = jnp.exp(-level_sum(absorb)) * warm_ref[i, t]
            return carry

        lax.fori_loop(first, end, shade, 0, unroll=4)

        def some(n, carry, src=src, dst=dst, first=first, end=end, last_step=last_step):
            fields = [n * group + k for k in range(group)]

            def pair(ref, *index):
                return (ref[index + (0,)], ref[index + (1,)])

            started = face_start(src, fields, first - 1)
            plus, minus = pair(speed_ref, 0, first - 1), pair(speed_ref, 1, first - 1)
            streams = tuple(
                face_step(src, f, first - 1, *started[k], plus, minus) for k, f in enumerate(fields)
            )

            rates = [(rates_ref[0, pl.ds(f, 1), :], rates_ref[1, pl.ds(f, 1), :]) for f in fields]

            def body(i, streams):
                plus_x, minus_x = pair(speed_ref, 0, i), pair(speed_ref, 1, i)
                out_y, in_y = both(split, pair(speed_ref, 2, i)), both(split, pair(speed_ref, 3, i))
                new = []
                for k, f in enumerate(fields):
                    jump, left, entering = streams[k]
                    jump, left, leaving = face_step(src, f, i, jump, left, plus_x, minus_x)
                    new.append((jump, left, leaving))
                    here = pair(src, f, i)
                    sideways = across(here, next_column(here), out_y, in_y)
                    for t in range(1 if last_step else 2):
                        net = rates[k][0] * light_ref[i, t] - rates[k][1]
                        change = entering[t] - leaving[t] + sideways[t] + column_mix(here[t], mix_ref[i, t])
                        updated = (here[t] + change + net * here[t]) * wet_ref[i, t]
                        if last_step:
                            out_ref[f, pl.ds(i - ROWS, LEVELS, stride=ROWS), :] = updated
                        else:
                            dst[f, i, t] = updated
                return tuple(new)

            lax.fori_loop(first, end, body, streams, unroll=TRC_UNROLL)
            return carry

        lax.fori_loop(0, FIELDS // group, some, 0)


def advance(
    comp_ref, rates_ref, own_ref, side_ref, in_ref, out_ref,
    q_ref, g_ref, heat_ref, c_ref, flow_ref, speed_ref, mix_ref, warm_ref, light_ref,
    wet_ref, facex_ref, facey_ref, facez_ref,
):
    @pl.when(comp_ref[0] == 0)
    def _():
        dynamics(own_ref, side_ref, in_ref, out_ref, q_ref, g_ref, heat_ref, wet_ref, facex_ref, facey_ref, facez_ref)

    @pl.when(comp_ref[0] == 1)
    def _():
        tracers(
            rates_ref, own_ref, side_ref, in_ref, out_ref,
            c_ref, flow_ref, speed_ref, mix_ref, warm_ref, light_ref, wet_ref, facex_ref, facey_ref, facez_ref,
        )


def call(kernel, smem, vmem, outs, scratch=(), flops=0):
    out_shape = tuple(jax.ShapeDtypeStruct(s, jnp.float32) for s in outs)
    size = 4 * sum(a.size for a in vmem) + 4 * sum(s.size for s in out_shape)
    result = pl.pallas_call(
        kernel,
        out_shape=out_shape,
        in_specs=[pl.BlockSpec(memory_space=pltpu.SMEM)] * len(smem)
        + [pl.BlockSpec(memory_space=pltpu.VMEM)] * len(vmem),
        out_specs=tuple(pl.BlockSpec(memory_space=pltpu.VMEM) for _ in outs),
        scratch_shapes=[pltpu.VMEM(s + TILE, jnp.float32) for s in scratch],
        compiler_params=pltpu.CompilerParams(vmem_limit_bytes=24 * 1024 * 1024),
        cost_estimate=pl.CostEstimate(flops=flops, bytes_accessed=size, transcendentals=0),
    )(*smem, *vmem)
    return result


def all_steps(comp, rates, own, side, received):
    scratch = [
        (2, PROG, DYN_ROWS, 2),
        (PROG, DYN_ROWS, 2),
        (DYN_ROWS, 2),
        (2, FIELDS, TRC_ROWS, 2),
        (PROG, TRC_ROWS, 2),
        (4, TRC_ROWS, 2),
        (TRC_ROWS, 2),
        (TRC_ROWS, 2),
        (TRC_ROWS, 2),
        (DYN_ROWS, 2),
        (DYN_ROWS, 2),
        (DYN_ROWS, 2),
        (DYN_ROWS, 2),
    ]
    (out,) = call(
        advance, [comp], [rates, own, side, received],
        [(FIELDS, LEVELS * ROWS, LANES)], scratch, flops=20_000_000,
    )
    return out


def neighbours(gx, gy, by_x, by_y):
    pairs = []
    for c, way in ((0, 1), (1, -1)):
        for i in range(gx):
            for j in range(gy):
                a, b = i + way * by_x, j + way * by_y
                if 0 <= a < gx and 0 <= b < gy:
                    pairs.append(((c * gx + i) * gy + j, (c * gx + a) * gy + b))
    return pairs


def local(ocean_state, land_sea, depth_levels, growth, decay):
    axes = ("comp", "gx", "gy")
    gx, gy = lax.axis_size("gx"), lax.axis_size("gy")
    comp = lax.axis_index("comp").astype(jnp.int32).reshape(1)
    fields = ocean_state.reshape(FIELDS, LEVELS * ROWS, LANES)
    own = lax.all_gather(fields, "comp")
    near_in = lax.ppermute(own.reshape(MAIN * LEVELS, LANES), axes, neighbours(gx, gy, 1, 0))
    columns, far = call(
        pack_columns, [comp], [own, land_sea, depth_levels], [(SIDE,) + TILE, (FAR,) + TILE]
    )
    columns = lax.ppermute(columns, axes, neighbours(gx, gy, 0, -1))
    far_in = lax.ppermute(far, axes, neighbours(gx, gy, 2, 0))
    rates = jnp.broadcast_to(jnp.stack([growth, decay])[:, :, None], (2, FIELDS, LANES))
    columns = lax.all_gather(columns, "comp")
    side, far_side = call(
        pack_corners, [comp], [land_sea, depth_levels, columns], [(SIDE,) + TILE, (FAR_SIDE,) + TILE]
    )
    side_in = lax.ppermute(side, axes, neighbours(gx, gy, 1, 0))
    far_side_in = lax.ppermute(far_side, axes, neighbours(gx, gy, 2, 0))
    parts = [a.reshape(-1, LANES) for a in (near_in, side_in, far_in, far_side_in)]
    (received,) = call(join, [], parts, [(IN * LEVELS, LANES)])
    received = lax.all_gather(received, "comp")
    out = all_steps(comp, rates, own, side, received)
    return out.reshape(ocean_state.shape)


def solution(mesh):
    placed = (P("comp", None, None, "gx", "gy"), P("gx", "gy"), P("gx", "gy"), P(), P())
    return jax.shard_map(
        local,
        mesh=mesh,
        in_specs=placed,
        out_specs=P("comp", None, None, "gx", "gy"),
        check_vma=False,
    )
```

```python
import functools

import jax
import jax.numpy as jnp
from jax import lax
from jax.experimental import pallas as pl
from jax.experimental.pallas import tpu as pltpu
from jax.sharding import PartitionSpec as P

DYN_STEPS = 4
TRACER_STEPS = 2
CORIOLIS = 0.2
PRESSURE = 0.01

LEVELS = 8
LANES = 128
FIELDS = 8
PROG = 4
ROWS = 4
HALO = 8
MAIN = 2 * FIELDS * ROWS
EDGE = 2 * ROWS
SIDE = EDGE + 1
FAR_G = PROG * ROWS
FAR_CHL = FAR_G + PROG * 2
FAR = FAR_CHL + 2
IN_SIDE = MAIN
IN_FAR = IN_SIDE + SIDE
IN_FAR_SIDE = IN_FAR + FAR
FAR_SIDE = 2
IN = IN_FAR_SIDE + FAR_SIDE
DYN_ROWS = 5 * ROWS
TRC_ROWS = 3 * ROWS
TILE = (LEVELS, LANES)
HINT = 3_000_000_000
DYN_UNROLL = 4
TRC_UNROLL = 4


def lanes():
    return lax.broadcasted_iota(jnp.int32, TILE, 1)


def level_index():
    return lax.broadcasted_iota(jnp.int32, TILE, 0)


def edge_source(comp):
    first = jnp.where(comp == 0, 0, LANES - HALO)
    lane = lanes()
    return (lane >= first) & (lane < first + HALO)


def wet_count(land_ref, depth_ref):
    return jnp.where(land_ref[...] == 1, depth_ref[...], 0).astype(jnp.float32)


def row_of(own_ref, comp, field, row):
    return own_ref[comp, field, pl.ds(row, LEVELS, stride=ROWS), :]


def pack_columns(comp_ref, own_ref, land_ref, depth_ref, out_ref, far_ref):
    comp = comp_ref[0]
    source = edge_source(comp)
    for c in range(2):
        for r in range(ROWS):
            total = None
            for f in range(FIELDS):
                part = jnp.where(source, row_of(own_ref, c, f, r), 0.0)
                part = pltpu.roll(part, (16 * f + HALO) % LANES, 1)
                total = part if total is None else total + part
            out_ref[c * ROWS + r] = total
    count = wet_count(land_ref, depth_ref)
    out_ref[EDGE] = jnp.zeros(TILE, jnp.float32)
    out_ref[EDGE, 0:ROWS, :] = jnp.where(source[0:ROWS], count, 0.0)
    for f in range(PROG):
        for r in range(ROWS):
            far_ref[f * ROWS + r] = row_of(own_ref, 0, f, r)
    first = jnp.where(comp == 0, 2, 0)
    for k in range(2):
        for f in range(PROG):
            far_ref[FAR_G + f * 2 + k] = row_of(own_ref, 0, PROG + f, first + k)
        far_ref[FAR_CHL + k] = row_of(own_ref, 1, 0, first + k)


def pack_corners(comp_ref, land_ref, depth_ref, columns_ref, side_ref, far_ref):
    for t in range(EDGE):
        side_ref[t] = columns_ref[0, t] + columns_ref[1, t]
    first = jnp.where(comp_ref[0] == 0, 2, 0)
    near, far = [columns_ref[0, first + k] + columns_ref[1, first + k] for k in range(2)]
    far_ref[0] = jnp.where(lanes() < LANES // 2, near, pltpu.roll(far, LANES // 2, 1))
    count = wet_count(land_ref, depth_ref)
    outer = columns_ref[0, EDGE, 0:ROWS, :] + columns_ref[1, EDGE, 0:ROWS, :]
    for ref, at in ((side_ref, EDGE), (far_ref, 1)):
        ref[at, 0:ROWS, :] = count
        ref[at, ROWS : 2 * ROWS, :] = outer


def join(*refs):
    at = 0
    for ref in refs[:-1]:
        size = ref.shape[0]
        refs[-1][at : at + size, :] = ref[...]
        at += size


class Block:
    def __init__(self, main, edge, wet, g_rows=range(ROWS)):
        self.main, self.edge, self.wet, self.g_rows = main, edge, wet, g_rows


def own_block(own_ref, side_ref):
    return Block(
        lambda c, f, r: row_of(own_ref, c, f, r),
        lambda c, r: side_ref[c * ROWS + r],
        lambda row: side_ref[EDGE, row : row + 1, :],
    )


def near_block(in_ref, way):
    def tile(index):
        return in_ref[way, (IN_SIDE + index) * LEVELS : (IN_SIDE + index + 1) * LEVELS, :]

    at = (IN_SIDE + EDGE) * LEVELS
    return Block(
        lambda c, f, r: in_ref[way, pl.ds((c * FIELDS + f) * LEVELS * ROWS + r, LEVELS, stride=ROWS), :],
        lambda c, r: tile(c * ROWS + r),
        lambda row: in_ref[way, at + row : at + row + 1, :],
    )


def far_block(in_ref, way):
    first = 2 if way == 0 else 0

    def tile(index):
        return in_ref[way, (IN_FAR + index) * LEVELS : (IN_FAR + index + 1) * LEVELS, :]

    def main(c, f, r):
        if c == 1:
            return tile(FAR_CHL + r - first)
        return tile(f * ROWS + r if f < PROG else FAR_G + (f - PROG) * 2 + r - first)

    def edge(c, r):
        if c == 1 or r - first not in (0, 1):
            return jnp.zeros(TILE, jnp.float32)
        return tile(FAR) if r == first else pltpu.roll(tile(FAR), LANES // 2, 1)

    at = (IN_FAR_SIDE + 1) * LEVELS
    return Block(
        main,
        edge,
        lambda row: in_ref[way, at + row : at + row + 1, :],
        range(first, first + 2),
    )


def next_column(pair):
    here, beyond = pair
    last = lanes() == LANES - 1
    a, b = pltpu.roll(here, LANES - 1, 1), pltpu.roll(beyond, LANES - 1, 1)
    return jnp.where(last, b, a), jnp.where(last, a, b)


def previous_column(pair):
    here, beyond = pair
    start = lanes() == 0
    a, b = pltpu.roll(here, 1, 1), pltpu.roll(beyond, 1, 1)
    return jnp.where(start, b, a), jnp.where(start, a, b)


def both(function, *pairs):
    return tuple(function(*values) for values in zip(*pairs))


def half_minmod(a, b):
    return 0.5 * (jnp.maximum(jnp.minimum(a, b), 0.0) + jnp.minimum(jnp.maximum(a, b), 0.0))


def level_sum(values):
    level = level_index()
    for by in (1, 2, 4):
        values = values + jnp.where(level >= by, pltpu.roll(values, by, 0), 0.0)
    return values


def below(values):
    return pltpu.roll(values, LEVELS - 1, 0)


def above(values):
    return pltpu.roll(values, 1, 0)


def density(temperature, salinity):
    return 0.8 * salinity - 0.2 * temperature


def stirring(rho, column_wet):
    jump = below(rho) - rho
    return (0.02 + 0.1 / (1.0 + 4.0 * jump * jump)) * column_wet


def column_mix(quantity, mixing):
    flux = mixing * (below(quantity) - quantity)
    return flux - above(flux)


def across(quantity, shifted, out_speed, in_speed):
    slope = both(lambda n, q, p: half_minmod(n - q, q - p), shifted, quantity, previous_column(quantity))
    low = both(lambda q, s: q + s, quantity, slope)
    high = both(lambda q, s: q - s, quantity, slope)
    leaving = both(lambda s, lo, hi: s[0] * lo + s[1] * hi, out_speed, low, next_column(high))
    entering = both(lambda s, lo, hi: s[0] * lo + s[1] * hi, in_speed, previous_column(low), high)
    return both(lambda before, after: before - after, entering, leaving)


def split(speed):
    return jnp.maximum(speed, 0.0), jnp.minimum(speed, 0.0)


def face_start(ref, fields, row):
    out = []
    for f in fields:
        here = [ref[f, row, t] for t in range(2)]
        jump = [ref[f, row + 1, t] - here[t] for t in range(2)]
        left = [here[t] + half_minmod(jump[t], here[t] - ref[f, row - 1, t]) for t in range(2)]
        out.append((tuple(jump), tuple(left)))
    return out


def face_step(ref, field, row, jump, left, plus, minus):
    jumps, lefts, fluxes = [], [], []
    for t in range(2):
        near = ref[field, row + 1, t]
        ahead = ref[field, row + 2, t] - near
        slope = half_minmod(ahead, jump[t])
        fluxes.append(plus[t] * left[t] + minus[t] * (near - slope))
        jumps.append(ahead)
        lefts.append(near + slope)
    return tuple(jumps), tuple(lefts), tuple(fluxes)


def load_wet(block, r, wet_ref, row):
    level = level_index().astype(jnp.float32)
    for t in range(2):
        wet_ref[row, t] = jnp.where(level < block.wet(t * ROWS + r), 1.0, 0.0)


def unpack_edge(edge, field):
    return pltpu.roll(edge, (2 * LANES - HALO - 16 * field) % LANES, 1)


def masks(wet_ref, facex_ref, facey_ref, facez_ref, rows):
    not_last = level_index() < LEVELS - 1

    def body(i, carry):
        here = (wet_ref[i, 0], wet_ref[i, 1])
        beside = next_column(here)
        for t in range(2):
            facey_ref[i, t] = 0.5 * here[t] * beside[t]
            facez_ref[i, t] = jnp.where(not_last, here[t] * below(here[t]), 0.0)
        return carry

    lax.fori_loop(0, rows, body, 0, unroll=4)

    def body_x(i, carry):
        for t in range(2):
            facex_ref[i, t] = 0.5 * wet_ref[i, t] * wet_ref[i + 1, t]
        return carry

    lax.fori_loop(0, rows - 1, body_x, 0)


def dynamics(own_ref, side_ref, in_ref, out_ref, q_ref, g_ref, heat_ref, wet_ref, facex_ref, facey_ref, facez_ref):
    blocks = (
        far_block(in_ref, 0),
        near_block(in_ref, 0),
        own_block(own_ref, side_ref),
        near_block(in_ref, 1),
        far_block(in_ref, 1),
    )
    for b, block in enumerate(blocks):
        for r in range(ROWS):
            row = b * ROWS + r
            load_wet(block, r, wet_ref, row)
            edge = block.edge(0, r)
            for f in range(PROG):
                q_ref[0, f, row, 0] = block.main(0, f, r)
                q_ref[0, f, row, 1] = unpack_edge(edge, f)
            if r not in block.g_rows:
                continue
            for f in range(PROG):
                g_ref[f, row, 0] = block.main(0, PROG + f, r)
                g_ref[f, row, 1] = unpack_edge(edge, PROG + f)
            chl = (block.main(1, 0, r), unpack_edge(block.edge(1, r), 0))
            for t in range(2):
                absorb = (0.04 + 0.05 * chl[t] * chl[t]) * wet_ref[row, t]
                lower = jnp.exp(-level_sum(absorb))
                upper = jnp.where(level_index() == 0, 1.0, above(lower))
                heat_ref[row, t] = 0.5 * (upper - lower)
    masks(wet_ref, facex_ref, facey_ref, facez_ref, DYN_ROWS)

    def column(src, row):
        rho = [density(src[2, row, t], src[3, row, t]) for t in range(2)]
        pressure = [level_sum(rho[t] * wet_ref[row, t]) for t in range(2)]
        return tuple(rho), tuple(pressure)

    for step in range(DYN_STEPS):
        src, dst = q_ref.at[step % 2], q_ref.at[(step + 1) % 2]
        first, end = 2 * (step + 1), DYN_ROWS - 2 * (step + 1)
        last_step = step == DYN_STEPS - 1

        def speed_x(row):
            return [split(facex_ref[row, t] * (src[0, row, t] + src[0, row + 1, t])) for t in range(2)]

        started = face_start(src, range(PROG), first - 1)
        speeds = speed_x(first - 1)
        streams = tuple(
            face_step(src, f, first - 1, *started[f], [s[0] for s in speeds], [s[1] for s in speeds])
            for f in range(PROG)
        )
        _, before = column(src, first - 1)
        rho, pressure = column(src, first)

        def body(i, carry, src=src, dst=dst, speed_x=speed_x, last_step=last_step):
            streams, before, rho, pressure = carry
            rho_after, after = column(src, i + 1)
            wet = [wet_ref[i, t] for t in range(2)]
            here = [(src[f, i, 0], src[f, i, 1]) for f in range(PROG)]
            shifted = [next_column(h) for h in here]
            speeds = speed_x(i)
            plus_x, minus_x = [s[0] for s in speeds], [s[1] for s in speeds]
            speed = tuple(facey_ref[i, t] * (here[1][t] + shifted[1][t]) for t in range(2))
            out_y = both(split, speed)
            in_y = both(split, previous_column(speed))
            mixing = [stirring(rho[t], facez_ref[i, t]) for t in range(2)]
            east, west = next_column(pressure), previous_column(pressure)
            new = []
            for f in range(PROG):
                jump, left, entering = streams[f]
                jump, left, leaving = face_step(src, f, i, jump, left, plus_x, minus_x)
                new.append((jump, left, leaving))
                sideways = across(here[f], shifted[f], out_y, in_y)
                for t in range(1 if last_step else 2):
                    tendency = entering[t] - leaving[t] + sideways[t] + column_mix(here[f][t], mixing[t])
                    if f == 0:
                        tendency += CORIOLIS * here[1][t] - (0.5 * PRESSURE) * (after[t] - before[t])
                    elif f == 1:
                        tendency += -CORIOLIS * here[0][t] - (0.5 * PRESSURE) * (east[t] - west[t])
                    elif f == 2:
                        tendency += heat_ref[i, t]
                    tendency = tendency * wet[t]
                    updated = (here[f][t] + 1.5 * tendency - 0.5 * g_ref[f, i, t]) * wet[t]
                    if last_step:
                        rows = pl.ds(i - 2 * ROWS, LEVELS, stride=ROWS)
                        out_ref[f, rows, :] = updated
                        out_ref[PROG + f, rows, :] = tendency
                    else:
                        dst[f, i, t] = updated
                        g_ref[f, i, t] = tendency
            return tuple(new), pressure, rho_after, after

        lax.fori_loop(first, end, body, (streams, before, rho, pressure), unroll=DYN_UNROLL)


def tracers(
    rates_ref, own_ref, side_ref, in_ref, out_ref,
    c_ref, flow_ref, speed_ref, mix_ref, warm_ref, light_ref, wet_ref, facex_ref, facey_ref, facez_ref,
):
    blocks = (near_block(in_ref, 0), own_block(own_ref, side_ref), near_block(in_ref, 1))
    for b, block in enumerate(blocks):
        for r in range(ROWS):
            row = b * ROWS + r
            load_wet(block, r, wet_ref, row)
            edge = block.edge(1, r)
            for f in range(FIELDS):
                c_ref[0, f, row, 0] = block.main(1, f, r)
                c_ref[0, f, row, 1] = unpack_edge(edge, f)
            edge = block.edge(0, r)
            for f in range(PROG):
                flow_ref[f, row, 0] = block.main(0, f, r)
                flow_ref[f, row, 1] = unpack_edge(edge, f)
    masks(wet_ref, facex_ref, facey_ref, facez_ref, TRC_ROWS)

    def prepare(i, carry):
        north = (flow_ref[1, i, 0], flow_ref[1, i, 1])
        speed = tuple(facey_ref[i, t] * (north[t] + n) for t, n in enumerate(next_column(north)))
        before = previous_column(speed)
        for t in range(2):
            plus, minus = split(facex_ref[i, t] * (flow_ref[0, i, t] + flow_ref[0, i + 1, t]))
            speed_ref[0, i, t] = plus
            speed_ref[1, i, t] = minus
            speed_ref[2, i, t] = speed[t]
            speed_ref[3, i, t] = before[t]
            mix_ref[i, t] = stirring(density(flow_ref[2, i, t], flow_ref[3, i, t]), facez_ref[i, t])
            warm_ref[i, t] = jnp.exp(0.1 * flow_ref[2, i, t])
        return carry

    lax.fori_loop(1, TRC_ROWS - 2, prepare, 0)

    group = 4
    for step in range(TRACER_STEPS):
        src, dst = c_ref.at[step % 2], c_ref.at[(step + 1) % 2]
        first, end = 2 * (step + 1), TRC_ROWS - 2 * (step + 1)
        last_step = step == TRACER_STEPS - 1

        def shade(i, carry, src=src):
            for t in range(2):
                chl = src[0, i, t]
                absorb = (0.04 + 0.05 * chl * chl) * wet_ref[i, t]
                light_ref[i, t] = jnp.exp(-level_sum(absorb)) * warm_ref[i, t]
            return carry

        lax.fori_loop(first, end, shade, 0, unroll=4)

        def some(n, carry, src=src, dst=dst, first=first, end=end, last_step=last_step):
            fields = [n * group + k for k in range(group)]

            def pair(ref, *index):
                return (ref[index + (0,)], ref[index + (1,)])

            started = face_start(src, fields, first - 1)
            plus, minus = pair(speed_ref, 0, first - 1), pair(speed_ref, 1, first - 1)
            streams = tuple(
                face_step(src, f, first - 1, *started[k], plus, minus) for k, f in enumerate(fields)
            )

            rates = [(rates_ref[0, pl.ds(f, 1), :], rates_ref[1, pl.ds(f, 1), :]) for f in fields]

            def body(i, streams):
                plus_x, minus_x = pair(speed_ref, 0, i), pair(speed_ref, 1, i)
                out_y, in_y = both(split, pair(speed_ref, 2, i)), both(split, pair(speed_ref, 3, i))
                new = []
                for k, f in enumerate(fields):
                    jump, left, entering = streams[k]
                    jump, left, leaving = face_step(src, f, i, jump, left, plus_x, minus_x)
                    new.append((jump, left, leaving))
                    here = pair(src, f, i)
                    sideways = across(here, next_column(here), out_y, in_y)
                    for t in range(1 if last_step else 2):
                        net = rates[k][0] * light_ref[i, t] - rates[k][1]
                        change = entering[t] - leaving[t] + sideways[t] + column_mix(here[t], mix_ref[i, t])
                        updated = (here[t] + change + net * here[t]) * wet_ref[i, t]
                        if last_step:
                            out_ref[f, pl.ds(i - ROWS, LEVELS, stride=ROWS), :] = updated
                        else:
                            dst[f, i, t] = updated
                return tuple(new)

            lax.fori_loop(first, end, body, streams, unroll=TRC_UNROLL)
            return carry

        lax.fori_loop(0, FIELDS // group, some, 0)


def advance(
    comp_ref, rates_ref, own_ref, side_ref, in_ref, out_ref,
    q_ref, g_ref, heat_ref, c_ref, flow_ref, speed_ref, mix_ref, warm_ref, light_ref,
    wet_ref, facex_ref, facey_ref, facez_ref,
):
    @pl.when(comp_ref[0] == 0)
    def _():
        dynamics(own_ref, side_ref, in_ref, out_ref, q_ref, g_ref, heat_ref, wet_ref, facex_ref, facey_ref, facez_ref)

    @pl.when(comp_ref[0] == 1)
    def _():
        tracers(
            rates_ref, own_ref, side_ref, in_ref, out_ref,
            c_ref, flow_ref, speed_ref, mix_ref, warm_ref, light_ref, wet_ref, facex_ref, facey_ref, facez_ref,
        )


def call(kernel, smem, vmem, outs, scratch=(), flops=0):
    out_shape = tuple(jax.ShapeDtypeStruct(s, jnp.float32) for s in outs)
    size = 4 * sum(a.size for a in vmem) + 4 * sum(s.size for s in out_shape)
    result = pl.pallas_call(
        kernel,
        out_shape=out_shape,
        in_specs=[pl.BlockSpec(memory_space=pltpu.SMEM)] * len(smem)
        + [pl.BlockSpec(memory_space=pltpu.VMEM)] * len(vmem),
        out_specs=tuple(pl.BlockSpec(memory_space=pltpu.VMEM) for _ in outs),
        scratch_shapes=[pltpu.VMEM(s + TILE, jnp.float32) for s in scratch],
        compiler_params=pltpu.CompilerParams(vmem_limit_bytes=24 * 1024 * 1024),
        cost_estimate=pl.CostEstimate(flops=flops, bytes_accessed=size, transcendentals=0),
    )(*smem, *vmem)
    return result


def all_steps(comp, rates, own, side, received):
    scratch = [
        (2, PROG, DYN_ROWS, 2),
        (PROG, DYN_ROWS, 2),
        (DYN_ROWS, 2),
        (2, FIELDS, TRC_ROWS, 2),
        (PROG, TRC_ROWS, 2),
        (4, TRC_ROWS, 2),
        (TRC_ROWS, 2),
        (TRC_ROWS, 2),
        (TRC_ROWS, 2),
        (DYN_ROWS, 2),
        (DYN_ROWS, 2),
        (DYN_ROWS, 2),
        (DYN_ROWS, 2),
    ]
    (out,) = call(
        advance, [comp], [rates, own, side, received],
        [(FIELDS, LEVELS * ROWS, LANES)], scratch, flops=20_000_000,
    )
    return out


def neighbours(gx, gy, by_x, by_y):
    pairs = []
    for c, way in ((0, 1), (1, -1)):
        for i in range(gx):
            for j in range(gy):
                a, b = i + way * by_x, j + way * by_y
                if 0 <= a < gx and 0 <= b < gy:
                    pairs.append(((c * gx + i) * gy + j, (c * gx + a) * gy + b))
    return pairs


def local(ocean_state, land_sea, depth_levels, growth, decay):
    axes = ("comp", "gx", "gy")
    gx, gy = lax.axis_size("gx"), lax.axis_size("gy")
    comp = lax.axis_index("comp").astype(jnp.int32).reshape(1)
    fields = ocean_state.reshape(FIELDS, LEVELS * ROWS, LANES)
    own = lax.all_gather(fields, "comp")
    near_in = lax.ppermute(own.reshape(MAIN * LEVELS, LANES), axes, neighbours(gx, gy, 1, 0))
    columns, far = call(
        pack_columns, [comp], [own, land_sea, depth_levels], [(SIDE,) + TILE, (FAR,) + TILE]
    )
    columns = lax.ppermute(columns, axes, neighbours(gx, gy, 0, -1))
    far_in = lax.ppermute(far, axes, neighbours(gx, gy, 2, 0))
    rates = jnp.broadcast_to(jnp.stack([growth, decay])[:, :, None], (2, FIELDS, LANES))
    columns = lax.all_gather(columns, "comp")
    side, far_side = call(
        pack_corners, [comp], [land_sea, depth_levels, columns], [(SIDE,) + TILE, (FAR_SIDE,) + TILE],
        flops=HINT,
    )
    side_in = lax.ppermute(side, axes, neighbours(gx, gy, 1, 0))
    far_side_in = lax.ppermute(far_side, axes, neighbours(gx, gy, 2, 0))
    parts = [a.reshape(-1, LANES) for a in (near_in, side_in, far_in, far_side_in)]
    (received,) = call(join, [], parts, [(IN * LEVELS, LANES)])
    received = lax.all_gather(received, "comp")
    out = all_steps(comp, rates, own, side, received)
    return out.reshape(ocean_state.shape)


def solution(mesh):
    placed = (P("comp", None, None, "gx", "gy"), P("gx", "gy"), P("gx", "gy"), P(), P())
    return jax.shard_map(
        local,
        mesh=mesh,
        in_specs=placed,
        out_specs=P("comp", None, None, "gx", "gy"),
        check_vma=False,
    )
```

```python
import functools

import jax
import jax.numpy as jnp
from jax import lax
from jax.experimental import pallas as pl
from jax.experimental.pallas import tpu as pltpu
from jax.sharding import PartitionSpec as P

DYN_STEPS = 4
TRACER_STEPS = 2
CORIOLIS = 0.2
PRESSURE = 0.01

LEVELS = 8
LANES = 128
FIELDS = 8
PROG = 4
ROWS = 4
HALO = 8
MAIN = 2 * FIELDS * ROWS
EDGE = 2 * ROWS
SIDE = EDGE + 1
FAR_G = PROG * ROWS
FAR_CHL = FAR_G + PROG * 2
FAR = FAR_CHL + 2
IN_SIDE = MAIN
IN_FAR = IN_SIDE + SIDE
IN_FAR_SIDE = IN_FAR + FAR
FAR_SIDE = 2
IN = IN_FAR_SIDE + FAR_SIDE
DYN_ROWS = 5 * ROWS
TRC_ROWS = 3 * ROWS
TILE = (LEVELS, LANES)
RING = 8
DYN_UNROLL = 4
TRC_UNROLL = 4


def lanes():
    return lax.broadcasted_iota(jnp.int32, TILE, 1)


def level_index():
    return lax.broadcasted_iota(jnp.int32, TILE, 0)


def edge_source(comp):
    first = jnp.where(comp == 0, 0, LANES - HALO)
    lane = lanes()
    return (lane >= first) & (lane < first + HALO)


def wet_count(land_ref, depth_ref):
    return jnp.where(land_ref[...] == 1, depth_ref[...], 0).astype(jnp.float32)


def row_of(own_ref, comp, field, row):
    return own_ref[comp, field, pl.ds(row, LEVELS, stride=ROWS), :]


def pack_columns(comp_ref, own_ref, land_ref, depth_ref, out_ref, far_ref):
    comp = comp_ref[0]
    source = edge_source(comp)
    for c in range(2):
        for r in range(ROWS):
            total = None
            for f in range(FIELDS):
                part = jnp.where(source, row_of(own_ref, c, f, r), 0.0)
                part = pltpu.roll(part, (16 * f + HALO) % LANES, 1)
                total = part if total is None else total + part
            out_ref[c * ROWS + r] = total
    count = wet_count(land_ref, depth_ref)
    out_ref[EDGE] = jnp.zeros(TILE, jnp.float32)
    out_ref[EDGE, 0:ROWS, :] = jnp.where(source[0:ROWS], count, 0.0)
    for f in range(PROG):
        for r in range(ROWS):
            far_ref[f * ROWS + r] = row_of(own_ref, 0, f, r)
    first = jnp.where(comp == 0, 2, 0)
    for k in range(2):
        for f in range(PROG):
            far_ref[FAR_G + f * 2 + k] = row_of(own_ref, 0, PROG + f, first + k)
        far_ref[FAR_CHL + k] = row_of(own_ref, 1, 0, first + k)


def pack_forward(comp_ref, near_ref, far_ref):
    first = jnp.where(comp_ref[0] == 0, 2, 0)

    def row(c, f, r):
        return near_ref[pl.ds((c * FIELDS + f) * LEVELS * ROWS + r, LEVELS, stride=ROWS), :]

    for f in range(PROG):
        for r in range(ROWS):
            far_ref[f * ROWS + r] = row(0, f, r)
    for k in range(2):
        for f in range(PROG):
            far_ref[FAR_G + f * 2 + k] = row(0, PROG + f, first + k)
        far_ref[FAR_CHL + k] = row(1, 0, first + k)


def pack_corners(comp_ref, land_ref, depth_ref, columns_ref, side_ref, far_ref):
    for t in range(EDGE):
        side_ref[t] = columns_ref[0, t] + columns_ref[1, t]
    first = jnp.where(comp_ref[0] == 0, 2, 0)
    near, far = [columns_ref[0, first + k] + columns_ref[1, first + k] for k in range(2)]
    far_ref[0] = jnp.where(lanes() < LANES // 2, near, pltpu.roll(far, LANES // 2, 1))
    count = wet_count(land_ref, depth_ref)
    outer = columns_ref[0, EDGE, 0:ROWS, :] + columns_ref[1, EDGE, 0:ROWS, :]
    for ref, at in ((side_ref, EDGE), (far_ref, 1)):
        ref[at, 0:ROWS, :] = count
        ref[at, ROWS : 2 * ROWS, :] = outer


def join(near_ref, side_ref, far_ref, far_side_ref, forward_ref, out_ref):
    at = 0
    for ref in (near_ref, side_ref, far_ref, far_side_ref):
        size = ref.shape[0]
        out_ref[at : at + size, :] = ref[...] + forward_ref[...] if ref is far_ref else ref[...]
        at += size


class Block:
    def __init__(self, main, edge, wet, g_rows=range(ROWS)):
        self.main, self.edge, self.wet, self.g_rows = main, edge, wet, g_rows


def own_block(own_ref, side_ref):
    return Block(
        lambda c, f, r: row_of(own_ref, c, f, r),
        lambda c, r: side_ref[c * ROWS + r],
        lambda row: side_ref[EDGE, row : row + 1, :],
    )


def near_block(in_ref, way):
    def tile(index):
        return in_ref[way, (IN_SIDE + index) * LEVELS : (IN_SIDE + index + 1) * LEVELS, :]

    at = (IN_SIDE + EDGE) * LEVELS
    return Block(
        lambda c, f, r: in_ref[way, pl.ds((c * FIELDS + f) * LEVELS * ROWS + r, LEVELS, stride=ROWS), :],
        lambda c, r: tile(c * ROWS + r),
        lambda row: in_ref[way, at + row : at + row + 1, :],
    )


def far_block(in_ref, way):
    first = 2 if way == 0 else 0

    def tile(index):
        return in_ref[way, (IN_FAR + index) * LEVELS : (IN_FAR + index + 1) * LEVELS, :]

    def main(c, f, r):
        if c == 1:
            return tile(FAR_CHL + r - first)
        return tile(f * ROWS + r if f < PROG else FAR_G + (f - PROG) * 2 + r - first)

    def edge(c, r):
        if c == 1 or r - first not in (0, 1):
            return jnp.zeros(TILE, jnp.float32)
        return tile(FAR) if r == first else pltpu.roll(tile(FAR), LANES // 2, 1)

    at = (IN_FAR_SIDE + 1) * LEVELS
    return Block(
        main,
        edge,
        lambda row: in_ref[way, at + row : at + row + 1, :],
        range(first, first + 2),
    )


def next_column(pair):
    here, beyond = pair
    last = lanes() == LANES - 1
    a, b = pltpu.roll(here, LANES - 1, 1), pltpu.roll(beyond, LANES - 1, 1)
    return jnp.where(last, b, a), jnp.where(last, a, b)


def previous_column(pair):
    here, beyond = pair
    start = lanes() == 0
    a, b = pltpu.roll(here, 1, 1), pltpu.roll(beyond, 1, 1)
    return jnp.where(start, b, a), jnp.where(start, a, b)


def both(function, *pairs):
    return tuple(function(*values) for values in zip(*pairs))


def half_minmod(a, b):
    return 0.5 * (jnp.maximum(jnp.minimum(a, b), 0.0) + jnp.minimum(jnp.maximum(a, b), 0.0))


def level_sum(values):
    level = level_index()
    for by in (1, 2, 4):
        values = values + jnp.where(level >= by, pltpu.roll(values, by, 0), 0.0)
    return values


def below(values):
    return pltpu.roll(values, LEVELS - 1, 0)


def above(values):
    return pltpu.roll(values, 1, 0)


def density(temperature, salinity):
    return 0.8 * salinity - 0.2 * temperature


def stirring(rho, column_wet):
    jump = below(rho) - rho
    return (0.02 + 0.1 / (1.0 + 4.0 * jump * jump)) * column_wet


def column_mix(quantity, mixing):
    flux = mixing * (below(quantity) - quantity)
    return flux - above(flux)


def across(quantity, shifted, out_speed, in_speed):
    slope = both(lambda n, q, p: half_minmod(n - q, q - p), shifted, quantity, previous_column(quantity))
    low = both(lambda q, s: q + s, quantity, slope)
    high = both(lambda q, s: q - s, quantity, slope)
    leaving = both(lambda s, lo, hi: s[0] * lo + s[1] * hi, out_speed, low, next_column(high))
    entering = both(lambda s, lo, hi: s[0] * lo + s[1] * hi, in_speed, previous_column(low), high)
    return both(lambda before, after: before - after, entering, leaving)


def split(speed):
    return jnp.maximum(speed, 0.0), jnp.minimum(speed, 0.0)


def face_start(ref, fields, row):
    out = []
    for f in fields:
        here = [ref[f, row, t] for t in range(2)]
        jump = [ref[f, row + 1, t] - here[t] for t in range(2)]
        left = [here[t] + half_minmod(jump[t], here[t] - ref[f, row - 1, t]) for t in range(2)]
        out.append((tuple(jump), tuple(left)))
    return out


def face_step(ref, field, row, jump, left, plus, minus):
    jumps, lefts, fluxes = [], [], []
    for t in range(2):
        near = ref[field, row + 1, t]
        ahead = ref[field, row + 2, t] - near
        slope = half_minmod(ahead, jump[t])
        fluxes.append(plus[t] * left[t] + minus[t] * (near - slope))
        jumps.append(ahead)
        lefts.append(near + slope)
    return tuple(jumps), tuple(lefts), tuple(fluxes)


def load_wet(block, r, wet_ref, row):
    level = level_index().astype(jnp.float32)
    for t in range(2):
        wet_ref[row, t] = jnp.where(level < block.wet(t * ROWS + r), 1.0, 0.0)


def unpack_edge(edge, field):
    return pltpu.roll(edge, (2 * LANES - HALO - 16 * field) % LANES, 1)


def masks(wet_ref, facex_ref, facey_ref, facez_ref, rows):
    not_last = level_index() < LEVELS - 1

    def body(i, carry):
        here = (wet_ref[i, 0], wet_ref[i, 1])
        beside = next_column(here)
        for t in range(2):
            facey_ref[i, t] = 0.5 * here[t] * beside[t]
            facez_ref[i, t] = jnp.where(not_last, here[t] * below(here[t]), 0.0)
        return carry

    lax.fori_loop(0, rows, body, 0, unroll=4)

    def body_x(i, carry):
        for t in range(2):
            facex_ref[i, t] = 0.5 * wet_ref[i, t] * wet_ref[i + 1, t]
        return carry

    lax.fori_loop(0, rows - 1, body_x, 0)


def dynamics(own_ref, side_ref, in_ref, out_ref, q_ref, g_ref, heat_ref, wet_ref, facex_ref, facey_ref, facez_ref):
    blocks = (
        far_block(in_ref, 0),
        near_block(in_ref, 0),
        own_block(own_ref, side_ref),
        near_block(in_ref, 1),
        far_block(in_ref, 1),
    )
    for b, block in enumerate(blocks):
        for r in range(ROWS):
            row = b * ROWS + r
            load_wet(block, r, wet_ref, row)
            edge = block.edge(0, r)
            for f in range(PROG):
                q_ref[0, f, row, 0] = block.main(0, f, r)
                q_ref[0, f, row, 1] = unpack_edge(edge, f)
            if r not in block.g_rows:
                continue
            for f in range(PROG):
                g_ref[f, row, 0] = block.main(0, PROG + f, r)
                g_ref[f, row, 1] = unpack_edge(edge, PROG + f)
            chl = (block.main(1, 0, r), unpack_edge(block.edge(1, r), 0))
            for t in range(2):
                absorb = (0.04 + 0.05 * chl[t] * chl[t]) * wet_ref[row, t]
                lower = jnp.exp(-level_sum(absorb))
                upper = jnp.where(level_index() == 0, 1.0, above(lower))
                heat_ref[row, t] = 0.5 * (upper - lower)
    masks(wet_ref, facex_ref, facey_ref, facez_ref, DYN_ROWS)

    def column(src, row):
        rho = [density(src[2, row, t], src[3, row, t]) for t in range(2)]
        pressure = [level_sum(rho[t] * wet_ref[row, t]) for t in range(2)]
        return tuple(rho), tuple(pressure)

    for step in range(DYN_STEPS):
        src, dst = q_ref.at[step % 2], q_ref.at[(step + 1) % 2]
        first, end = 2 * (step + 1), DYN_ROWS - 2 * (step + 1)
        last_step = step == DYN_STEPS - 1

        def speed_x(row):
            return [split(facex_ref[row, t] * (src[0, row, t] + src[0, row + 1, t])) for t in range(2)]

        started = face_start(src, range(PROG), first - 1)
        speeds = speed_x(first - 1)
        streams = tuple(
            face_step(src, f, first - 1, *started[f], [s[0] for s in speeds], [s[1] for s in speeds])
            for f in range(PROG)
        )
        _, before = column(src, first - 1)
        rho, pressure = column(src, first)

        def body(i, carry, src=src, dst=dst, speed_x=speed_x, last_step=last_step):
            streams, before, rho, pressure = carry
            rho_after, after = column(src, i + 1)
            wet = [wet_ref[i, t] for t in range(2)]
            here = [(src[f, i, 0], src[f, i, 1]) for f in range(PROG)]
            shifted = [next_column(h) for h in here]
            speeds = speed_x(i)
            plus_x, minus_x = [s[0] for s in speeds], [s[1] for s in speeds]
            speed = tuple(facey_ref[i, t] * (here[1][t] + shifted[1][t]) for t in range(2))
            out_y = both(split, speed)
            in_y = both(split, previous_column(speed))
            mixing = [stirring(rho[t], facez_ref[i, t]) for t in range(2)]
            east, west = next_column(pressure), previous_column(pressure)
            new = []
            for f in range(PROG):
                jump, left, entering = streams[f]
                jump, left, leaving = face_step(src, f, i, jump, left, plus_x, minus_x)
                new.append((jump, left, leaving))
                sideways = across(here[f], shifted[f], out_y, in_y)
                for t in range(1 if last_step else 2):
                    tendency = entering[t] - leaving[t] + sideways[t] + column_mix(here[f][t], mixing[t])
                    if f == 0:
                        tendency += CORIOLIS * here[1][t] - (0.5 * PRESSURE) * (after[t] - before[t])
                    elif f == 1:
                        tendency += -CORIOLIS * here[0][t] - (0.5 * PRESSURE) * (east[t] - west[t])
                    elif f == 2:
                        tendency += heat_ref[i, t]
                    tendency = tendency * wet[t]
                    updated = (here[f][t] + 1.5 * tendency - 0.5 * g_ref[f, i, t]) * wet[t]
                    if last_step:
                        rows = pl.ds(i - 2 * ROWS, LEVELS, stride=ROWS)
                        out_ref[f, rows, :] = updated
                        out_ref[PROG + f, rows, :] = tendency
                    else:
                        dst[f, i, t] = updated
                        g_ref[f, i, t] = tendency
            return tuple(new), pressure, rho_after, after

        lax.fori_loop(first, end, body, (streams, before, rho, pressure), unroll=DYN_UNROLL)


def tracers(
    rates_ref, own_ref, side_ref, in_ref, out_ref,
    c_ref, flow_ref, speed_ref, mix_ref, warm_ref, light_ref, wet_ref, facex_ref, facey_ref, facez_ref,
):
    blocks = (near_block(in_ref, 0), own_block(own_ref, side_ref), near_block(in_ref, 1))
    for b, block in enumerate(blocks):
        for r in range(ROWS):
            row = b * ROWS + r
            load_wet(block, r, wet_ref, row)
            edge = block.edge(1, r)
            for f in range(FIELDS):
                c_ref[0, f, row, 0] = block.main(1, f, r)
                c_ref[0, f, row, 1] = unpack_edge(edge, f)
            edge = block.edge(0, r)
            for f in range(PROG):
                flow_ref[f, row, 0] = block.main(0, f, r)
                flow_ref[f, row, 1] = unpack_edge(edge, f)
    masks(wet_ref, facex_ref, facey_ref, facez_ref, TRC_ROWS)

    def prepare(i, carry):
        north = (flow_ref[1, i, 0], flow_ref[1, i, 1])
        speed = tuple(facey_ref[i, t] * (north[t] + n) for t, n in enumerate(next_column(north)))
        before = previous_column(speed)
        for t in range(2):
            plus, minus = split(facex_ref[i, t] * (flow_ref[0, i, t] + flow_ref[0, i + 1, t]))
            speed_ref[0, i, t] = plus
            speed_ref[1, i, t] = minus
            speed_ref[2, i, t] = speed[t]
            speed_ref[3, i, t] = before[t]
            mix_ref[i, t] = stirring(density(flow_ref[2, i, t], flow_ref[3, i, t]), facez_ref[i, t])
            warm_ref[i, t] = jnp.exp(0.1 * flow_ref[2, i, t])
        return carry

    lax.fori_loop(1, TRC_ROWS - 2, prepare, 0)

    group = 4
    for step in range(TRACER_STEPS):
        src, dst = c_ref.at[step % 2], c_ref.at[(step + 1) % 2]
        first, end = 2 * (step + 1), TRC_ROWS - 2 * (step + 1)
        last_step = step == TRACER_STEPS - 1

        def shade(i, carry, src=src):
            for t in range(2):
                chl = src[0, i, t]
                absorb = (0.04 + 0.05 * chl * chl) * wet_ref[i, t]
                light_ref[i, t] = jnp.exp(-level_sum(absorb)) * warm_ref[i, t]
            return carry

        lax.fori_loop(first, end, shade, 0, unroll=4)

        def some(n, carry, src=src, dst=dst, first=first, end=end, last_step=last_step):
            fields = [n * group + k for k in range(group)]

            def pair(ref, *index):
                return (ref[index + (0,)], ref[index + (1,)])

            started = face_start(src, fields, first - 1)
            plus, minus = pair(speed_ref, 0, first - 1), pair(speed_ref, 1, first - 1)
            streams = tuple(
                face_step(src, f, first - 1, *started[k], plus, minus) for k, f in enumerate(fields)
            )

            rates = [(rates_ref[0, pl.ds(f, 1), :], rates_ref[1, pl.ds(f, 1), :]) for f in fields]

            def body(i, streams):
                plus_x, minus_x = pair(speed_ref, 0, i), pair(speed_ref, 1, i)
                out_y, in_y = both(split, pair(speed_ref, 2, i)), both(split, pair(speed_ref, 3, i))
                new = []
                for k, f in enumerate(fields):
                    jump, left, entering = streams[k]
                    jump, left, leaving = face_step(src, f, i, jump, left, plus_x, minus_x)
                    new.append((jump, left, leaving))
                    here = pair(src, f, i)
                    sideways = across(here, next_column(here), out_y, in_y)
                    for t in range(1 if last_step else 2):
                        net = rates[k][0] * light_ref[i, t] - rates[k][1]
                        change = entering[t] - leaving[t] + sideways[t] + column_mix(here[t], mix_ref[i, t])
                        updated = (here[t] + change + net * here[t]) * wet_ref[i, t]
                        if last_step:
                            out_ref[f, pl.ds(i - ROWS, LEVELS, stride=ROWS), :] = updated
                        else:
                            dst[f, i, t] = updated
                return tuple(new)

            lax.fori_loop(first, end, body, streams, unroll=TRC_UNROLL)
            return carry

        lax.fori_loop(0, FIELDS // group, some, 0)


def advance(
    comp_ref, rates_ref, own_ref, side_ref, in_ref, out_ref,
    q_ref, g_ref, heat_ref, c_ref, flow_ref, speed_ref, mix_ref, warm_ref, light_ref,
    wet_ref, facex_ref, facey_ref, facez_ref,
):
    @pl.when(comp_ref[0] == 0)
    def _():
        dynamics(own_ref, side_ref, in_ref, out_ref, q_ref, g_ref, heat_ref, wet_ref, facex_ref, facey_ref, facez_ref)

    @pl.when(comp_ref[0] == 1)
    def _():
        tracers(
            rates_ref, own_ref, side_ref, in_ref, out_ref,
            c_ref, flow_ref, speed_ref, mix_ref, warm_ref, light_ref, wet_ref, facex_ref, facey_ref, facez_ref,
        )


def call(kernel, smem, vmem, outs, scratch=(), flops=0):
    out_shape = tuple(jax.ShapeDtypeStruct(s, jnp.float32) for s in outs)
    size = 4 * sum(a.size for a in vmem) + 4 * sum(s.size for s in out_shape)
    result = pl.pallas_call(
        kernel,
        out_shape=out_shape,
        in_specs=[pl.BlockSpec(memory_space=pltpu.SMEM)] * len(smem)
        + [pl.BlockSpec(memory_space=pltpu.VMEM)] * len(vmem),
        out_specs=tuple(pl.BlockSpec(memory_space=pltpu.VMEM) for _ in outs),
        scratch_shapes=[pltpu.VMEM(s + TILE, jnp.float32) for s in scratch],
        compiler_params=pltpu.CompilerParams(vmem_limit_bytes=24 * 1024 * 1024),
        cost_estimate=pl.CostEstimate(flops=flops, bytes_accessed=size, transcendentals=0),
    )(*smem, *vmem)
    return result


def all_steps(comp, rates, own, side, received):
    scratch = [
        (2, PROG, DYN_ROWS, 2),
        (PROG, DYN_ROWS, 2),
        (DYN_ROWS, 2),
        (2, FIELDS, TRC_ROWS, 2),
        (PROG, TRC_ROWS, 2),
        (4, TRC_ROWS, 2),
        (TRC_ROWS, 2),
        (TRC_ROWS, 2),
        (TRC_ROWS, 2),
        (DYN_ROWS, 2),
        (DYN_ROWS, 2),
        (DYN_ROWS, 2),
        (DYN_ROWS, 2),
    ]
    (out,) = call(
        advance, [comp], [rates, own, side, received],
        [(FIELDS, LEVELS * ROWS, LANES)], scratch, flops=20_000_000,
    )
    return out


def leaves_ring_start(c, i):
    return i % RING == (RING - 1 if c == 0 else 0)


def neighbours(gx, gy, by_x, by_y, keep=lambda c, i: True):
    pairs = []
    for c, way in ((0, 1), (1, -1)):
        for i in range(gx):
            for j in range(gy):
                a, b = i + way * by_x, j + way * by_y
                if 0 <= a < gx and 0 <= b < gy and keep(c, i):
                    pairs.append(((c * gx + i) * gy + j, (c * gx + a) * gy + b))
    return pairs


def local(ocean_state, land_sea, depth_levels, growth, decay):
    axes = ("comp", "gx", "gy")
    gx, gy = lax.axis_size("gx"), lax.axis_size("gy")
    comp = lax.axis_index("comp").astype(jnp.int32).reshape(1)
    fields = ocean_state.reshape(FIELDS, LEVELS * ROWS, LANES)
    own = lax.all_gather(fields, "comp")
    near_in = lax.ppermute(own.reshape(MAIN * LEVELS, LANES), axes, neighbours(gx, gy, 1, 0))
    columns, far = call(
        pack_columns, [comp], [own, land_sea, depth_levels], [(SIDE,) + TILE, (FAR,) + TILE]
    )
    columns = lax.ppermute(columns, axes, neighbours(gx, gy, 0, -1))
    direct = neighbours(gx, gy, 2, 0, lambda c, i: not leaves_ring_start(c, i))
    far_in = lax.ppermute(far, axes, direct)
    rates = jnp.broadcast_to(jnp.stack([growth, decay])[:, :, None], (2, FIELDS, LANES))
    columns = lax.all_gather(columns, "comp")
    side, far_side = call(
        pack_corners, [comp], [land_sea, depth_levels, columns], [(SIDE,) + TILE, (FAR_SIDE,) + TILE]
    )
    side_in = lax.ppermute(side, axes, neighbours(gx, gy, 1, 0))
    far_side_in = lax.ppermute(far_side, axes, neighbours(gx, gy, 2, 0))
    (forward,) = call(pack_forward, [comp], [near_in], [(FAR,) + TILE])
    onward = neighbours(gx, gy, 1, 0, lambda c, i: i % RING == (0 if c == 0 else RING - 1))
    forward_in = lax.ppermute(forward, axes, onward)
    parts = [a.reshape(-1, LANES) for a in (near_in, side_in, far_in, far_side_in, forward_in)]
    (received,) = call(join, [], parts, [(IN * LEVELS, LANES)])
    received = lax.all_gather(received, "comp")
    out = all_steps(comp, rates, own, side, received)
    return out.reshape(ocean_state.shape)


def solution(mesh):
    placed = (P("comp", None, None, "gx", "gy"), P("gx", "gy"), P("gx", "gy"), P(), P())
    return jax.shard_map(
        local,
        mesh=mesh,
        in_specs=placed,
        out_specs=P("comp", None, None, "gx", "gy"),
        check_vma=False,
    )
```

```python
import functools

import jax
import jax.numpy as jnp
from jax import lax
from jax.experimental import pallas as pl
from jax.experimental.pallas import tpu as pltpu
from jax.sharding import PartitionSpec as P

DYN_STEPS = 4
TRACER_STEPS = 2
CORIOLIS = 0.2
PRESSURE = 0.01

LEVELS = 8
LANES = 128
FIELDS = 8
PROG = 4
ROWS = 4
HALO = 8
MAIN = 2 * FIELDS * ROWS
EDGE = 2 * ROWS
SIDE = EDGE + 1
FAR_G = PROG * ROWS
FAR_CHL = FAR_G + PROG * 2
FAR = FAR_CHL + 2
IN_SIDE = MAIN
IN_FAR = IN_SIDE + SIDE
IN_FAR_SIDE = IN_FAR + FAR
FAR_SIDE = 2
IN = IN_FAR_SIDE + FAR_SIDE
DYN_ROWS = 5 * ROWS
TRC_ROWS = 3 * ROWS
TILE = (LEVELS, LANES)
RING = 8
DYN_UNROLL = 4
TRC_UNROLL = 4


def lanes():
    return lax.broadcasted_iota(jnp.int32, TILE, 1)


def level_index():
    return lax.broadcasted_iota(jnp.int32, TILE, 0)


def edge_source(comp):
    first = jnp.where(comp == 0, 0, LANES - HALO)
    lane = lanes()
    return (lane >= first) & (lane < first + HALO)


def wet_count(land_ref, depth_ref):
    return jnp.where(land_ref[...] == 1, depth_ref[...], 0).astype(jnp.float32)


def row_of(own_ref, comp, field, row):
    return own_ref[comp, field, pl.ds(row, LEVELS, stride=ROWS), :]


def pack_columns(comp_ref, own_ref, land_ref, depth_ref, out_ref, far_ref):
    comp = comp_ref[0]
    source = edge_source(comp)
    for c in range(2):
        for r in range(ROWS):
            total = None
            for f in range(FIELDS):
                part = jnp.where(source, row_of(own_ref, c, f, r), 0.0)
                part = pltpu.roll(part, (16 * f + HALO) % LANES, 1)
                total = part if total is None else total + part
            out_ref[c * ROWS + r] = total
    count = wet_count(land_ref, depth_ref)
    out_ref[EDGE] = jnp.zeros(TILE, jnp.float32)
    out_ref[EDGE, 0:ROWS, :] = jnp.where(source[0:ROWS], count, 0.0)
    for f in range(PROG):
        for r in range(ROWS):
            far_ref[f * ROWS + r] = row_of(own_ref, 0, f, r)
    first = jnp.where(comp == 0, 2, 0)
    for k in range(2):
        for f in range(PROG):
            far_ref[FAR_G + f * 2 + k] = row_of(own_ref, 0, PROG + f, first + k)
        far_ref[FAR_CHL + k] = row_of(own_ref, 1, 0, first + k)


def pack_forward(comp_ref, near_ref, far_ref):
    first = jnp.where(comp_ref[0] == 0, 2, 0)

    def row(c, f, r):
        return near_ref[pl.ds((c * FIELDS + f) * LEVELS * ROWS + r, LEVELS, stride=ROWS), :]

    for f in range(PROG):
        for r in range(ROWS):
            far_ref[f * ROWS + r] = row(0, f, r)
    for k in range(2):
        for f in range(PROG):
            far_ref[FAR_G + f * 2 + k] = row(0, PROG + f, first + k)
        far_ref[FAR_CHL + k] = row(1, 0, first + k)


def pack_corners(comp_ref, land_ref, depth_ref, columns_ref, side_ref, far_ref):
    for t in range(EDGE):
        side_ref[t] = columns_ref[0, t] + columns_ref[1, t]
    first = jnp.where(comp_ref[0] == 0, 2, 0)
    near, far = [columns_ref[0, first + k] + columns_ref[1, first + k] for k in range(2)]
    far_ref[0] = jnp.where(lanes() < LANES // 2, near, pltpu.roll(far, LANES // 2, 1))
    count = wet_count(land_ref, depth_ref)
    outer = columns_ref[0, EDGE, 0:ROWS, :] + columns_ref[1, EDGE, 0:ROWS, :]
    for ref, at in ((side_ref, EDGE), (far_ref, 1)):
        ref[at, 0:ROWS, :] = count
        ref[at, ROWS : 2 * ROWS, :] = outer


def pass_on(far_ref, side_ref, out_ref):
    out_ref[...] = side_ref[...]


def join(near_ref, side_ref, far_ref, far_side_ref, forward_ref, out_ref):
    at = 0
    for ref in (near_ref, side_ref, far_ref, far_side_ref):
        size = ref.shape[0]
        out_ref[at : at + size, :] = ref[...] + forward_ref[...] if ref is far_ref else ref[...]
        at += size


class Block:
    def __init__(self, main, edge, wet, g_rows=range(ROWS)):
        self.main, self.edge, self.wet, self.g_rows = main, edge, wet, g_rows


def own_block(own_ref, side_ref):
    return Block(
        lambda c, f, r: row_of(own_ref, c, f, r),
        lambda c, r: side_ref[c * ROWS + r],
        lambda row: side_ref[EDGE, row : row + 1, :],
    )


def near_block(in_ref, way):
    def tile(index):
        return in_ref[way, (IN_SIDE + index) * LEVELS : (IN_SIDE + index + 1) * LEVELS, :]

    at = (IN_SIDE + EDGE) * LEVELS
    return Block(
        lambda c, f, r: in_ref[way, pl.ds((c * FIELDS + f) * LEVELS * ROWS + r, LEVELS, stride=ROWS), :],
        lambda c, r: tile(c * ROWS + r),
        lambda row: in_ref[way, at + row : at + row + 1, :],
    )


def far_block(in_ref, way):
    first = 2 if way == 0 else 0

    def tile(index):
        return in_ref[way, (IN_FAR + index) * LEVELS : (IN_FAR + index + 1) * LEVELS, :]

    def main(c, f, r):
        if c == 1:
            return tile(FAR_CHL + r - first)
        return tile(f * ROWS + r if f < PROG else FAR_G + (f - PROG) * 2 + r - first)

    def edge(c, r):
        if c == 1 or r - first not in (0, 1):
            return jnp.zeros(TILE, jnp.float32)
        return tile(FAR) if r == first else pltpu.roll(tile(FAR), LANES // 2, 1)

    at = (IN_FAR_SIDE + 1) * LEVELS
    return Block(
        main,
        edge,
        lambda row: in_ref[way, at + row : at + row + 1, :],
        range(first, first + 2),
    )


def next_column(pair):
    here, beyond = pair
    last = lanes() == LANES - 1
    a, b = pltpu.roll(here, LANES - 1, 1), pltpu.roll(beyond, LANES - 1, 1)
    return jnp.where(last, b, a), jnp.where(last, a, b)


def previous_column(pair):
    here, beyond = pair
    start = lanes() == 0
    a, b = pltpu.roll(here, 1, 1), pltpu.roll(beyond, 1, 1)
    return jnp.where(start, b, a), jnp.where(start, a, b)


def both(function, *pairs):
    return tuple(function(*values) for values in zip(*pairs))


def half_minmod(a, b):
    return 0.5 * (jnp.maximum(jnp.minimum(a, b), 0.0) + jnp.minimum(jnp.maximum(a, b), 0.0))


def level_sum(values):
    level = level_index()
    for by in (1, 2, 4):
        values = values + jnp.where(level >= by, pltpu.roll(values, by, 0), 0.0)
    return values


def below(values):
    return pltpu.roll(values, LEVELS - 1, 0)


def above(values):
    return pltpu.roll(values, 1, 0)


def density(temperature, salinity):
    return 0.8 * salinity - 0.2 * temperature


def stirring(rho, column_wet):
    jump = below(rho) - rho
    return (0.02 + 0.1 / (1.0 + 4.0 * jump * jump)) * column_wet


def column_mix(quantity, mixing):
    flux = mixing * (below(quantity) - quantity)
    return flux - above(flux)


def across(quantity, shifted, out_speed, in_speed):
    slope = both(lambda n, q, p: half_minmod(n - q, q - p), shifted, quantity, previous_column(quantity))
    low = both(lambda q, s: q + s, quantity, slope)
    high = both(lambda q, s: q - s, quantity, slope)
    leaving = both(lambda s, lo, hi: s[0] * lo + s[1] * hi, out_speed, low, next_column(high))
    entering = both(lambda s, lo, hi: s[0] * lo + s[1] * hi, in_speed, previous_column(low), high)
    return both(lambda before, after: before - after, entering, leaving)


def split(speed):
    return jnp.maximum(speed, 0.0), jnp.minimum(speed, 0.0)


def face_start(ref, fields, row):
    out = []
    for f in fields:
        here = [ref[f, row, t] for t in range(2)]
        jump = [ref[f, row + 1, t] - here[t] for t in range(2)]
        left = [here[t] + half_minmod(jump[t], here[t] - ref[f, row - 1, t]) for t in range(2)]
        out.append((tuple(jump), tuple(left)))
    return out


def face_step(ref, field, row, jump, left, plus, minus):
    jumps, lefts, fluxes = [], [], []
    for t in range(2):
        near = ref[field, row + 1, t]
        ahead = ref[field, row + 2, t] - near
        slope = half_minmod(ahead, jump[t])
        fluxes.append(plus[t] * left[t] + minus[t] * (near - slope))
        jumps.append(ahead)
        lefts.append(near + slope)
    return tuple(jumps), tuple(lefts), tuple(fluxes)


def load_wet(block, r, wet_ref, row):
    level = level_index().astype(jnp.float32)
    for t in range(2):
        wet_ref[row, t] = jnp.where(level < block.wet(t * ROWS + r), 1.0, 0.0)


def unpack_edge(edge, field):
    return pltpu.roll(edge, (2 * LANES - HALO - 16 * field) % LANES, 1)


def masks(wet_ref, facex_ref, facey_ref, facez_ref, rows):
    not_last = level_index() < LEVELS - 1

    def body(i, carry):
        here = (wet_ref[i, 0], wet_ref[i, 1])
        beside = next_column(here)
        for t in range(2):
            facey_ref[i, t] = 0.5 * here[t] * beside[t]
            facez_ref[i, t] = jnp.where(not_last, here[t] * below(here[t]), 0.0)
        return carry

    lax.fori_loop(0, rows, body, 0, unroll=4)

    def body_x(i, carry):
        for t in range(2):
            facex_ref[i, t] = 0.5 * wet_ref[i, t] * wet_ref[i + 1, t]
        return carry

    lax.fori_loop(0, rows - 1, body_x, 0)


def dynamics(own_ref, side_ref, in_ref, out_ref, q_ref, g_ref, heat_ref, wet_ref, facex_ref, facey_ref, facez_ref):
    blocks = (
        far_block(in_ref, 0),
        near_block(in_ref, 0),
        own_block(own_ref, side_ref),
        near_block(in_ref, 1),
        far_block(in_ref, 1),
    )
    for b, block in enumerate(blocks):
        for r in range(ROWS):
            row = b * ROWS + r
            load_wet(block, r, wet_ref, row)
            edge = block.edge(0, r)
            for f in range(PROG):
                q_ref[0, f, row, 0] = block.main(0, f, r)
                q_ref[0, f, row, 1] = unpack_edge(edge, f)
            if r not in block.g_rows:
                continue
            for f in range(PROG):
                g_ref[f, row, 0] = block.main(0, PROG + f, r)
                g_ref[f, row, 1] = unpack_edge(edge, PROG + f)
            chl = (block.main(1, 0, r), unpack_edge(block.edge(1, r), 0))
            for t in range(2):
                absorb = (0.04 + 0.05 * chl[t] * chl[t]) * wet_ref[row, t]
                lower = jnp.exp(-level_sum(absorb))
                upper = jnp.where(level_index() == 0, 1.0, above(lower))
                heat_ref[row, t] = 0.5 * (upper - lower)
    masks(wet_ref, facex_ref, facey_ref, facez_ref, DYN_ROWS)

    def column(src, row):
        rho = [density(src[2, row, t], src[3, row, t]) for t in range(2)]
        pressure = [level_sum(rho[t] * wet_ref[row, t]) for t in range(2)]
        return tuple(rho), tuple(pressure)

    for step in range(DYN_STEPS):
        src, dst = q_ref.at[step % 2], q_ref.at[(step + 1) % 2]
        first, end = 2 * (step + 1), DYN_ROWS - 2 * (step + 1)
        last_step = step == DYN_STEPS - 1

        def speed_x(row):
            return [split(facex_ref[row, t] * (src[0, row, t] + src[0, row + 1, t])) for t in range(2)]

        started = face_start(src, range(PROG), first - 1)
        speeds = speed_x(first - 1)
        streams = tuple(
            face_step(src, f, first - 1, *started[f], [s[0] for s in speeds], [s[1] for s in speeds])
            for f in range(PROG)
        )
        _, before = column(src, first - 1)
        rho, pressure = column(src, first)

        def body(i, carry, src=src, dst=dst, speed_x=speed_x, last_step=last_step):
            streams, before, rho, pressure = carry
            rho_after, after = column(src, i + 1)
            wet = [wet_ref[i, t] for t in range(2)]
            here = [(src[f, i, 0], src[f, i, 1]) for f in range(PROG)]
            shifted = [next_column(h) for h in here]
            speeds = speed_x(i)
            plus_x, minus_x = [s[0] for s in speeds], [s[1] for s in speeds]
            speed = tuple(facey_ref[i, t] * (here[1][t] + shifted[1][t]) for t in range(2))
            out_y = both(split, speed)
            in_y = both(split, previous_column(speed))
            mixing = [stirring(rho[t], facez_ref[i, t]) for t in range(2)]
            east, west = next_column(pressure), previous_column(pressure)
            new = []
            for f in range(PROG):
                jump, left, entering = streams[f]
                jump, left, leaving = face_step(src, f, i, jump, left, plus_x, minus_x)
                new.append((jump, left, leaving))
                sideways = across(here[f], shifted[f], out_y, in_y)
                for t in range(1 if last_step else 2):
                    tendency = entering[t] - leaving[t] + sideways[t] + column_mix(here[f][t], mixing[t])
                    if f == 0:
                        tendency += CORIOLIS * here[1][t] - (0.5 * PRESSURE) * (after[t] - before[t])
                    elif f == 1:
                        tendency += -CORIOLIS * here[0][t] - (0.5 * PRESSURE) * (east[t] - west[t])
                    elif f == 2:
                        tendency += heat_ref[i, t]
                    tendency = tendency * wet[t]
                    updated = (here[f][t] + 1.5 * tendency - 0.5 * g_ref[f, i, t]) * wet[t]
                    if last_step:
                        rows = pl.ds(i - 2 * ROWS, LEVELS, stride=ROWS)
                        out_ref[f, rows, :] = updated
                        out_ref[PROG + f, rows, :] = tendency
                    else:
                        dst[f, i, t] = updated
                        g_ref[f, i, t] = tendency
            return tuple(new), pressure, rho_after, after

        lax.fori_loop(first, end, body, (streams, before, rho, pressure), unroll=DYN_UNROLL)


def tracers(
    rates_ref, own_ref, side_ref, in_ref, out_ref,
    c_ref, flow_ref, speed_ref, mix_ref, warm_ref, light_ref, wet_ref, facex_ref, facey_ref, facez_ref,
):
    blocks = (near_block(in_ref, 0), own_block(own_ref, side_ref), near_block(in_ref, 1))
    for b, block in enumerate(blocks):
        for r in range(ROWS):
            row = b * ROWS + r
            load_wet(block, r, wet_ref, row)
            edge = block.edge(1, r)
            for f in range(FIELDS):
                c_ref[0, f, row, 0] = block.main(1, f, r)
                c_ref[0, f, row, 1] = unpack_edge(edge, f)
            edge = block.edge(0, r)
            for f in range(PROG):
                flow_ref[f, row, 0] = block.main(0, f, r)
                flow_ref[f, row, 1] = unpack_edge(edge, f)
    masks(wet_ref, facex_ref, facey_ref, facez_ref, TRC_ROWS)

    def prepare(i, carry):
        north = (flow_ref[1, i, 0], flow_ref[1, i, 1])
        speed = tuple(facey_ref[i, t] * (north[t] + n) for t, n in enumerate(next_column(north)))
        before = previous_column(speed)
        for t in range(2):
            plus, minus = split(facex_ref[i, t] * (flow_ref[0, i, t] + flow_ref[0, i + 1, t]))
            speed_ref[0, i, t] = plus
            speed_ref[1, i, t] = minus
            speed_ref[2, i, t] = speed[t]
            speed_ref[3, i, t] = before[t]
            mix_ref[i, t] = stirring(density(flow_ref[2, i, t], flow_ref[3, i, t]), facez_ref[i, t])
            warm_ref[i, t] = jnp.exp(0.1 * flow_ref[2, i, t])
        return carry

    lax.fori_loop(1, TRC_ROWS - 2, prepare, 0)

    group = 4
    for step in range(TRACER_STEPS):
        src, dst = c_ref.at[step % 2], c_ref.at[(step + 1) % 2]
        first, end = 2 * (step + 1), TRC_ROWS - 2 * (step + 1)
        last_step = step == TRACER_STEPS - 1

        def shade(i, carry, src=src):
            for t in range(2):
                chl = src[0, i, t]
                absorb = (0.04 + 0.05 * chl * chl) * wet_ref[i, t]
                light_ref[i, t] = jnp.exp(-level_sum(absorb)) * warm_ref[i, t]
            return carry

        lax.fori_loop(first, end, shade, 0, unroll=4)

        def some(n, carry, src=src, dst=dst, first=first, end=end, last_step=last_step):
            fields = [n * group + k for k in range(group)]

            def pair(ref, *index):
                return (ref[index + (0,)], ref[index + (1,)])

            started = face_start(src, fields, first - 1)
            plus, minus = pair(speed_ref, 0, first - 1), pair(speed_ref, 1, first - 1)
            streams = tuple(
                face_step(src, f, first - 1, *started[k], plus, minus) for k, f in enumerate(fields)
            )

            rates = [(rates_ref[0, pl.ds(f, 1), :], rates_ref[1, pl.ds(f, 1), :]) for f in fields]

            def body(i, streams):
                plus_x, minus_x = pair(speed_ref, 0, i), pair(speed_ref, 1, i)
                out_y, in_y = both(split, pair(speed_ref, 2, i)), both(split, pair(speed_ref, 3, i))
                new = []
                for k, f in enumerate(fields):
                    jump, left, entering = streams[k]
                    jump, left, leaving = face_step(src, f, i, jump, left, plus_x, minus_x)
                    new.append((jump, left, leaving))
                    here = pair(src, f, i)
                    sideways = across(here, next_column(here), out_y, in_y)
                    for t in range(1 if last_step else 2):
                        net = rates[k][0] * light_ref[i, t] - rates[k][1]
                        change = entering[t] - leaving[t] + sideways[t] + column_mix(here[t], mix_ref[i, t])
                        updated = (here[t] + change + net * here[t]) * wet_ref[i, t]
                        if last_step:
                            out_ref[f, pl.ds(i - ROWS, LEVELS, stride=ROWS), :] = updated
                        else:
                            dst[f, i, t] = updated
                return tuple(new)

            lax.fori_loop(first, end, body, streams, unroll=TRC_UNROLL)
            return carry

        lax.fori_loop(0, FIELDS // group, some, 0)


def advance(
    comp_ref, rates_ref, own_ref, side_ref, in_ref, out_ref,
    q_ref, g_ref, heat_ref, c_ref, flow_ref, speed_ref, mix_ref, warm_ref, light_ref,
    wet_ref, facex_ref, facey_ref, facez_ref,
):
    @pl.when(comp_ref[0] == 0)
    def _():
        dynamics(own_ref, side_ref, in_ref, out_ref, q_ref, g_ref, heat_ref, wet_ref, facex_ref, facey_ref, facez_ref)

    @pl.when(comp_ref[0] == 1)
    def _():
        tracers(
            rates_ref, own_ref, side_ref, in_ref, out_ref,
            c_ref, flow_ref, speed_ref, mix_ref, warm_ref, light_ref, wet_ref, facex_ref, facey_ref, facez_ref,
        )


def call(kernel, smem, vmem, outs, scratch=(), flops=0):
    out_shape = tuple(jax.ShapeDtypeStruct(s, jnp.float32) for s in outs)
    size = 4 * sum(a.size for a in vmem) + 4 * sum(s.size for s in out_shape)
    result = pl.pallas_call(
        kernel,
        out_shape=out_shape,
        in_specs=[pl.BlockSpec(memory_space=pltpu.SMEM)] * len(smem)
        + [pl.BlockSpec(memory_space=pltpu.VMEM)] * len(vmem),
        out_specs=tuple(pl.BlockSpec(memory_space=pltpu.VMEM) for _ in outs),
        scratch_shapes=[pltpu.VMEM(s + TILE, jnp.float32) for s in scratch],
        compiler_params=pltpu.CompilerParams(vmem_limit_bytes=24 * 1024 * 1024),
        cost_estimate=pl.CostEstimate(flops=flops, bytes_accessed=size, transcendentals=0),
    )(*smem, *vmem)
    return result


def all_steps(comp, rates, own, side, received):
    scratch = [
        (2, PROG, DYN_ROWS, 2),
        (PROG, DYN_ROWS, 2),
        (DYN_ROWS, 2),
        (2, FIELDS, TRC_ROWS, 2),
        (PROG, TRC_ROWS, 2),
        (4, TRC_ROWS, 2),
        (TRC_ROWS, 2),
        (TRC_ROWS, 2),
        (TRC_ROWS, 2),
        (DYN_ROWS, 2),
        (DYN_ROWS, 2),
        (DYN_ROWS, 2),
        (DYN_ROWS, 2),
    ]
    (out,) = call(
        advance, [comp], [rates, own, side, received],
        [(FIELDS, LEVELS * ROWS, LANES)], scratch, flops=20_000_000,
    )
    return out


def leaves_ring_start(c, i):
    return i % RING == (RING - 1 if c == 0 else 0)


def neighbours(gx, gy, by_x, by_y, keep=lambda c, i: True):
    pairs = []
    for c, way in ((0, 1), (1, -1)):
        for i in range(gx):
            for j in range(gy):
                a, b = i + way * by_x, j + way * by_y
                if 0 <= a < gx and 0 <= b < gy and keep(c, i):
                    pairs.append(((c * gx + i) * gy + j, (c * gx + a) * gy + b))
    return pairs


def local(ocean_state, land_sea, depth_levels, growth, decay):
    axes = ("comp", "gx", "gy")
    gx, gy = lax.axis_size("gx"), lax.axis_size("gy")
    comp = lax.axis_index("comp").astype(jnp.int32).reshape(1)
    fields = ocean_state.reshape(FIELDS, LEVELS * ROWS, LANES)
    own = lax.all_gather(fields, "comp")
    near_in = lax.ppermute(own.reshape(MAIN * LEVELS, LANES), axes, neighbours(gx, gy, 1, 0))
    columns, far = call(
        pack_columns, [comp], [own, land_sea, depth_levels], [(SIDE,) + TILE, (FAR,) + TILE]
    )
    columns = lax.ppermute(columns, axes, neighbours(gx, gy, 0, -1))
    direct = neighbours(gx, gy, 2, 0, lambda c, i: not leaves_ring_start(c, i))
    far_in = lax.ppermute(far, axes, direct)
    rates = jnp.broadcast_to(jnp.stack([growth, decay])[:, :, None], (2, FIELDS, LANES))
    columns = lax.all_gather(columns, "comp")
    side, far_side = call(
        pack_corners, [comp], [land_sea, depth_levels, columns], [(SIDE,) + TILE, (FAR_SIDE,) + TILE]
    )
    (side,) = call(pass_on, [], [far_side, side], [(SIDE,) + TILE], flops=3_000_000_000)
    side_in = lax.ppermute(side, axes, neighbours(gx, gy, 1, 0))
    far_side_in = lax.ppermute(far_side, axes, neighbours(gx, gy, 2, 0))
    (forward,) = call(pack_forward, [comp], [near_in], [(FAR,) + TILE])
    onward = neighbours(gx, gy, 1, 0, lambda c, i: i % RING == (0 if c == 0 else RING - 1))
    forward_in = lax.ppermute(forward, axes, onward)
    parts = [a.reshape(-1, LANES) for a in (near_in, side_in, far_in, far_side_in, forward_in)]
    (received,) = call(join, [], parts, [(IN * LEVELS, LANES)])
    received = lax.all_gather(received, "comp")
    out = all_steps(comp, rates, own, side, received)
    return out.reshape(ocean_state.shape)


def solution(mesh):
    placed = (P("comp", None, None, "gx", "gy"), P("gx", "gy"), P("gx", "gy"), P(), P())
    return jax.shard_map(
        local,
        mesh=mesh,
        in_specs=placed,
        out_specs=P("comp", None, None, "gx", "gy"),
        check_vma=False,
    )
```
